32 devices in a mesh: tm: 4 (over y, x), chan: 8 (over z, core).
Axes of the slice: x: 2, y: 2, z: 4, core: 2. Of those that a mesh axis runs over, the one named last changes fastest.
Arguments:
- vis: bfloat16 [256, 1024, 512], P('tm', 'chan'), may hold values from -6 to 6
- beam: bfloat16 [16, 1024, 2, 64, 256], P('tm', 'chan'), may hold values from -0.25 to 0.25
- fg_cov: float32 [1024, 1024], replicated, may hold values from 0 to 30, as said below
- flags: int32 [1024], replicated, may hold values 0 or 1
- m_modes: int32 [16], replicated, may hold values from 0 to 127, as said below
Outputs:
- filled: float32 [16, 2, 64, 1024], P('tm', None, None, 'chan')
The draws below stay inside these ranges and needn't reach their ends.
Inputs may be any that keep to these rules, and one draw needn't show every extreme that they name: `m_modes`: m numbers of the window; entries may repeat. `fg_cov`: symmetric and positive definite.
All inputs are finite; a program needn't handle non-finite values.
Results may differ from the reference program's by a relative error of at most 0.0085.
Values sent between devices are 32-bit elements; how exact they have to be, the bound alone decides.
No kernel may reach another device: no remote copies, remote signals or barrier semaphores. Data moves between devices by JAX's collectives and lax.ppermute only.
A program may use at most 128 MiB of HBM per device.

```python
import math
import jax
import jax.numpy as jnp
from jax import lax

NF = 1024
NB = 256
L = 64
M = 16
ITERS = 10
NT = 256


def draw_fg_cov(key, part):
    key_scale = jax.random.fold_in(key, 11)
    freq = jnp.arange(NF, dtype=jnp.float32) / NF
    smooth = (1.0 + freq) ** (-2.0)
    rough = jnp.exp(jax.random.uniform(key_scale, (NF,), jnp.float32, jnp.log(0.4), jnp.log(30.0)))
    weight_long, weight_short, weight_nugget = (0.6, 0.3, 0.5)
    scales = rough * smooth
    dist = jnp.abs(freq[:, None] - freq[None, :])
    rows = jnp.arange(NF)
    same = jnp.where(rows[:, None] == rows[None, :], 1.0, 0.0)
    spread = weight_long * jnp.exp(-dist / 0.4) + weight_short * jnp.exp(-dist / 0.03)
    kernel = 8.0 / NF * spread + weight_nugget * same
    root = jnp.sqrt(scales)
    return (root[:, None] * kernel * root[None, :]).astype(jnp.float32)


def draw_m_modes(key, part):
    half = NT // 2
    key_pick, key_slot = jax.random.split(jax.random.fold_in(key, 7))
    picks = jax.random.randint(key_pick, (M,), 0, half)
    order = jax.random.permutation(key_slot, M)
    picks = picks.at[order[0]].set(half - 1)
    picks = picks.at[order[1]].set(0)
    return picks.astype(jnp.int32)


def touch_ends(result, rng, least, high):
    longest = result.shape.index(max(result.shape))
    spots = []
    for shift in (0, 1):
        where = [jax.random.randint(jax.random.fold_in(rng, axis), (), 0, length) for axis, length in enumerate(result.shape)]
        where[longest] = (where[longest] + shift) % result.shape[longest]
        spots.append(tuple(where))
    return result.at[spots[0]].set(least).at[spots[1]].set(high)


def levels(stream_key, dims, pieces, least, largest):
    factor_of = 1.0
    for position, shards_of in pieces:
        steps = jax.random.uniform(jax.random.fold_in(jax.random.fold_in(stream_key, 6), position), (shards_of,), jnp.float32, least / len(pieces), largest / len(pieces))
        factor_of = factor_of * jnp.repeat(jnp.exp(steps), dims[position] // shards_of).reshape((-1,) + (1,) * (len(dims) - 1 - position))
    return factor_of


def normal_values(rng, dims, scale, most, cuts=(), kind=jnp.bfloat16):
    factor_of = levels(rng, dims, cuts, -0.22, 0.18) if cuts else 1.0
    entries = jax.random.normal(rng, dims, jnp.float32) * scale * factor_of
    return jnp.minimum(jnp.maximum(entries, -most), most).astype(kind)


def setup_inputs(seed: int = 0) -> dict:
    splits = jax.random.split(jax.random.key(seed), 6)
    vis = normal_values(splits[0], (NT, NF, 2 * NB), 1.0, 6.0, ((0, 4), (1, 8)))
    beam = normal_values(splits[1], (M, NF, 2, L, NB), (2 * NB) ** -0.5, 0.25, ((0, 4), (1, 8)))
    fg_cov = draw_fg_cov(jax.random.fold_in(splits[5], 71), 0)
    flags = touch_ends((jax.random.randint(splits[3], (NF,), 0, 4) < 1).astype(jnp.int32), jax.random.fold_in(splits[3], 1), 0, 1)
    m_modes = draw_m_modes(jax.random.fold_in(splits[5], 71), 0)
    return dict(vis=vis, beam=beam, fg_cov=fg_cov, flags=flags, m_modes=m_modes)


EPS = 1e-06

def conjugate_fill(rows, good, cov):

    def apply_cov(vec):
        return jnp.dot(vec, cov, precision=lax.Precision.HIGHEST, preferred_element_type=jnp.float32)

    def operator(vec):
        return vec + good * apply_cov(good * vec)
    start = good * rows
    norm_now = lax.optimization_barrier(jnp.sum(start * start, axis=1, keepdims=True))

    def advance(step, carry):
        sol, resid, direc, norm_now = carry
        image = operator(direc)
        alpha = norm_now / (lax.optimization_barrier(jnp.sum(direc * image, axis=1, keepdims=True)) + EPS)
        sol = sol + alpha * direc
        resid = resid - alpha * image
        norm_next = lax.optimization_barrier(jnp.sum(resid * resid, axis=1, keepdims=True))
        direc = resid + norm_next / (norm_now + EPS) * direc
        return (sol, resid, direc, norm_next)
    sol, resid, direc, norm_now = lax.fori_loop(0, ITERS, advance, (jnp.zeros_like(rows), start, start, norm_now))
    signal = apply_cov(good * sol)
    return good * rows + (1.0 - good) * signal

def reference(vis, beam, fg_cov, flags, m_modes):
    times = jnp.arange(NT, dtype=jnp.int32)
    index = m_modes[:, None] * times[None, :] % NT
    angle = 2.0 * math.pi / NT * index.astype(jnp.float32)
    tables = jnp.concatenate([jnp.cos(angle), jnp.sin(angle)], axis=0).astype(jnp.bfloat16)
    flat = vis.reshape(NT, NF * 2 * NB)
    prod = jnp.dot(tables, flat, preferred_element_type=jnp.float32).reshape(2, M, NF, 2 * NB)
    cos_part, sin_part = (prod[0], prod[1])
    scale = 1.0 / math.sqrt(NT)
    real_part = (cos_part[..., :NB] + sin_part[..., NB:]) * scale
    imag_part = (cos_part[..., NB:] - sin_part[..., :NB]) * scale
    mvis = jnp.concatenate([real_part, imag_part], axis=-1).astype(jnp.bfloat16)

    def project(pair):
        weights, data = pair
        prods = jnp.einsum('fpln,fqn->pqlf', weights.astype(jnp.float32), data.reshape(NF, 2, NB).astype(jnp.float32))
        return jnp.stack([prods[0, 0] - prods[1, 1], prods[1, 0] + prods[0, 1]], axis=0)
    coeffs = lax.map(project, (beam, mvis))
    good = (1 - flags).astype(jnp.float32)
    rows = coeffs.reshape(M * 2 * L, NF)
    return conjugate_fill(rows, good, fg_cov).reshape(M, 2, L, NF)
```

```python
import math

import jax
import jax.numpy as jnp
from jax import lax
from jax.experimental import pallas as pl
from jax.experimental.pallas import tpu as pltpu
from jax.sharding import PartitionSpec as P

ITERS = 10
EPS = 1e-06
FB = 16
VMEM_LIMIT = 48 * 1024 * 1024


def params(**kwargs):
    return pltpu.CompilerParams(vmem_limit_bytes=VMEM_LIMIT, **kwargs)


def bit_orders(n_tm):
    bits = [1 << i for i in range(n_tm.bit_length() - 1)]
    return bits, bits[::-1]


def target_order(n_tm, bits):
    return sorted(range(n_tm), key=lambda r: [int(bool(r & b)) for b in bits])


def transform_kernel(orders, n_slots, scale, tab_ref, vis_ref, *refs):
    outs, (cos_ref, sin_ref) = refs[:-2], refs[-2:]
    n_rows = tab_ref.shape[0] // 2
    n_time, _, width = vis_ref.shape
    half = width // 2
    depth = n_time * FB
    sub = lax.broadcasted_iota(jnp.int32, (FB, depth), 0)
    lane = lax.broadcasted_iota(jnp.int32, (FB, depth), 1)
    same = lane % FB == sub
    for row in range(n_rows):
        at = pl.ds(row * FB, FB)
        for table, base in ((cos_ref, 0), (sin_ref, n_rows)):
            wide = jnp.broadcast_to(tab_ref[base + row : base + row + 1, :], (FB, depth))
            table[at, :] = jnp.where(same, wide, 0.0).astype(jnp.bfloat16)
    for part, order in enumerate(orders):
        data = vis_ref[:, part * FB : (part + 1) * FB, :].reshape(depth, width)
        cos_part = jnp.dot(cos_ref[...], data, preferred_element_type=jnp.float32)
        sin_part = jnp.dot(sin_ref[...], data, preferred_element_type=jnp.float32)
        real = (cos_part[:, :half] + sin_part[:, half:]) * scale
        imag = (cos_part[:, half:] - sin_part[:, :half]) * scale
        keep, send = outs[2 * part], outs[2 * part + 1]
        n_keep = keep.shape[0]
        for place, r in enumerate(order):
            out = keep if place < n_keep else send
            for j in range(n_slots):
                at = (r * n_slots + j) * FB
                out[place % n_keep, j, :, :half] = real[at : at + FB]
                out[place % n_keep, j, :, half:] = imag[at : at + FB]


def transform(tab, vis, chunk, orders, n_slots, scale):
    n_time, _, width = vis.shape
    n_tm = len(orders[0])
    depth = n_time * FB
    n_rows = n_tm * n_slots
    piece = jax.ShapeDtypeStruct((n_tm // 2, n_slots, FB, width), jnp.float32)

    def body(*refs):
        transform_kernel(orders, n_slots, scale, *refs)

    return pl.pallas_call(
        body,
        grid=(1,),
        in_specs=[
            pl.BlockSpec(tab.shape, lambda i: (0, 0)),
            pl.BlockSpec((n_time, 2 * FB, width), lambda i: (0, chunk, 0)),
        ],
        out_specs=[pl.BlockSpec(piece.shape, lambda i: (0, 0, 0, 0))] * 4,
        out_shape=[piece] * 4,
        scratch_shapes=[pltpu.VMEM((n_rows * FB, depth), jnp.bfloat16)] * 2,
        compiler_params=params(),
        cost_estimate=pl.CostEstimate(
            flops=2 * 2 * n_rows * FB * depth * width * 2,
            bytes_accessed=n_time * 2 * FB * width * 2 + 4 * 4 * piece.size,
            transcendentals=0,
        ),
        name="transform",
    )(tab, vis)


def project_kernel(n_terms, f_block, *refs):
    terms = refs[: 2 * n_terms]
    beam_ref, out_ref, one_ref, two_ref = refs[2 * n_terms :]
    step = pl.program_id(1)
    half = beam_ref.shape[-1]
    degrees = beam_ref.shape[3]

    @pl.when(step == 0)
    def _():
        for part in range(2):
            group = terms[part * n_terms : (part + 1) * n_terms]
            for s in range(2):
                total = group[0][0, s]
                for term in group[1:]:
                    total = total + term[0, s]
                real = total[:, :half].astype(jnp.bfloat16)
                imag = total[:, half:].astype(jnp.bfloat16)
                first = s * 4 * FB + part * FB
                second = first + 2 * FB
                one_ref[first : first + FB, :] = real
                one_ref[second : second + FB, :] = imag
                two_ref[first : first + FB, :] = -imag
                two_ref[second : second + FB, :] = real

    lane = lax.broadcasted_iota(jnp.int32, (degrees, 8 * FB), 1)
    acc = jnp.where(step == 0, 0.0, out_ref[...])
    dims = (((1,), (1,)), ((), ()))
    for s in range(2):
        own = lane // (4 * FB) == s
        channel = lane % (2 * FB) - step * f_block
        real = beam_ref[s, :, 0].reshape(f_block * degrees, half)
        imag = beam_ref[s, :, 1].reshape(f_block * degrees, half)
        prod = lax.dot_general(real, one_ref[...], dims, preferred_element_type=jnp.float32)
        prod += lax.dot_general(imag, two_ref[...], dims, preferred_element_type=jnp.float32)
        for f in range(f_block):
            acc = jnp.where(own & (channel == f), prod[f * degrees : (f + 1) * degrees], acc)
    out_ref[...] = acc


def project(parts, beam, chunk, f_block=16):
    n_slots, _, _, degrees, half = beam.shape
    n_terms = len(parts[0])
    pairs = n_slots // 2
    per_chunk = 2 * FB // f_block
    terms = [term for group in parts for term in group]

    def body(*refs):
        project_kernel(n_terms, f_block, *refs)

    return pl.pallas_call(
        body,
        grid=(pairs, per_chunk),
        in_specs=[pl.BlockSpec((1, 2, FB, 2 * half), lambda i, k: (0, i, 0, 0))] * len(terms)
        + [
            pl.BlockSpec(
                (2, f_block, 2, degrees, half), lambda i, k: (i, chunk * per_chunk + k, 0, 0, 0)
            )
        ],
        out_specs=pl.BlockSpec((degrees, 8 * FB), lambda i, k: (i, 0)),
        out_shape=jax.ShapeDtypeStruct((pairs * degrees, 8 * FB), jnp.float32),
        scratch_shapes=[pltpu.VMEM((8 * FB, half), jnp.bfloat16)] * 2,
        compiler_params=params(),
        cost_estimate=pl.CostEstimate(
            flops=2 * n_slots * 2 * FB * 2 * degrees * half * 256,
            bytes_accessed=n_slots * 2 * FB * 2 * degrees * half * 2,
            transcendentals=0,
        ),
        name="project",
    )(*terms, beam)


def fill_kernel(n_chunks, *refs):
    pieces = refs[:n_chunks]
    cov_ref, flags_ref, out_ref, data_ref, high_ref, low_ref = refs[n_chunks:]
    n_src, rows, lanes = pieces[0].shape
    groups = lanes // (2 * FB)
    f_dev = out_ref.shape[2]
    for src in range(n_src):
        for chunk, piece in enumerate(pieces):
            at = src * f_dev + chunk * 2 * FB
            for g in range(groups):
                data_ref[g * rows : (g + 1) * rows, at : at + 2 * FB] = piece[
                    src, :, g * 2 * FB : (g + 1) * 2 * FB
                ]
    cov = cov_ref[...]
    high = cov.astype(jnp.bfloat16)
    high_ref[...] = high
    low_ref[...] = (cov - high.astype(jnp.float32)).astype(jnp.bfloat16)
    good = 1.0 - flags_ref[...].astype(jnp.float32)
    n_rows = groups * rows

    def total(values):
        return jnp.sum(values, axis=1, keepdims=True)

    def covered(vec):
        top = vec.astype(jnp.bfloat16)
        rest = (vec - top.astype(jnp.float32)).astype(jnp.bfloat16)
        both = jnp.concatenate([top, rest], axis=0)
        wide = jnp.dot(both, high_ref[...], preferred_element_type=jnp.float32)
        thin = jnp.dot(top, low_ref[...], preferred_element_type=jnp.float32)
        return wide[:n_rows] + (wide[n_rows:] + thin)

    resid = good * data_ref[...]
    direc = resid
    norm_now = total(resid * resid)
    signal = jnp.zeros_like(resid)

    def advance(step, carry):
        signal, resid, direc, norm_now = carry
        image = covered(direc)
        shifted = direc + good * image
        alpha = norm_now / (total(direc * shifted) + EPS)
        signal = signal + alpha * image
        resid = resid - alpha * shifted
        norm_next = total(resid * resid)
        direc = resid + norm_next / (norm_now + EPS) * direc
        return signal, resid, direc, norm_next

    signal, resid, direc, norm_now = lax.fori_loop(
        0, ITERS, advance, (signal, resid, direc, norm_now)
    )
    filled = good * data_ref[...] + (1.0 - good) * signal
    for dst in range(n_src):
        out_ref[dst] = filled[:, dst * f_dev : (dst + 1) * f_dev]


def fill(pieces, cov, flags, f_dev):
    n_src, rows, lanes = pieces[0].shape
    groups = lanes // (2 * FB)
    n_freq = cov.shape[0]

    def body(*refs):
        fill_kernel(len(pieces), *refs)

    return pl.pallas_call(
        body,
        in_specs=[pl.BlockSpec(memory_space=pltpu.VMEM)] * (len(pieces) + 2),
        out_specs=pl.BlockSpec(memory_space=pltpu.VMEM),
        out_shape=jax.ShapeDtypeStruct((n_src, groups * rows, f_dev), jnp.float32),
        scratch_shapes=[
            pltpu.VMEM((groups * rows, n_freq), jnp.float32),
            pltpu.VMEM((n_freq, n_freq), jnp.bfloat16),
            pltpu.VMEM((n_freq, n_freq), jnp.bfloat16),
        ],
        compiler_params=params(),
        cost_estimate=pl.CostEstimate(
            flops=2 * ITERS * 3 * groups * rows * n_freq * n_freq,
            bytes_accessed=4 * n_freq * n_freq,
            transcendentals=0,
        ),
        name="fill",
    )(*pieces, cov, flags)


def make_tables(m_modes, n_tm, n_slots, t_dev):
    me = lax.axis_index("tm")
    n_time = t_dev * n_tm
    n_modes = n_tm * n_slots
    place = jnp.arange(n_modes, dtype=jnp.int32)
    source = (me ^ (place // n_slots)) * n_slots + place % n_slots
    hit = source[:, None] == place[None, :]
    modes = jnp.sum(jnp.where(hit, m_modes[None, :], 0), axis=1, dtype=jnp.int32)
    times = me * t_dev + jnp.arange(t_dev * FB, dtype=jnp.int32) // FB
    index = modes[:, None] * times[None, :] % n_time
    angle = 2.0 * math.pi / n_time * index.astype(jnp.float32)
    return jnp.concatenate([jnp.cos(angle), jnp.sin(angle)], axis=0)


def scatter_half(keep, send, bits, n_tm):
    terms = [keep]
    for place, bit in enumerate(bits):
        pairs = [(i, i ^ bit) for i in range(n_tm)]
        got = lax.ppermute(send, "tm", pairs)
        terms = [*terms, got]
        size = got.shape[0] // 2
        if size:
            send = sum(term[size : 2 * size] for term in terms)
    return terms


def per_device(vis, beam, fg_cov, flags, m_modes):
    t_dev, f_dev, width = vis.shape
    n_tm = lax.axis_size("tm")
    n_chan = lax.axis_size("chan")
    n_slots = m_modes.shape[0] // n_tm
    degrees = beam.shape[3]
    scale = 1.0 / math.sqrt(t_dev * n_tm)
    orders = bit_orders(n_tm)
    tab = make_tables(m_modes, n_tm, n_slots, t_dev)
    targets = [target_order(n_tm, bits) for bits in orders]
    pieces = []
    for chunk in range(f_dev // (2 * FB)):
        outs = transform(tab, vis, chunk, targets, n_slots, scale)
        parts = [
            scatter_half(outs[2 * h], outs[2 * h + 1], bits, n_tm) for h, bits in enumerate(orders)
        ]
        coeffs = project(parts, beam, chunk)
        blocks = coeffs.reshape(n_chan, coeffs.shape[0] // n_chan, coeffs.shape[1])
        pieces.append(lax.all_to_all(blocks, "chan", split_axis=0, concat_axis=0, tiled=True))
    whole = fill(pieces, fg_cov, flags[None, :], f_dev)
    back = lax.all_to_all(whole, "chan", split_axis=0, concat_axis=0, tiled=True)
    pairs = n_slots // 2
    back = back.reshape(pairs, n_chan // pairs, 2, 2, -1, f_dev)
    return back.transpose(0, 2, 3, 1, 4, 5).reshape(n_slots, 2, degrees, f_dev)


def solution(mesh):
    placed = (P("tm", "chan", None), P("tm", "chan", None, None, None), P(), P(), P())
    return jax.shard_map(
        per_device,
        mesh=mesh,
        in_specs=placed,
        out_specs=P("tm", None, None, "chan"),
        check_vma=False,
    )
```

```python
import math

import jax
import jax.numpy as jnp
from jax import lax
from jax.experimental import pallas as pl
from jax.experimental.pallas import tpu as pltpu
from jax.sharding import PartitionSpec as P

ITERS = 10
EPS = 1e-06
FB = 16
VMEM_LIMIT = 32 * 1024 * 1024


def params(**kwargs):
    return pltpu.CompilerParams(vmem_limit_bytes=VMEM_LIMIT, **kwargs)


def bit_orders(n_tm):
    bits = [1 << i for i in range(n_tm.bit_length() - 1)]
    return bits, bits[::-1]


def target_order(n_tm, bits):
    return sorted(range(n_tm), key=lambda r: [int(bool(r & b)) for b in bits])


def transform_kernel(orders, n_slots, scale, tab_ref, vis_ref, *refs):
    outs, full_ref = refs[:-1], refs[-1]
    n_rows = tab_ref.shape[0] // 2
    n_time, _, width = vis_ref.shape
    half = width // 2
    depth = n_time * FB
    sub = lax.broadcasted_iota(jnp.int32, (FB, depth), 0)
    lane = lax.broadcasted_iota(jnp.int32, (FB, depth), 1)
    same = lane % FB == sub
    for row in range(2 * n_rows):
        wide = jnp.broadcast_to(tab_ref[row : row + 1, :], (FB, depth))
        full_ref[row * FB : (row + 1) * FB, :] = jnp.where(same, wide, 0.0).astype(jnp.bfloat16)
    for part, order in enumerate(orders):
        data = vis_ref[:, part * FB : (part + 1) * FB, :].reshape(depth, width)
        prod = jnp.dot(full_ref[...], data, preferred_element_type=jnp.float32)
        cos_part, sin_part = prod[: n_rows * FB], prod[n_rows * FB :]
        real = (cos_part[:, :half] + sin_part[:, half:]) * scale
        imag = (cos_part[:, half:] - sin_part[:, :half]) * scale
        keep, send = outs[2 * part], outs[2 * part + 1]
        n_keep = keep.shape[0]
        for place, r in enumerate(order):
            out = keep if place < n_keep else send
            for j in range(n_slots):
                at = (r * n_slots + j) * FB
                out[place % n_keep, j, :, :half] = real[at : at + FB]
                out[place % n_keep, j, :, half:] = imag[at : at + FB]


def transform(tab, vis, chunk, orders, n_slots, scale):
    n_time, _, width = vis.shape
    n_tm = len(orders[0])
    depth = n_time * FB
    n_rows = n_tm * n_slots
    piece = jax.ShapeDtypeStruct((n_tm // 2, n_slots, FB, width), jnp.float32)

    def body(*refs):
        transform_kernel(orders, n_slots, scale, *refs)

    return pl.pallas_call(
        body,
        grid=(1,),
        in_specs=[
            pl.BlockSpec(tab.shape, lambda i: (0, 0)),
            pl.BlockSpec((n_time, 2 * FB, width), lambda i: (0, chunk, 0)),
        ],
        out_specs=[pl.BlockSpec(piece.shape, lambda i: (0, 0, 0, 0))] * 4,
        out_shape=[piece] * 4,
        scratch_shapes=[pltpu.VMEM((2 * n_rows * FB, depth), jnp.bfloat16)],
        compiler_params=params(),
        cost_estimate=pl.CostEstimate(
            flops=2 * 2 * n_rows * FB * depth * width * 2,
            bytes_accessed=n_time * 2 * FB * width * 2 + 4 * 4 * piece.size,
            transcendentals=0,
        ),
        name="transform",
    )(tab, vis)


def project_kernel(n_terms, f_block, *refs):
    terms = refs[: 2 * n_terms]
    beam_ref, out_ref, vis_ref = refs[2 * n_terms], refs[-2], refs[-1]
    step = pl.program_id(1)
    half = beam_ref.shape[-1]
    degrees = beam_ref.shape[3]

    @pl.when(step == 0)
    def _():
        for part in range(2):
            group = terms[part * n_terms : (part + 1) * n_terms]
            for s in range(2):
                total = group[0][0, s]
                for term in group[1:]:
                    total = total + term[0, s]
                real = total[:, :half].astype(jnp.bfloat16)
                imag = total[:, half:].astype(jnp.bfloat16)
                first = s * 4 * FB + part * FB
                second = first + 2 * FB
                vis_ref[first : first + FB, :half] = real
                vis_ref[second : second + FB, :half] = imag
                vis_ref[first : first + FB, half:] = -imag
                vis_ref[second : second + FB, half:] = real

    lane = lax.broadcasted_iota(jnp.int32, (degrees, 8 * FB), 1)
    shape = out_ref.shape
    acc = jnp.where(step == 0, 0.0, out_ref[...].reshape(degrees, 8 * FB))
    dims = (((1,), (1,)), ((), ()))
    for s in range(2):
        place = lane - (s * 4 * FB + step * f_block)
        real = beam_ref[s, :, 0].reshape(f_block * degrees, half)
        imag = beam_ref[s, :, 1].reshape(f_block * degrees, half)
        both = jnp.concatenate([real, imag], axis=1)
        prod = lax.dot_general(both, vis_ref[...], dims, preferred_element_type=jnp.float32)
        for f in range(f_block):
            hit = (place == f) | (place == f + 2 * FB)
            acc = jnp.where(hit, prod[f * degrees : (f + 1) * degrees], acc)
    out_ref[...] = acc.reshape(shape)


def project(parts, beam, chunk, n_chan, buffer, f_block=8):
    n_slots, f_dev, _, degrees, half = beam.shape
    n_terms = len(parts[0])
    pairs = n_slots // 2
    per_chunk = 2 * FB // f_block
    n_chunks = f_dev // (2 * FB)
    rows = pairs * degrees // n_chan
    terms = [term for group in parts for term in group]
    more = [] if buffer is None else [buffer]

    def body(*refs):
        project_kernel(n_terms, f_block, *refs)

    return pl.pallas_call(
        body,
        grid=(pairs, per_chunk),
        in_specs=[pl.BlockSpec((1, 2, FB, 2 * half), lambda i, k: (0, i, 0, 0))] * len(terms)
        + [
            pl.BlockSpec(
                (2, f_block, 2, degrees, half), lambda i, k: (i, chunk * per_chunk + k, 0, 0, 0)
            )
        ]
        + [pl.BlockSpec(memory_space=pl.ANY)] * len(more),
        out_specs=pl.BlockSpec(
            (n_chan // pairs, None, rows, 8 * FB), lambda i, k: (i, chunk, 0, 0)
        ),
        out_shape=jax.ShapeDtypeStruct((n_chan, n_chunks, rows, 8 * FB), jnp.float32),
        scratch_shapes=[pltpu.VMEM((8 * FB, 2 * half), jnp.bfloat16)],
        input_output_aliases={len(terms) + 1: 0} if more else {},
        compiler_params=params(),
        cost_estimate=pl.CostEstimate(
            flops=2 * n_slots * 2 * FB * 2 * degrees * half * 256,
            bytes_accessed=n_slots * 2 * FB * 2 * degrees * half * 2,
            transcendentals=0,
        ),
        name="project",
    )(*terms, beam, *more)


def split_kernel(cov_ref, high_ref, low_ref):
    cov = cov_ref[...]
    high = cov.astype(jnp.bfloat16)
    high_ref[...] = high
    low_ref[...] = (cov - high.astype(jnp.float32)).astype(jnp.bfloat16)


def split(cov, n_blocks=4):
    rows, cols = cov.shape
    spec = pl.BlockSpec((rows // n_blocks, cols), lambda i: (i, 0))
    half = jax.ShapeDtypeStruct(cov.shape, jnp.bfloat16)
    return pl.pallas_call(
        split_kernel,
        grid=(n_blocks,),
        in_specs=[spec],
        out_specs=[spec, spec],
        out_shape=[half, half],
        compiler_params=params(),
        cost_estimate=pl.CostEstimate(
            flops=4 * cov.size, bytes_accessed=8 * cov.size, transcendentals=0
        ),
        name="split",
    )(cov)


def fill_kernel(pieces_ref, high_ref, low_ref, flags_ref, out_ref, data_ref):
    n_src, n_chunks, rows, lanes = pieces_ref.shape
    groups = lanes // (2 * FB)
    f_dev = out_ref.shape[2]
    for src in range(n_src):
        for chunk in range(n_chunks):
            at = src * f_dev + chunk * 2 * FB
            for g in range(groups):
                data_ref[g * rows : (g + 1) * rows, at : at + 2 * FB] = pieces_ref[
                    src, chunk, :, g * 2 * FB : (g + 1) * 2 * FB
                ]
    good = 1.0 - flags_ref[...].astype(jnp.float32)
    n_rows = groups * rows

    def total(values):
        return jnp.sum(values, axis=1, keepdims=True)

    def covered(vec):
        top = vec.astype(jnp.bfloat16)
        rest = (vec - top.astype(jnp.float32)).astype(jnp.bfloat16)
        both = jnp.concatenate([top, rest], axis=0)
        wide = jnp.dot(both, high_ref[...], preferred_element_type=jnp.float32)
        thin = jnp.dot(top, low_ref[...], preferred_element_type=jnp.float32)
        return wide[:n_rows] + (wide[n_rows:] + thin)

    resid = good * data_ref[...]
    direc = resid
    norm_now = total(resid * resid)
    signal = jnp.zeros_like(resid)

    def advance(step, carry):
        signal, resid, direc, norm_now = carry
        image = covered(direc)
        shifted = direc + good * image
        alpha = norm_now / (total(direc * shifted) + EPS)
        signal = signal + alpha * image
        resid = resid - alpha * shifted
        norm_next = total(resid * resid)
        direc = resid + norm_next / (norm_now + EPS) * direc
        return signal, resid, direc, norm_next

    signal, resid, direc, norm_now = lax.fori_loop(
        0, ITERS, advance, (signal, resid, direc, norm_now)
    )
    filled = good * data_ref[...] + (1.0 - good) * signal
    for dst in range(n_src):
        out_ref[dst] = filled[:, dst * f_dev : (dst + 1) * f_dev]


def fill(pieces, high, low, flags, f_dev):
    n_src, _, rows, lanes = pieces.shape
    groups = lanes // (2 * FB)
    n_freq = high.shape[0]
    return pl.pallas_call(
        fill_kernel,
        in_specs=[pl.BlockSpec(memory_space=pltpu.VMEM)] * 4,
        out_specs=pl.BlockSpec(memory_space=pltpu.VMEM),
        out_shape=jax.ShapeDtypeStruct((n_src, groups * rows, f_dev), jnp.float32),
        scratch_shapes=[pltpu.VMEM((groups * rows, n_freq), jnp.float32)],
        compiler_params=params(),
        cost_estimate=pl.CostEstimate(
            flops=2 * ITERS * 3 * groups * rows * n_freq * n_freq,
            bytes_accessed=4 * n_freq * n_freq,
            transcendentals=0,
        ),
        name="fill",
    )(pieces, high, low, flags)


def make_tables(m_modes, n_tm, n_slots, t_dev):
    me = lax.axis_index("tm")
    n_time = t_dev * n_tm
    n_modes = n_tm * n_slots
    place = jnp.arange(n_modes, dtype=jnp.int32)
    source = (me ^ (place // n_slots)) * n_slots + place % n_slots
    hit = source[:, None] == place[None, :]
    modes = jnp.sum(jnp.where(hit, m_modes[None, :], 0), axis=1, dtype=jnp.int32)
    times = me * t_dev + jnp.arange(t_dev * FB, dtype=jnp.int32) // FB
    index = modes[:, None] * times[None, :] % n_time
    angle = 2.0 * math.pi / n_time * index.astype(jnp.float32)
    return jnp.concatenate([jnp.cos(angle), jnp.sin(angle)], axis=0)


def exchange(send, bit, n_tm):
    return lax.ppermute(send, "tm", [(i, i ^ bit) for i in range(n_tm)])


def per_device(vis, beam, fg_cov, flags, m_modes):
    t_dev, f_dev, _ = vis.shape
    n_tm = lax.axis_size("tm")
    n_chan = lax.axis_size("chan")
    n_slots = m_modes.shape[0] // n_tm
    degrees = beam.shape[3]
    scale = 1.0 / math.sqrt(t_dev * n_tm)
    orders = bit_orders(n_tm)
    targets = [target_order(n_tm, bits) for bits in orders]
    n_chunks = f_dev // (2 * FB)
    tab = make_tables(m_modes, n_tm, n_slots, t_dev)

    parts = [None] * n_chunks
    sends = [None] * n_chunks

    def begin(chunk):
        outs = transform(tab, vis, chunk, targets, n_slots, scale)
        parts[chunk] = [[outs[0]], [outs[2]]]
        sends[chunk] = [outs[1], outs[3]]

    def go_on(chunk, place):
        for h, bits in enumerate(orders):
            got = exchange(sends[chunk][h], bits[place], n_tm)
            parts[chunk][h].append(got)
            size = got.shape[0] // 2
            sends[chunk][h] = sum(term[size : 2 * size] for term in parts[chunk][h])

    n_steps = len(orders[0])
    high = low = None
    for chunk in range(n_chunks + n_steps - 1):
        if chunk < n_chunks:
            begin(chunk)
            go_on(chunk, 0)
        for place in range(1, n_steps):
            if 0 <= chunk - place < n_chunks:
                go_on(chunk - place, place)
                if place == 1 and chunk < n_chunks:
                    tab, *sends[chunk - 1] = lax.optimization_barrier((tab, *sends[chunk - 1]))
    high, low = split(fg_cov)

    coeffs = None
    for chunk in range(n_chunks):
        coeffs = project(parts[chunk], beam, chunk, n_chan, coeffs)
    pieces = lax.all_to_all(coeffs, "chan", split_axis=0, concat_axis=0, tiled=True)
    whole = fill(pieces, high, low, flags[None, :], f_dev)
    back = lax.all_to_all(whole, "chan", split_axis=0, concat_axis=0, tiled=True)
    pairs = n_slots // 2
    back = back.reshape(pairs, n_chan // pairs, 2, 2, -1, f_dev)
    return back.transpose(0, 2, 3, 1, 4, 5).reshape(n_slots, 2, degrees, f_dev)


def solution(mesh):
    placed = (P("tm", "chan", None), P("tm", "chan", None, None, None), P(), P(), P())
    return jax.shard_map(
        per_device,
        mesh=mesh,
        in_specs=placed,
        out_specs=P("tm", None, None, "chan"),
        check_vma=False,
    )
```

```python
import math

import jax
import jax.numpy as jnp
from jax import lax
from jax.experimental import pallas as pl
from jax.experimental.pallas import tpu as pltpu
from jax.sharding import PartitionSpec as P

ITERS = 10
EPS = 1e-06
FB = 16


def params(mebibytes):
    return pltpu.CompilerParams(vmem_limit_bytes=mebibytes * 1024 * 1024)


def bit_orders(n_tm):
    bits = [1 << i for i in range(n_tm.bit_length() - 1)]
    return bits, bits[::-1]


def target_order(n_tm, bits):
    return sorted(range(n_tm), key=lambda r: [int(bool(r & b)) for b in bits])


def transform_kernel(orders, n_slots, start, units, modes_ref, vis_ref, *refs):
    outs, (held_ref, full_ref, sems) = refs[:-3], refs[-3:]
    _, n_dev_time, _, width = held_ref.shape
    n_tm = len(orders[0])
    n_time = n_dev_time * n_tm
    n_rows = n_tm * n_slots
    half = width // 2
    depth = n_dev_time * FB
    scale = 1.0 / math.sqrt(n_time)

    def copy(group):
        source = vis_ref.at[:, pl.ds(start + group * FB, FB), :]
        return pltpu.make_async_copy(source, held_ref.at[group], sems.at[group])

    for group in range(2 * units):
        copy(group).start()

    me = lax.axis_index("tm")
    row = lax.broadcasted_iota(jnp.int32, (n_rows, depth), 0)
    lane = lax.broadcasted_iota(jnp.int32, (n_rows, depth), 1)
    modes = jnp.zeros((n_rows, depth), jnp.int32)
    for r in range(n_tm):
        for j in range(n_slots):
            modes = jnp.where(row == r * n_slots + j, modes_ref[(me ^ r) * n_slots + j], modes)
    index = modes * (me * n_dev_time + lax.div(lane, FB))
    index = index & (n_time - 1) if n_time & (n_time - 1) == 0 else lax.rem(index, n_time)
    angle = 2.0 * math.pi / n_time * index.astype(jnp.float32)
    sub = lax.broadcasted_iota(jnp.int32, (FB, depth), 0)
    same = lax.rem(lax.broadcasted_iota(jnp.int32, (FB, depth), 1), FB) == sub
    for base, table in ((0, jnp.cos(angle)), (n_rows, jnp.sin(angle))):
        for k in range(n_rows):
            wide = jnp.broadcast_to(table[k : k + 1, :], (FB, depth))
            at = (base + k) * FB
            full_ref[at : at + FB, :] = jnp.where(same, wide, 0.0).astype(jnp.bfloat16)

    for group in range(2 * units):
        part, place_f = group // units, group % units * FB
        order, keep, send = orders[part], outs[2 * part], outs[2 * part + 1]
        n_keep = keep.shape[0]
        copy(group).wait()
        data = held_ref[group].reshape(depth, width)
        prod = jnp.dot(full_ref[...], data, preferred_element_type=jnp.float32)
        cos_part, sin_part = prod[: n_rows * FB], prod[n_rows * FB :]
        real = (cos_part[:, :half] + sin_part[:, half:]) * scale
        imag = (cos_part[:, half:] - sin_part[:, :half]) * scale
        for place, r in enumerate(order):
            out = keep if place < n_keep else send
            for j in range(n_slots):
                at = (r * n_slots + j) * FB
                out[place % n_keep, j, place_f : place_f + FB, :half] = real[at : at + FB]
                out[place % n_keep, j, place_f : place_f + FB, half:] = imag[at : at + FB]


def transform(modes, vis, start, units, orders, n_slots):
    n_time, _, width = vis.shape
    n_tm = len(orders[0])
    depth = n_time * FB
    n_rows = n_tm * n_slots
    piece = jax.ShapeDtypeStruct((n_tm // 2, n_slots, units * FB, width), jnp.float32)

    def body(*refs):
        transform_kernel(orders, n_slots, start, units, *refs)

    return pl.pallas_call(
        body,
        in_specs=[
            pl.BlockSpec(memory_space=pltpu.SMEM),
            pl.BlockSpec(memory_space=pltpu.HBM),
        ],
        out_specs=[pl.BlockSpec(memory_space=pltpu.VMEM)] * 4,
        out_shape=[piece] * 4,
        scratch_shapes=[
            pltpu.VMEM((2 * units, n_time, FB, width), jnp.bfloat16),
            pltpu.VMEM((2 * n_rows * FB, depth), jnp.bfloat16),
            pltpu.SemaphoreType.DMA((2 * units,)),
        ],
        compiler_params=params(50),
        cost_estimate=pl.CostEstimate(
            flops=2 * 2 * n_rows * FB * depth * width * 2 * units,
            bytes_accessed=n_time * 2 * FB * units * width * 2 + 4 * 4 * piece.size,
            transcendentals=0,
        ),
        name="transform",
    )(modes, vis)


def project_kernel(n_terms, start, units, *refs):
    terms = refs[: 2 * n_terms]
    beam_ref, out_ref, held_ref, vis_ref, sems = refs[2 * n_terms], *refs[-4:]
    n_slots, _, _, degrees, half = beam_ref.shape
    pairs = n_slots // 2
    pieces = [(u, i, s, h) for u in range(units) for i in range(pairs) for s in range(2) for h in range(2)]

    def copy(at):
        u, i, s, h = pieces[at]
        source = beam_ref.at[2 * i + s, pl.ds(start + (2 * u + h) * FB, FB)]
        return pltpu.make_async_copy(source, held_ref.at[at], sems.at[at])

    for at in range(len(pieces)):
        copy(at).start()

    for u in range(units):
        for h in range(2):
            part, place = (2 * u + h) // units, (2 * u + h) % units * FB
            group = terms[part * n_terms : (part + 1) * n_terms]
            for j in range(n_slots):
                total = group[0][0, j, place : place + FB, :]
                for term in group[1:]:
                    total = total + term[0, j, place : place + FB, :]
                real = total[:, :half].astype(jnp.bfloat16)
                imag = total[:, half:].astype(jnp.bfloat16)
                first = j % 2 * 4 * FB + h * FB
                second = first + 2 * FB
                at = u * pairs + j // 2
                vis_ref[at, first : first + FB, :half] = real
                vis_ref[at, second : second + FB, :half] = imag
                vis_ref[at, first : first + FB, half:] = -imag
                vis_ref[at, second : second + FB, half:] = real

    lane = lax.broadcasted_iota(jnp.int32, (degrees, 8 * FB), 1)
    dims = (((1,), (1,)), ((), ()))
    shape = (out_ref.shape[0] // pairs, out_ref.shape[2], 8 * FB)
    acc = None
    for at, (u, i, s, h) in enumerate(pieces):
        if s == 0 and h == 0:
            acc = jnp.zeros((degrees, 8 * FB), jnp.float32)
        copy(at).wait()
        real = held_ref[at, :, 0].reshape(FB * degrees, half)
        imag = held_ref[at, :, 1].reshape(FB * degrees, half)
        both = jnp.concatenate([real, imag], axis=1)
        prod = lax.dot_general(
            both, vis_ref[u * pairs + i], dims, preferred_element_type=jnp.float32
        )
        for f in range(FB):
            place = s * 4 * FB + h * FB + f
            hit = (lane == place) | (lane == place + 2 * FB)
            acc = jnp.where(hit, prod[f * degrees : (f + 1) * degrees], acc)
        if s == 1 and h == 1:
            out_ref[i * shape[0] : (i + 1) * shape[0], u] = acc.reshape(shape)


def project(parts, beam, start, units, n_chan, buffer):
    n_slots, f_dev, _, degrees, half = beam.shape
    n_terms = len(parts[0])
    pairs = n_slots // 2
    n_units = f_dev // (2 * FB)
    rows = pairs * degrees // n_chan
    terms = [term for group in parts for term in group]
    more = [] if buffer is None else [buffer]
    place = start // (2 * FB) // units
    n_pieces = units * n_slots * 2

    def body(*refs):
        project_kernel(n_terms, start, units, *refs)

    term_spec = pl.BlockSpec((1, n_slots, units * FB, 2 * half), lambda i: (0, 0, 0, 0))
    return pl.pallas_call(
        body,
        grid=(1,),
        in_specs=[term_spec] * len(terms)
        + [pl.BlockSpec(memory_space=pltpu.HBM)]
        + [pl.BlockSpec(memory_space=pl.ANY)] * len(more),
        out_specs=pl.BlockSpec((n_chan, units, rows, 8 * FB), lambda i: (0, place, 0, 0)),
        out_shape=jax.ShapeDtypeStruct((n_chan, n_units, rows, 8 * FB), jnp.float32),
        scratch_shapes=[
            pltpu.VMEM((n_pieces, FB, 2, degrees, half), jnp.bfloat16),
            pltpu.VMEM((units * pairs, 8 * FB, 2 * half), jnp.bfloat16),
            pltpu.SemaphoreType.DMA((n_pieces,)),
        ],
        input_output_aliases={len(terms) + 1: 0} if more else {},
        compiler_params=params(14 + 12 * units),
        cost_estimate=pl.CostEstimate(
            flops=2 * n_slots * 2 * FB * units * 2 * degrees * half * 256,
            bytes_accessed=n_slots * 2 * FB * units * 2 * degrees * half * 2,
            transcendentals=0,
        ),
        name="project",
    )(*terms, beam, *more)


def split_kernel(cov_ref, high_ref, low_ref):
    cov = cov_ref[...]
    high = cov.astype(jnp.bfloat16)
    high_ref[...] = high
    low_ref[...] = (cov - high.astype(jnp.float32)).astype(jnp.bfloat16)


def split(cov, n_blocks=4):
    rows, cols = cov.shape
    spec = pl.BlockSpec((rows // n_blocks, cols), lambda i: (i, 0))
    half = jax.ShapeDtypeStruct(cov.shape, jnp.bfloat16)
    return pl.pallas_call(
        split_kernel,
        grid=(n_blocks,),
        in_specs=[spec],
        out_specs=[spec, spec],
        out_shape=[half, half],
        compiler_params=params(16),
        cost_estimate=pl.CostEstimate(
            flops=4 * cov.size, bytes_accessed=8 * cov.size, transcendentals=0
        ),
        name="split",
    )(cov)


def fill_kernel(pieces_ref, high_ref, low_ref, flags_ref, out_ref, data_ref):
    n_src, n_chunks, rows, lanes = pieces_ref.shape
    groups = lanes // (2 * FB)
    f_dev = out_ref.shape[2]
    for src in range(n_src):
        for chunk in range(n_chunks):
            at = src * f_dev + chunk * 2 * FB
            for g in range(groups):
                data_ref[g * rows : (g + 1) * rows, at : at + 2 * FB] = pieces_ref[
                    src, chunk, :, g * 2 * FB : (g + 1) * 2 * FB
                ]
    good = 1.0 - flags_ref[...].astype(jnp.float32)
    n_rows = groups * rows

    def total(values):
        return jnp.sum(values, axis=1, keepdims=True)

    def covered(vec):
        top = vec.astype(jnp.bfloat16)
        rest = (vec - top.astype(jnp.float32)).astype(jnp.bfloat16)
        both = jnp.concatenate([top, rest], axis=0)
        wide = jnp.dot(both, high_ref[...], preferred_element_type=jnp.float32)
        thin = jnp.dot(top, low_ref[...], preferred_element_type=jnp.float32)
        return wide[:n_rows] + (wide[n_rows:] + thin)

    resid = good * data_ref[...]
    direc = resid
    norm_now = total(resid * resid)
    signal = jnp.zeros_like(resid)

    def advance(step, carry):
        signal, resid, direc, norm_now = carry
        image = covered(direc)
        shifted = direc + good * image
        alpha = norm_now / (total(direc * shifted) + EPS)
        signal = signal + alpha * image
        resid = resid - alpha * shifted
        norm_next = total(resid * resid)
        direc = resid + norm_next / (norm_now + EPS) * direc
        return signal, resid, direc, norm_next

    signal, resid, direc, norm_now = lax.fori_loop(
        0, ITERS, advance, (signal, resid, direc, norm_now)
    )
    filled = good * data_ref[...] + (1.0 - good) * signal
    for dst in range(n_src):
        out_ref[dst] = filled[:, dst * f_dev : (dst + 1) * f_dev]


def fill(pieces, high, low, flags, f_dev):
    n_src, _, rows, lanes = pieces.shape
    groups = lanes // (2 * FB)
    n_freq = high.shape[0]
    return pl.pallas_call(
        fill_kernel,
        in_specs=[pl.BlockSpec(memory_space=pltpu.VMEM)] * 4,
        out_specs=pl.BlockSpec(memory_space=pltpu.VMEM),
        out_shape=jax.ShapeDtypeStruct((n_src, groups * rows, f_dev), jnp.float32),
        scratch_shapes=[pltpu.VMEM((groups * rows, n_freq), jnp.float32)],
        compiler_params=params(24),
        cost_estimate=pl.CostEstimate(
            flops=2 * ITERS * 3 * groups * rows * n_freq * n_freq,
            bytes_accessed=4 * n_freq * n_freq,
            transcendentals=0,
        ),
        name="fill",
    )(pieces, high, low, flags)


def exchange(send, bit, n_tm):
    return lax.ppermute(send, "tm", [(i, i ^ bit) for i in range(n_tm)])


def make_chunks(n_units):
    sizes = [2, 1, 1] if n_units == 4 else [1] * n_units
    return [(sum(sizes[:i]), size) for i, size in enumerate(sizes)]


def per_device(vis, beam, fg_cov, flags, m_modes):
    f_dev = vis.shape[1]
    n_tm = lax.axis_size("tm")
    n_chan = lax.axis_size("chan")
    n_slots = m_modes.shape[0] // n_tm
    degrees = beam.shape[3]
    orders = bit_orders(n_tm)
    targets = [target_order(n_tm, bits) for bits in orders]
    chunks = make_chunks(f_dev // (2 * FB))
    n_chunks = len(chunks)
    n_steps = len(orders[0])
    high, low = split(fg_cov)

    parts = [None] * n_chunks
    sends = [None] * n_chunks

    def begin(chunk, modes):
        first, units = chunks[chunk]
        outs = transform(modes, vis, first * 2 * FB, units, targets, n_slots)
        parts[chunk] = [[outs[0]], [outs[2]]]
        sends[chunk] = [outs[1], outs[3]]

    def go_on(chunk, place):
        for h, bits in enumerate(orders):
            got = exchange(sends[chunk][h], bits[place], n_tm)
            parts[chunk][h].append(got)
            size = got.shape[0] // 2
            sends[chunk][h] = sum(term[size : 2 * size] for term in parts[chunk][h])

    modes = m_modes
    for chunk in range(n_chunks + n_steps - 1):
        if chunk < n_chunks:
            begin(chunk, modes)
            go_on(chunk, 0)
        for place in range(1, n_steps):
            if 0 <= chunk - place < n_chunks:
                last = chunk - place
                if place == 1 and last == 0:
                    *sends[last], high, low = lax.optimization_barrier((*sends[last], high, low))
                if place == 1 and chunk + 1 < n_chunks:
                    *sends[last], modes = lax.optimization_barrier((*sends[last], modes))
                go_on(last, place)

    coeffs = None
    for chunk, (first, units) in enumerate(chunks):
        coeffs = project(parts[chunk], beam, first * 2 * FB, units, n_chan, coeffs)
    pieces = lax.all_to_all(coeffs, "chan", split_axis=0, concat_axis=0, tiled=True)
    whole = fill(pieces, high, low, flags[None, :], f_dev)
    back = lax.all_to_all(whole, "chan", split_axis=0, concat_axis=0, tiled=True)
    pairs = n_slots // 2
    back = back.reshape(pairs, n_chan // pairs, 2, 2, -1, f_dev)
    return back.transpose(0, 2, 3, 1, 4, 5).reshape(n_slots, 2, degrees, f_dev)


def solution(mesh):
    placed = (P("tm", "chan", None), P("tm", "chan", None, None, None), P(), P(), P())
    return jax.shard_map(
        per_device,
        mesh=mesh,
        in_specs=placed,
        out_specs=P("tm", None, None, "chan"),
        check_vma=False,
    )
```

```python
import math

import jax
import jax.numpy as jnp
from jax import lax
from jax.experimental import pallas as pl
from jax.experimental.pallas import tpu as pltpu
from jax.sharding import PartitionSpec as P

ITERS = 10
EPS = 1e-06
FB = 16


def params(mebibytes):
    return pltpu.CompilerParams(vmem_limit_bytes=mebibytes * 1024 * 1024)


def bit_orders(n_tm):
    bits = [1 << i for i in range(n_tm.bit_length() - 1)]
    return bits, bits[::-1]


def target_order(n_tm, bits):
    return sorted(range(n_tm), key=lambda r: [int(bool(r & b)) for b in bits])


def transform_kernel(orders, n_slots, start, units, tab_ref, vis_ref, *refs):
    outs, (held_ref, full_ref, sems) = refs[:-3], refs[-3:]
    _, n_dev_time, _, width = held_ref.shape
    n_tm = len(orders[0])
    n_time = n_dev_time * n_tm
    n_rows = n_tm * n_slots
    half = width // 2
    depth = n_dev_time * FB
    scale = 1.0 / math.sqrt(n_time)

    def copy(group):
        source = vis_ref.at[:, pl.ds(start + group * FB, FB), :]
        return pltpu.make_async_copy(source, held_ref.at[group], sems.at[group])

    for group in range(2 * units):
        copy(group).start()

    me = lax.axis_index("tm")
    sub = lax.broadcasted_iota(jnp.int32, (FB, depth), 0)
    same = lax.rem(lax.broadcasted_iota(jnp.int32, (FB, depth), 1), FB) == sub
    for r in range(n_tm):
        for j in range(n_slots):
            for which in range(2):
                mode = which * n_rows + (me ^ r) * n_slots + j
                wide = jnp.broadcast_to(tab_ref[pl.ds(mode, 1), :], (FB, depth))
                at = (which * n_rows + r * n_slots + j) * FB
                full_ref[at : at + FB, :] = jnp.where(same, wide, 0.0).astype(jnp.bfloat16)

    for group in range(2 * units):
        part, place_f = group // units, group % units * FB
        order, keep, send = orders[part], outs[2 * part], outs[2 * part + 1]
        n_keep = keep.shape[0]
        copy(group).wait()
        data = held_ref[group].reshape(depth, width)
        prod = jnp.dot(full_ref[...], data, preferred_element_type=jnp.float32)
        cos_part, sin_part = prod[: n_rows * FB], prod[n_rows * FB :]
        real = (cos_part[:, :half] + sin_part[:, half:]) * scale
        imag = (cos_part[:, half:] - sin_part[:, :half]) * scale
        for place, r in enumerate(order):
            out = keep if place < n_keep else send
            for j in range(n_slots):
                at = (r * n_slots + j) * FB
                out[place % n_keep, j, place_f : place_f + FB, :half] = real[at : at + FB]
                out[place % n_keep, j, place_f : place_f + FB, half:] = imag[at : at + FB]


def transform(tab, vis, start, units, orders, n_slots):
    n_time, _, width = vis.shape
    n_tm = len(orders[0])
    depth = n_time * FB
    n_rows = n_tm * n_slots
    piece = jax.ShapeDtypeStruct((n_tm // 2, n_slots, units * FB, width), jnp.float32)

    def body(*refs):
        transform_kernel(orders, n_slots, start, units, *refs)

    return pl.pallas_call(
        body,
        in_specs=[
            pl.BlockSpec(memory_space=pltpu.VMEM),
            pl.BlockSpec(memory_space=pltpu.HBM),
        ],
        out_specs=[pl.BlockSpec(memory_space=pltpu.VMEM)] * 4,
        out_shape=[piece] * 4,
        scratch_shapes=[
            pltpu.VMEM((2 * units, n_time, FB, width), jnp.bfloat16),
            pltpu.VMEM((2 * n_rows * FB, depth), jnp.bfloat16),
            pltpu.SemaphoreType.DMA((2 * units,)),
        ],
        compiler_params=params(50),
        cost_estimate=pl.CostEstimate(
            flops=2 * 2 * n_rows * FB * depth * width * 2 * units,
            bytes_accessed=n_time * 2 * FB * units * width * 2 + 4 * 4 * piece.size,
            transcendentals=0,
        ),
        name="transform",
    )(tab, vis)


def project_kernel(n_terms, start, units, *refs):
    terms = refs[: 2 * n_terms]
    beam_ref, out_ref, held_ref, vis_ref, flat_ref, sems = refs[2 * n_terms], *refs[-5:]
    n_slots, _, _, degrees, half = beam_ref.shape
    pairs = n_slots // 2
    pieces = [(u, i, s, h) for u in range(units) for i in range(pairs) for s in range(2) for h in range(2)]

    def copy(at):
        u, i, s, h = pieces[at]
        source = beam_ref.at[2 * i + s, pl.ds(start + (2 * u + h) * FB, FB)]
        return pltpu.make_async_copy(source, held_ref.at[at], sems.at[at])

    for at in range(len(pieces)):
        copy(at).start()

    for at, (u, i, s, h) in enumerate(pieces):
        part, place = (2 * u + h) // units, (2 * u + h) % units * FB
        total = None
        for term in terms[part * n_terms : (part + 1) * n_terms]:
            value = term[0, 2 * i + s, place : place + FB, :]
            total = value if total is None else total + value
        real = total[:, :half].astype(jnp.bfloat16)
        imag = total[:, half:].astype(jnp.bfloat16)
        vis_ref[at, :FB, :half] = real
        vis_ref[at, FB:, :half] = imag
        vis_ref[at, :FB, half:] = -imag
        vis_ref[at, FB:, half:] = real

    dims = (((1,), (1,)), ((), ()))
    shape = (out_ref.shape[0] // pairs, out_ref.shape[2], 8 * FB)
    per_tile = 128 // degrees
    sub = lax.broadcasted_iota(jnp.int32, (8, 128), 0)
    for at, (u, i, s, h) in enumerate(pieces):
        copy(at).wait()
        real = held_ref[at, :, 0].reshape(FB * degrees, half)
        imag = held_ref[at, :, 1].reshape(FB * degrees, half)
        both = jnp.concatenate([real, imag], axis=1)
        prod = lax.dot_general(vis_ref[at], both, dims, preferred_element_type=jnp.float32)
        for p in range(2):
            for g in range(FB // 8):
                own = prod[p * FB + g * 8 : p * FB + g * 8 + 8, g * 8 * degrees : (g + 1) * 8 * degrees]
                pick = own[:, :128]
                for v in range(1, 8 // per_tile):
                    pick = jnp.where(sub // per_tile == v, own[:, v * 128 : (v + 1) * 128], pick)
                if per_tile == 2:
                    pick = jnp.where(sub % 2 == 0, pick, pltpu.roll(pick, degrees, 1))
                row = s * 4 * FB + p * 2 * FB + h * FB + g * 8
                flat_ref[row : row + 8, :] = pick
        if s == 1 and h == 1:
            turned = flat_ref[...].T[:degrees]
            out_ref[i * shape[0] : (i + 1) * shape[0], u] = turned.reshape(shape)


def project(parts, beam, start, units, n_chan, buffer):
    n_slots, f_dev, _, degrees, half = beam.shape
    n_terms = len(parts[0])
    pairs = n_slots // 2
    n_units = f_dev // (2 * FB)
    rows = pairs * degrees // n_chan
    terms = [term for group in parts for term in group]
    more = [] if buffer is None else [buffer]
    place = start // (2 * FB) // units
    n_pieces = units * n_slots * 2

    def body(*refs):
        project_kernel(n_terms, start, units, *refs)

    term_spec = pl.BlockSpec((1, n_slots, units * FB, 2 * half), lambda i: (0, 0, 0, 0))
    return pl.pallas_call(
        body,
        grid=(1,),
        in_specs=[term_spec] * len(terms)
        + [pl.BlockSpec(memory_space=pltpu.HBM)]
        + [pl.BlockSpec(memory_space=pl.ANY)] * len(more),
        out_specs=pl.BlockSpec((n_chan, units, rows, 8 * FB), lambda i: (0, place, 0, 0)),
        out_shape=jax.ShapeDtypeStruct((n_chan, n_units, rows, 8 * FB), jnp.float32),
        scratch_shapes=[
            pltpu.VMEM((n_pieces, FB, 2, degrees, half), jnp.bfloat16),
            pltpu.VMEM((n_pieces, 2 * FB, 2 * half), jnp.bfloat16),
            pltpu.VMEM((8 * FB, 128), jnp.float32),
            pltpu.SemaphoreType.DMA((n_pieces,)),
        ],
        input_output_aliases={len(terms) + 1: 0} if more else {},
        compiler_params=params(14 + 12 * units),
        cost_estimate=pl.CostEstimate(
            flops=2 * n_slots * 2 * FB * units * 2 * degrees * half * 256,
            bytes_accessed=n_slots * 2 * FB * units * 2 * degrees * half * 2,
            transcendentals=0,
        ),
        name="project",
    )(*terms, beam, *more)


def split_kernel(cov_ref, high_ref, low_ref):
    cov = cov_ref[...]
    high = cov.astype(jnp.bfloat16)
    high_ref[...] = high
    low_ref[...] = (cov - high.astype(jnp.float32)).astype(jnp.bfloat16)


def split(cov, n_blocks=4):
    rows, cols = cov.shape
    spec = pl.BlockSpec((rows // n_blocks, cols), lambda i: (i, 0))
    half = jax.ShapeDtypeStruct(cov.shape, jnp.bfloat16)
    return pl.pallas_call(
        split_kernel,
        grid=(n_blocks,),
        in_specs=[spec],
        out_specs=[spec, spec],
        out_shape=[half, half],
        compiler_params=params(16),
        cost_estimate=pl.CostEstimate(
            flops=4 * cov.size, bytes_accessed=8 * cov.size, transcendentals=0
        ),
        name="split",
    )(cov)


def fill_kernel(pieces_ref, high_ref, low_ref, flags_ref, out_ref, data_ref):
    n_src, n_chunks, rows, lanes = pieces_ref.shape
    groups = lanes // (2 * FB)
    f_dev = out_ref.shape[2]
    for src in range(n_src):
        for chunk in range(n_chunks):
            at = src * f_dev + chunk * 2 * FB
            for g in range(groups):
                data_ref[g * rows : (g + 1) * rows, at : at + 2 * FB] = pieces_ref[
                    src, chunk, :, g * 2 * FB : (g + 1) * 2 * FB
                ]
    good = 1.0 - flags_ref[...].astype(jnp.float32)
    n_rows = groups * rows

    def total(values):
        return jnp.sum(values, axis=1, keepdims=True)

    def covered(vec):
        top = vec.astype(jnp.bfloat16)
        rest = (vec - top.astype(jnp.float32)).astype(jnp.bfloat16)
        both = jnp.concatenate([top, rest], axis=0)
        wide = jnp.dot(both, high_ref[...], preferred_element_type=jnp.float32)
        thin = jnp.dot(top, low_ref[...], preferred_element_type=jnp.float32)
        return wide[:n_rows] + (wide[n_rows:] + thin)

    resid = good * data_ref[...]
    direc = resid
    norm_now = total(resid * resid)
    signal = jnp.zeros_like(resid)

    def advance(step, carry):
        signal, resid, direc, norm_now = carry
        image = covered(direc)
        shifted = direc + good * image
        alpha = norm_now / (total(direc * shifted) + EPS)
        signal = signal + alpha * image
        resid = resid - alpha * shifted
        norm_next = total(resid * resid)
        direc = resid + norm_next / (norm_now + EPS) * direc
        return signal, resid, direc, norm_next

    signal, resid, direc, norm_now = lax.fori_loop(
        0, ITERS, advance, (signal, resid, direc, norm_now)
    )
    filled = good * data_ref[...] + (1.0 - good) * signal
    for dst in range(n_src):
        out_ref[dst] = filled[:, dst * f_dev : (dst + 1) * f_dev]


def fill(pieces, high, low, flags, f_dev):
    n_src, _, rows, lanes = pieces.shape
    groups = lanes // (2 * FB)
    n_freq = high.shape[0]
    return pl.pallas_call(
        fill_kernel,
        in_specs=[pl.BlockSpec(memory_space=pltpu.VMEM)] * 4,
        out_specs=pl.BlockSpec(memory_space=pltpu.VMEM),
        out_shape=jax.ShapeDtypeStruct((n_src, groups * rows, f_dev), jnp.float32),
        scratch_shapes=[pltpu.VMEM((groups * rows, n_freq), jnp.float32)],
        compiler_params=params(24),
        cost_estimate=pl.CostEstimate(
            flops=2 * ITERS * 3 * groups * rows * n_freq * n_freq,
            bytes_accessed=4 * n_freq * n_freq,
            transcendentals=0,
        ),
        name="fill",
    )(pieces, high, low, flags)


def make_tables(m_modes, n_tm, t_dev):
    n_time = t_dev * n_tm
    times = lax.axis_index("tm") * t_dev + jnp.arange(t_dev * FB, dtype=jnp.int32) // FB
    index = m_modes[:, None] * times[None, :] % n_time
    angle = 2.0 * math.pi / n_time * index.astype(jnp.float32)
    return jnp.concatenate([jnp.cos(angle), jnp.sin(angle)], axis=0)


def exchange(send, bit, n_tm):
    return lax.ppermute(send, "tm", [(i, i ^ bit) for i in range(n_tm)])


def make_chunks(n_units):
    sizes = [2, 1, 1] if n_units == 4 else [1] * n_units
    return [(sum(sizes[:i]), size) for i, size in enumerate(sizes)]


def per_device(vis, beam, fg_cov, flags, m_modes):
    t_dev, f_dev, _ = vis.shape
    n_tm = lax.axis_size("tm")
    n_chan = lax.axis_size("chan")
    n_slots = m_modes.shape[0] // n_tm
    degrees = beam.shape[3]
    orders = bit_orders(n_tm)
    targets = [target_order(n_tm, bits) for bits in orders]
    chunks = make_chunks(f_dev // (2 * FB))
    n_chunks = len(chunks)
    n_steps = len(orders[0])
    high, low = split(fg_cov)

    parts = [None] * n_chunks
    sends = [None] * n_chunks

    def begin(chunk, tab):
        first, units = chunks[chunk]
        outs = transform(tab, vis, first * 2 * FB, units, targets, n_slots)
        parts[chunk] = [[outs[0]], [outs[2]]]
        sends[chunk] = [outs[1], outs[3]]

    def go_on(chunk, place):
        for h, bits in enumerate(orders):
            got = exchange(sends[chunk][h], bits[place], n_tm)
            parts[chunk][h].append(got)
            size = got.shape[0] // 2
            sends[chunk][h] = sum(term[size : 2 * size] for term in parts[chunk][h])

    tab = make_tables(m_modes, n_tm, t_dev)
    for chunk in range(n_chunks + n_steps - 1):
        if chunk < n_chunks:
            begin(chunk, tab)
            go_on(chunk, 0)
        for place in range(1, n_steps):
            if 0 <= chunk - place < n_chunks:
                last = chunk - place
                if place == 1 and last == 0:
                    *sends[last], high, low = lax.optimization_barrier((*sends[last], high, low))
                if place == 1 and chunk + 1 < n_chunks:
                    *sends[last], tab = lax.optimization_barrier((*sends[last], tab))
                go_on(last, place)

    coeffs = None
    for chunk, (first, units) in enumerate(chunks):
        coeffs = project(parts[chunk], beam, first * 2 * FB, units, n_chan, coeffs)
    pieces = lax.all_to_all(coeffs, "chan", split_axis=0, concat_axis=0, tiled=True)
    whole = fill(pieces, high, low, flags[None, :], f_dev)
    back = lax.all_to_all(whole, "chan", split_axis=0, concat_axis=0, tiled=True)
    pairs = n_slots // 2
    back = back.reshape(pairs, n_chan // pairs, 2, 2, -1, f_dev)
    return back.transpose(0, 2, 3, 1, 4, 5).reshape(n_slots, 2, degrees, f_dev)


def solution(mesh):
    placed = (P("tm", "chan", None), P("tm", "chan", None, None, None), P(), P(), P())
    return jax.shard_map(
        per_device,
        mesh=mesh,
        in_specs=placed,
        out_specs=P("tm", None, None, "chan"),
        check_vma=False,
    )
```

```python
import math

import jax
import jax.numpy as jnp
from jax import lax
from jax.experimental import pallas as pl
from jax.experimental.pallas import tpu as pltpu
from jax.sharding import PartitionSpec as P

ITERS = 10
EPS = 1e-06
FB = 16


def params(mebibytes):
    return pltpu.CompilerParams(vmem_limit_bytes=mebibytes * 1024 * 1024)


def bit_orders(n_tm):
    bits = [1 << i for i in range(n_tm.bit_length() - 1)]
    return bits, bits[::-1]


def target_order(n_tm, bits):
    return sorted(range(n_tm), key=lambda r: [int(bool(r & b)) for b in bits])


def transform_kernel(orders, n_slots, start, units, tab_ref, vis_ref, *refs):
    outs, (held_ref, full_ref, sems) = refs[:-3], refs[-3:]
    _, n_dev_time, _, width = held_ref.shape
    n_tm = len(orders[0])
    n_time = n_dev_time * n_tm
    n_rows = n_tm * n_slots
    half = width // 2
    depth = n_dev_time * FB
    scale = 1.0 / math.sqrt(n_time)

    def copies(unit):
        size = n_dev_time // 2
        for piece in range(2):
            times = pl.ds(piece * size, size)
            source = vis_ref.at[times, pl.ds(start + unit * 2 * FB, 2 * FB), :]
            target = held_ref.at[unit, times]
            yield pltpu.make_async_copy(source, target, sems.at[unit, piece])

    for unit in range(units):
        for copy in copies(unit):
            copy.start()

    me = lax.axis_index("tm")
    sub = lax.broadcasted_iota(jnp.int32, (FB, depth), 0)
    same = lax.rem(lax.broadcasted_iota(jnp.int32, (FB, depth), 1), FB) == sub
    for r in range(n_tm):
        for j in range(n_slots):
            for which in range(2):
                mode = which * n_rows + (me ^ r) * n_slots + j
                wide = jnp.broadcast_to(tab_ref[pl.ds(mode, 1), :], (FB, depth))
                at = (which * n_rows + r * n_slots + j) * FB
                full_ref[at : at + FB, :] = jnp.where(same, wide, 0.0).astype(jnp.bfloat16)

    for group in range(2 * units):
        part, place_f = group // units, group % units * FB
        order, keep, send = orders[part], outs[2 * part], outs[2 * part + 1]
        n_keep = keep.shape[0]
        if group % 2 == 0:
            for copy in copies(group // 2):
                copy.wait()
        first = group % 2 * FB
        data = held_ref[group // 2, :, first : first + FB, :].reshape(depth, width)
        prod = jnp.dot(full_ref[...], data, preferred_element_type=jnp.float32)
        cos_part, sin_part = prod[: n_rows * FB], prod[n_rows * FB :]
        real = (cos_part[:, :half] + sin_part[:, half:]) * scale
        imag = (cos_part[:, half:] - sin_part[:, :half]) * scale
        for place, r in enumerate(order):
            out = keep if place < n_keep else send
            for j in range(n_slots):
                at = (r * n_slots + j) * FB
                out[place % n_keep, j, place_f : place_f + FB, :half] = real[at : at + FB]
                out[place % n_keep, j, place_f : place_f + FB, half:] = imag[at : at + FB]


def transform(tab, vis, start, units, orders, n_slots):
    n_time, _, width = vis.shape
    n_tm = len(orders[0])
    depth = n_time * FB
    n_rows = n_tm * n_slots
    piece = jax.ShapeDtypeStruct((n_tm // 2, n_slots, units * FB, width), jnp.float32)

    def body(*refs):
        transform_kernel(orders, n_slots, start, units, *refs)

    return pl.pallas_call(
        body,
        in_specs=[
            pl.BlockSpec(memory_space=pltpu.VMEM),
            pl.BlockSpec(memory_space=pltpu.HBM),
        ],
        out_specs=[pl.BlockSpec(memory_space=pltpu.VMEM)] * 4,
        out_shape=[piece] * 4,
        scratch_shapes=[
            pltpu.VMEM((units, n_time, 2 * FB, width), jnp.bfloat16),
            pltpu.VMEM((2 * n_rows * FB, depth), jnp.bfloat16),
            pltpu.SemaphoreType.DMA((units, 2)),
        ],
        compiler_params=params(50),
        cost_estimate=pl.CostEstimate(
            flops=2 * 2 * n_rows * FB * depth * width * 2 * units,
            bytes_accessed=n_time * 2 * FB * units * width * 2 + 4 * 4 * piece.size,
            transcendentals=0,
        ),
        name="transform",
    )(tab, vis)


def project_kernel(n_terms, start, units, resident, *refs):
    terms = refs[: 2 * n_terms]
    beam_ref, out_ref, vis_ref, flat_ref = refs[2 * n_terms], *refs[-5:-2]
    held_ref, sems = refs[-2:]
    n_slots, _, _, degrees, half = beam_ref.shape
    pairs = n_slots // 2
    pieces = [(u, i, s, h) for u in range(units) for i in range(pairs) for s in range(2) for h in range(2)]

    def copy(at):
        u, i, s, h = pieces[at]
        source = beam_ref.at[2 * i + s, pl.ds(start + (2 * u + h) * FB, FB)]
        return pltpu.make_async_copy(source, held_ref.at[at], sems.at[at])

    if not resident:
        for at in range(len(pieces)):
            copy(at).start()

    for at, (u, i, s, h) in enumerate(pieces):
        part, place = (2 * u + h) // units, (2 * u + h) % units * FB
        total = None
        for term in terms[part * n_terms : (part + 1) * n_terms]:
            value = term[0, 2 * i + s, place : place + FB, :]
            total = value if total is None else total + value
        real = total[:, :half].astype(jnp.bfloat16)
        imag = total[:, half:].astype(jnp.bfloat16)
        vis_ref[at, :FB, :half] = real
        vis_ref[at, FB:, :half] = imag
        vis_ref[at, :FB, half:] = -imag
        vis_ref[at, FB:, half:] = real

    dims = (((1,), (1,)), ((), ()))
    shape = (out_ref.shape[0] // pairs, out_ref.shape[2], 8 * FB)
    per_tile = 128 // degrees
    sub = lax.broadcasted_iota(jnp.int32, (8, 128), 0)
    for at, (u, i, s, h) in enumerate(pieces):
        if resident:
            block = beam_ref.at[2 * i + s, pl.ds((2 * u + h) * FB, FB)]
        else:
            copy(at).wait()
            block = held_ref.at[at]
        real = block[:, 0].reshape(FB * degrees, half)
        imag = block[:, 1].reshape(FB * degrees, half)
        both = jnp.concatenate([real, imag], axis=1)
        prod = lax.dot_general(vis_ref[at], both, dims, preferred_element_type=jnp.float32)
        for p in range(2):
            for g in range(FB // 8):
                own = prod[p * FB + g * 8 : p * FB + g * 8 + 8, g * 8 * degrees : (g + 1) * 8 * degrees]
                pick = own[:, :128]
                for v in range(1, 8 // per_tile):
                    pick = jnp.where(sub // per_tile == v, own[:, v * 128 : (v + 1) * 128], pick)
                if per_tile == 2:
                    pick = jnp.where(sub % 2 == 0, pick, pltpu.roll(pick, degrees, 1))
                row = s * 4 * FB + p * 2 * FB + h * FB + g * 8
                flat_ref[row : row + 8, :] = pick
        if s == 1 and h == 1:
            turned = flat_ref[...].T[:degrees]
            out_ref[i * shape[0] : (i + 1) * shape[0], u] = turned.reshape(shape)


def load(beam, start, size):
    n_slots = beam.shape[0]
    pieces = [(j, f) for j in range(n_slots) for f in range(0, size, FB)]
    block = jax.ShapeDtypeStruct((n_slots, size, *beam.shape[2:]), beam.dtype)

    def body(beam_ref, out_ref, sems):
        copies = [
            pltpu.make_async_copy(
                beam_ref.at[j, pl.ds(start + f, FB)], out_ref.at[j, pl.ds(f, FB)], sems.at[at]
            )
            for at, (j, f) in enumerate(pieces)
        ]
        for copy in copies:
            copy.start()
        for copy in copies:
            copy.wait()

    return pl.pallas_call(
        body,
        in_specs=[pl.BlockSpec(memory_space=pltpu.HBM)],
        out_specs=pl.BlockSpec(memory_space=pltpu.VMEM),
        out_shape=block,
        scratch_shapes=[pltpu.SemaphoreType.DMA((len(pieces),))],
        compiler_params=params(20),
        cost_estimate=pl.CostEstimate(
            flops=0, bytes_accessed=4 * block.size, transcendentals=0
        ),
        name="load",
    )(beam)


def project(parts, beam, start, units, resident, n_chan, n_units, buffer):
    n_slots, _, _, degrees, half = beam.shape
    n_terms = len(parts[0])
    pairs = n_slots // 2
    rows = pairs * degrees // n_chan
    terms = [term for group in parts for term in group]
    more = [] if buffer is None else [buffer]
    place = start // (2 * FB) // units
    n_pieces = units * n_slots * 2

    def body(*refs):
        project_kernel(n_terms, start, units, resident, *refs)

    term_spec = pl.BlockSpec((1, n_slots, units * FB, 2 * half), lambda i: (0, 0, 0, 0))
    return pl.pallas_call(
        body,
        grid=(1,),
        in_specs=[term_spec] * len(terms)
        + [pl.BlockSpec(memory_space=pltpu.VMEM if resident else pltpu.HBM)]
        + [pl.BlockSpec(memory_space=pl.ANY)] * len(more),
        out_specs=pl.BlockSpec((n_chan, units, rows, 8 * FB), lambda i: (0, place, 0, 0)),
        out_shape=jax.ShapeDtypeStruct((n_chan, n_units, rows, 8 * FB), jnp.float32),
        scratch_shapes=[
            pltpu.VMEM((n_pieces, 2 * FB, 2 * half), jnp.bfloat16),
            pltpu.VMEM((8 * FB, 128), jnp.float32),
            pltpu.VMEM((1 if resident else n_pieces, FB, 2, degrees, half), jnp.bfloat16),
            pltpu.SemaphoreType.DMA((n_pieces,)),
        ],
        input_output_aliases={len(terms) + 1: 0} if more else {},
        compiler_params=params(10 if resident else 28),
        cost_estimate=pl.CostEstimate(
            flops=2 * n_slots * 2 * FB * units * 2 * degrees * half * 256,
            bytes_accessed=n_slots * 2 * FB * units * 2 * degrees * half * 2,
            transcendentals=0,
        ),
        name="project",
    )(*terms, beam, *more)


def split_kernel(cov_ref, high_ref, low_ref):
    cov = cov_ref[...]
    high = cov.astype(jnp.bfloat16)
    high_ref[...] = high
    low_ref[...] = (cov - high.astype(jnp.float32)).astype(jnp.bfloat16)


def split(cov, n_blocks=4):
    rows, cols = cov.shape
    spec = pl.BlockSpec((rows // n_blocks, cols), lambda i: (i, 0))
    half = jax.ShapeDtypeStruct(cov.shape, jnp.bfloat16)
    return pl.pallas_call(
        split_kernel,
        grid=(n_blocks,),
        in_specs=[spec],
        out_specs=[spec, spec],
        out_shape=[half, half],
        compiler_params=params(8),
        cost_estimate=pl.CostEstimate(
            flops=4 * cov.size, bytes_accessed=8 * cov.size, transcendentals=0
        ),
        name="split",
    )(cov)


def fill_kernel(pieces_ref, high_ref, low_ref, flags_ref, out_ref, data_ref):
    n_src, n_chunks, rows, lanes = pieces_ref.shape
    groups = lanes // (2 * FB)
    f_dev = out_ref.shape[2]
    for src in range(n_src):
        for chunk in range(n_chunks):
            at = src * f_dev + chunk * 2 * FB
            for g in range(groups):
                data_ref[g * rows : (g + 1) * rows, at : at + 2 * FB] = pieces_ref[
                    src, chunk, :, g * 2 * FB : (g + 1) * 2 * FB
                ]
    good = 1.0 - flags_ref[...].astype(jnp.float32)
    n_rows = groups * rows

    def total(values):
        return jnp.sum(values, axis=1, keepdims=True)

    def covered(vec):
        top = vec.astype(jnp.bfloat16)
        rest = (vec - top.astype(jnp.float32)).astype(jnp.bfloat16)
        both = jnp.concatenate([top, rest], axis=0)
        wide = jnp.dot(both, high_ref[...], preferred_element_type=jnp.float32)
        thin = jnp.dot(top, low_ref[...], preferred_element_type=jnp.float32)
        return wide[:n_rows] + (wide[n_rows:] + thin)

    resid = good * data_ref[...]
    direc = resid
    norm_now = total(resid * resid)
    signal = jnp.zeros_like(resid)

    def advance(step, carry):
        signal, resid, direc, norm_now = carry
        image = covered(direc)
        shifted = direc + good * image
        alpha = norm_now / (total(direc * shifted) + EPS)
        signal = signal + alpha * image
        resid = resid - alpha * shifted
        norm_next = total(resid * resid)
        direc = resid + norm_next / (norm_now + EPS) * direc
        return signal, resid, direc, norm_next

    signal, resid, direc, norm_now = lax.fori_loop(
        0, ITERS, advance, (signal, resid, direc, norm_now)
    )
    filled = good * data_ref[...] + (1.0 - good) * signal
    for dst in range(n_src):
        out_ref[dst] = filled[:, dst * f_dev : (dst + 1) * f_dev]


def fill(pieces, high, low, flags, f_dev):
    n_src, _, rows, lanes = pieces.shape
    groups = lanes // (2 * FB)
    n_freq = high.shape[0]
    return pl.pallas_call(
        fill_kernel,
        in_specs=[pl.BlockSpec(memory_space=pltpu.VMEM)] * 4,
        out_specs=pl.BlockSpec(memory_space=pltpu.VMEM),
        out_shape=jax.ShapeDtypeStruct((n_src, groups * rows, f_dev), jnp.float32),
        scratch_shapes=[pltpu.VMEM((groups * rows, n_freq), jnp.float32)],
        compiler_params=params(8),
        cost_estimate=pl.CostEstimate(
            flops=2 * ITERS * 3 * groups * rows * n_freq * n_freq,
            bytes_accessed=4 * n_freq * n_freq,
            transcendentals=0,
        ),
        name="fill",
    )(pieces, high, low, flags)


def make_tables(m_modes, n_tm, t_dev):
    n_time = t_dev * n_tm
    times = lax.axis_index("tm") * t_dev + jnp.arange(t_dev * FB, dtype=jnp.int32) // FB
    index = m_modes[:, None] * times[None, :] % n_time
    angle = 2.0 * math.pi / n_time * index.astype(jnp.float32)
    return jnp.concatenate([jnp.cos(angle), jnp.sin(angle)], axis=0)


def exchange(send, bit, n_tm):
    return lax.ppermute(send, "tm", [(i, i ^ bit) for i in range(n_tm)])


def make_chunks(n_units):
    sizes = [2, 2] if n_units == 4 else [1] * n_units
    return [(sum(sizes[:i]), size) for i, size in enumerate(sizes)]


def per_device(vis, beam, fg_cov, flags, m_modes):
    t_dev, f_dev, _ = vis.shape
    n_tm = lax.axis_size("tm")
    n_chan = lax.axis_size("chan")
    n_slots = m_modes.shape[0] // n_tm
    degrees = beam.shape[3]
    orders = bit_orders(n_tm)
    targets = [target_order(n_tm, bits) for bits in orders]
    n_units = f_dev // (2 * FB)
    chunks = make_chunks(n_units)
    n_chunks = len(chunks)
    n_steps = len(orders[0])
    high, low = split(fg_cov)

    parts = [None] * n_chunks
    sends = [None] * n_chunks

    def begin(chunk, tab):
        first, units = chunks[chunk]
        outs = transform(tab, vis, first * 2 * FB, units, targets, n_slots)
        parts[chunk] = [[outs[0]], [outs[2]]]
        sends[chunk] = [outs[1], outs[3]]

    def go_on(chunk, place):
        for h, bits in enumerate(orders):
            got = exchange(sends[chunk][h], bits[place], n_tm)
            parts[chunk][h].append(got)
            size = got.shape[0] // 2
            sends[chunk][h] = sum(term[size : 2 * size] for term in parts[chunk][h])

    tab = make_tables(m_modes, n_tm, t_dev)
    for chunk in range(n_chunks):
        begin(chunk, tab)
    first, units = chunks[-1]
    sends[-1][0], source = lax.optimization_barrier((sends[-1][0], beam))
    block = load(source, first * 2 * FB, units * 2 * FB)
    keeps = [group[0] for group in parts[0]]
    *keeps, block = lax.optimization_barrier((*keeps, block))
    parts[0] = [[keep] for keep in keeps]
    for place in range(n_steps):
        for chunk in range(n_chunks):
            go_on(chunk, place)

    coeffs = None
    for chunk, (first, units) in enumerate(chunks):
        last = chunk == n_chunks - 1
        coeffs = project(
            parts[chunk], block if last else beam, first * 2 * FB, units, last, n_chan, n_units, coeffs
        )
    pieces = lax.all_to_all(coeffs, "chan", split_axis=0, concat_axis=0, tiled=True)
    whole = fill(pieces, high, low, flags[None, :], f_dev)
    back = lax.all_to_all(whole, "chan", split_axis=0, concat_axis=0, tiled=True)
    pairs = n_slots // 2
    back = back.reshape(pairs, n_chan // pairs, 2, 2, -1, f_dev)
    return back.transpose(0, 2, 3, 1, 4, 5).reshape(n_slots, 2, degrees, f_dev)


def solution(mesh):
    placed = (P("tm", "chan", None), P("tm", "chan", None, None, None), P(), P(), P())
    return jax.shard_map(
        per_device,
        mesh=mesh,
        in_specs=placed,
        out_specs=P("tm", None, None, "chan"),
        check_vma=False,
    )
```

```python
import math

import jax
import jax.numpy as jnp
from jax import lax
from jax.experimental import pallas as pl
from jax.experimental.pallas import tpu as pltpu
from jax.sharding import PartitionSpec as P

ITERS = 10
EPS = 1e-06
FB = 16


def params(mebibytes):
    return pltpu.CompilerParams(vmem_limit_bytes=mebibytes * 1024 * 1024)


def bit_orders(n_tm):
    bits = [1 << i for i in range(n_tm.bit_length() - 1)]
    return bits, bits[::-1]


def target_order(n_tm, bits):
    return sorted(range(n_tm), key=lambda r: [int(bool(r & b)) for b in bits])


def transform_kernel(orders, n_slots, start, units, tab_ref, vis_ref, *refs):
    outs, (held_ref, full_ref, sems) = refs[:-3], refs[-3:]
    _, n_dev_time, _, width = held_ref.shape
    n_tm = len(orders[0])
    n_time = n_dev_time * n_tm
    n_rows = n_tm * n_slots
    half = width // 2
    depth = n_dev_time * FB
    scale = 1.0 / math.sqrt(n_time)

    def copies(unit):
        size = n_dev_time // 2
        for piece in range(2):
            times = pl.ds(piece * size, size)
            source = vis_ref.at[times, pl.ds(start + unit * 2 * FB, 2 * FB), :]
            target = held_ref.at[unit, times]
            yield pltpu.make_async_copy(source, target, sems.at[unit, piece])

    for unit in range(units):
        for copy in copies(unit):
            copy.start()

    me = lax.axis_index("tm")
    sub = lax.broadcasted_iota(jnp.int32, (FB, depth), 0)
    same = lax.rem(lax.broadcasted_iota(jnp.int32, (FB, depth), 1), FB) == sub
    for r in range(n_tm):
        for j in range(n_slots):
            for which in range(2):
                mode = which * n_rows + (me ^ r) * n_slots + j
                wide = jnp.broadcast_to(tab_ref[pl.ds(mode, 1), :], (FB, depth))
                at = (which * n_rows + r * n_slots + j) * FB
                full_ref[at : at + FB, :] = jnp.where(same, wide, 0.0).astype(jnp.bfloat16)

    for group in range(2 * units):
        part, place_f = group // units, group % units * FB
        order, keep, send = orders[part], outs[2 * part], outs[2 * part + 1]
        n_keep = keep.shape[0]
        if group % 2 == 0:
            for copy in copies(group // 2):
                copy.wait()
        first = group % 2 * FB
        data = held_ref[group // 2, :, first : first + FB, :].reshape(depth, width)
        prod = jnp.dot(full_ref[...], data, preferred_element_type=jnp.float32)
        cos_part, sin_part = prod[: n_rows * FB], prod[n_rows * FB :]
        real = (cos_part[:, :half] + sin_part[:, half:]) * scale
        imag = (cos_part[:, half:] - sin_part[:, :half]) * scale
        for place, r in enumerate(order):
            out = keep if place < n_keep else send
            for j in range(n_slots):
                at = (r * n_slots + j) * FB
                out[place % n_keep, j, place_f : place_f + FB, :half] = real[at : at + FB]
                out[place % n_keep, j, place_f : place_f + FB, half:] = imag[at : at + FB]


def transform(tab, vis, start, units, orders, n_slots):
    n_time, _, width = vis.shape
    n_tm = len(orders[0])
    depth = n_time * FB
    n_rows = n_tm * n_slots
    piece = jax.ShapeDtypeStruct((n_tm // 2, n_slots, units * FB, width), jnp.float32)

    def body(*refs):
        transform_kernel(orders, n_slots, start, units, *refs)

    return pl.pallas_call(
        body,
        in_specs=[
            pl.BlockSpec(memory_space=pltpu.VMEM),
            pl.BlockSpec(memory_space=pltpu.HBM),
        ],
        out_specs=[pl.BlockSpec(memory_space=pltpu.VMEM)] * 4,
        out_shape=[piece] * 4,
        scratch_shapes=[
            pltpu.VMEM((units, n_time, 2 * FB, width), jnp.bfloat16),
            pltpu.VMEM((2 * n_rows * FB, depth), jnp.bfloat16),
            pltpu.SemaphoreType.DMA((units, 2)),
        ],
        compiler_params=params(50),
        cost_estimate=pl.CostEstimate(
            flops=2 * 2 * n_rows * FB * depth * width * 2 * units,
            bytes_accessed=n_time * 2 * FB * units * width * 2 + 4 * 4 * piece.size,
            transcendentals=0,
        ),
        name="transform",
    )(tab, vis)


def position():
    me = lax.axis_index("chan")
    return lax.div(me, 2), lax.rem(me, 2)


def put(dst, keep_ref, send_ref, at, value):
    z, core = position()

    @pl.when(core == dst % 2)
    def _():
        keep_ref[(dst // 2) ^ z, *at] = value

    @pl.when(core != dst % 2)
    def _():
        send_ref[(dst // 2) ^ z, *at] = value


def exchange_chan(keep, send, n_chan):
    def swap(value, bits):
        return lax.ppermute(value, "chan", [(i, i ^ bits) for i in range(n_chan)])

    got = swap(send, 1)
    pairs = [(k, jnp.stack([keep[k], got[k]])) for k in reversed(range(1, n_chan // 2))]
    far = {k: swap(pair, 2 * k) for k, pair in pairs}
    return [keep, got, *(far[k] for k in range(1, n_chan // 2))]


def arrivals(refs):
    z, core = position()
    keep, got, far = refs[0], refs[1], refs[2:]
    yield 2 * z + core, lambda *at: keep[0, *at]
    yield 2 * z + 1 - core, lambda *at: got[0, *at]
    for k, ref in enumerate(far, 1):
        yield 2 * (z ^ k) + core, lambda *at, ref=ref: ref[0, *at]
        yield 2 * (z ^ k) + 1 - core, lambda *at, ref=ref: ref[1, *at]


def project_kernel(n_terms, units, *refs):
    terms = refs[: 2 * n_terms]
    beam_ref, keep_ref, send_ref, vis_ref, flat_ref = refs[2 * n_terms], *refs[-4:]
    n_slots, _, _, degrees, half = beam_ref.shape
    pairs = n_slots // 2
    pieces = [(u, i, s, h) for u in range(units) for i in range(pairs) for s in range(2) for h in range(2)]

    for at, (u, i, s, h) in enumerate(pieces):
        part, place = (2 * u + h) // units, (2 * u + h) % units * FB
        total = None
        for term in terms[part * n_terms : (part + 1) * n_terms]:
            value = term[0, 2 * i + s, place : place + FB, :]
            total = value if total is None else total + value
        real = total[:, :half].astype(jnp.bfloat16)
        imag = total[:, half:].astype(jnp.bfloat16)
        vis_ref[at, :FB, :half] = real
        vis_ref[at, FB:, :half] = imag
        vis_ref[at, :FB, half:] = -imag
        vis_ref[at, FB:, half:] = real

    dims = (((1,), (1,)), ((), ()))
    per_pair = 2 * keep_ref.shape[0] // pairs
    rows = keep_ref.shape[2]
    per_tile = 128 // degrees
    sub = lax.broadcasted_iota(jnp.int32, (8, 128), 0)
    for at, (u, i, s, h) in enumerate(pieces):
        block = beam_ref.at[2 * i + s, pl.ds((2 * u + h) * FB, FB)]
        real = block[:, 0].reshape(FB * degrees, half)
        imag = block[:, 1].reshape(FB * degrees, half)
        both = jnp.concatenate([real, imag], axis=1)
        prod = lax.dot_general(vis_ref[at], both, dims, preferred_element_type=jnp.float32)
        for p in range(2):
            for g in range(FB // 8):
                own = prod[p * FB + g * 8 : p * FB + g * 8 + 8, g * 8 * degrees : (g + 1) * 8 * degrees]
                pick = own[:, :128]
                for v in range(1, 8 // per_tile):
                    pick = jnp.where(sub // per_tile == v, own[:, v * 128 : (v + 1) * 128], pick)
                if per_tile == 2:
                    pick = jnp.where(sub % 2 == 0, pick, pltpu.roll(pick, degrees, 1))
                row = s * 4 * FB + p * 2 * FB + h * FB + g * 8
                flat_ref[row : row + 8, :] = pick
        if s == 1 and h == 1:
            turned = flat_ref[...].T[:degrees]
            for b in range(per_pair):
                put(i * per_pair + b, keep_ref, send_ref, (u,), turned[b * rows : (b + 1) * rows])


def load(beam, start, size):
    n_slots = beam.shape[0]
    pieces = [(j, f) for j in range(n_slots) for f in range(0, size, FB)]
    block = jax.ShapeDtypeStruct((n_slots, size, *beam.shape[2:]), beam.dtype)

    def body(beam_ref, out_ref, sems):
        copies = [
            pltpu.make_async_copy(
                beam_ref.at[j, pl.ds(start + f, FB)], out_ref.at[j, pl.ds(f, FB)], sems.at[at]
            )
            for at, (j, f) in enumerate(pieces)
        ]
        for copy in copies:
            copy.start()
        for copy in copies:
            copy.wait()

    return pl.pallas_call(
        body,
        in_specs=[pl.BlockSpec(memory_space=pltpu.HBM)],
        out_specs=pl.BlockSpec(memory_space=pltpu.VMEM),
        out_shape=block,
        scratch_shapes=[pltpu.SemaphoreType.DMA((len(pieces),))],
        compiler_params=params(14),
        cost_estimate=pl.CostEstimate(
            flops=0, bytes_accessed=4 * block.size, transcendentals=0
        ),
        name="load",
    )(beam)


def project(parts, beam, start, units, n_chan, n_units, buffers):
    n_slots, _, _, degrees, half = beam.shape
    n_terms = len(parts[0])
    pairs = n_slots // 2
    rows = pairs * degrees // n_chan
    terms = [term for group in parts for term in group]
    place = start // (2 * FB) // units
    n_pieces = units * n_slots * 2

    def body(*refs):
        project_kernel(n_terms, units, *refs)

    term_spec = pl.BlockSpec((1, n_slots, units * FB, 2 * half), lambda i: (0, 0, 0, 0))
    return pl.pallas_call(
        body,
        grid=(1,),
        in_specs=[term_spec] * len(terms)
        + [pl.BlockSpec(memory_space=pltpu.VMEM)]
        + [pl.BlockSpec(memory_space=pl.ANY)] * len(buffers),
        out_specs=[pl.BlockSpec((n_chan // 2, units, rows, 8 * FB), lambda i: (0, place, 0, 0))] * 2,
        out_shape=[jax.ShapeDtypeStruct((n_chan // 2, n_units, rows, 8 * FB), jnp.float32)] * 2,
        scratch_shapes=[
            pltpu.VMEM((n_pieces, 2 * FB, 2 * half), jnp.bfloat16),
            pltpu.VMEM((8 * FB, 128), jnp.float32),
        ],
        input_output_aliases={len(terms) + 1 + i: i for i in range(len(buffers))},
        compiler_params=params(14),
        cost_estimate=pl.CostEstimate(
            flops=2 * n_slots * 2 * FB * units * 2 * degrees * half * 256,
            bytes_accessed=n_slots * 2 * FB * units * 2 * degrees * half * 2,
            transcendentals=0,
        ),
        name="project",
    )(*terms, beam, *buffers)


def split_kernel(cov_ref, high_ref, low_ref):
    cov = cov_ref[...]
    high = cov.astype(jnp.bfloat16)
    high_ref[...] = high
    low_ref[...] = (cov - high.astype(jnp.float32)).astype(jnp.bfloat16)


def split(cov, n_blocks=4):
    rows, cols = cov.shape
    spec = pl.BlockSpec((rows // n_blocks, cols), lambda i: (i, 0))
    half = jax.ShapeDtypeStruct(cov.shape, jnp.bfloat16)
    return pl.pallas_call(
        split_kernel,
        grid=(n_blocks,),
        in_specs=[spec],
        out_specs=[spec, spec],
        out_shape=[half, half],
        compiler_params=params(14),
        cost_estimate=pl.CostEstimate(
            flops=4 * cov.size, bytes_accessed=8 * cov.size, transcendentals=0
        ),
        name="split",
    )(cov)


def fill_kernel(n_in, *refs):
    high_ref, low_ref, flags_ref, keep_ref, send_ref, data_ref = refs[n_in:]
    n_src, n_rows, f_dev = data_ref.shape
    _, n_units, rows, lanes = refs[0].shape
    groups = lanes // (2 * FB)
    for src, take in arrivals(refs[:n_in]):
        for u in range(n_units):
            piece = take(u)
            for g in range(groups):
                data_ref[src, g * rows : (g + 1) * rows, u * 2 * FB : (u + 1) * 2 * FB] = piece[
                    :, g * 2 * FB : (g + 1) * 2 * FB
                ]
    data = jnp.concatenate([data_ref[src] for src in range(n_src)], axis=1)
    good = 1.0 - flags_ref[...].astype(jnp.float32)

    def total(values):
        return jnp.sum(values, axis=1, keepdims=True)

    def covered(vec):
        top = vec.astype(jnp.bfloat16)
        rest = (vec - top.astype(jnp.float32)).astype(jnp.bfloat16)
        both = jnp.concatenate([top, rest], axis=0)
        wide = jnp.dot(both, high_ref[...], preferred_element_type=jnp.float32)
        thin = jnp.dot(top, low_ref[...], preferred_element_type=jnp.float32)
        return wide[:n_rows] + (wide[n_rows:] + thin)

    resid = good * data
    direc = resid
    norm_now = total(resid * resid)
    signal = jnp.zeros_like(resid)

    def advance(step, carry):
        signal, resid, direc, norm_now = carry
        image = covered(direc)
        shifted = direc + good * image
        alpha = norm_now / (total(direc * shifted) + EPS)
        signal = signal + alpha * image
        resid = resid - alpha * shifted
        norm_next = total(resid * resid)
        direc = resid + norm_next / (norm_now + EPS) * direc
        return signal, resid, direc, norm_next

    signal, resid, direc, norm_now = lax.fori_loop(
        0, ITERS, advance, (signal, resid, direc, norm_now)
    )
    data = jnp.concatenate([data_ref[src] for src in range(n_src)], axis=1)
    filled = good * data + (1.0 - good) * signal
    for dst in range(n_src):
        put(dst, keep_ref, send_ref, (), filled[:, dst * f_dev : (dst + 1) * f_dev])


def fill(pieces, high, low, flags, f_dev):
    n_hi, _, rows, lanes = pieces[0].shape
    n_rows = lanes // (2 * FB) * rows
    n_freq = high.shape[0]

    def body(*refs):
        fill_kernel(len(pieces), *refs)

    return pl.pallas_call(
        body,
        in_specs=[pl.BlockSpec(memory_space=pltpu.VMEM)] * (len(pieces) + 3),
        out_specs=[pl.BlockSpec(memory_space=pltpu.VMEM)] * 2,
        out_shape=[jax.ShapeDtypeStruct((n_hi, n_rows, f_dev), jnp.float32)] * 2,
        scratch_shapes=[pltpu.VMEM((2 * n_hi, n_rows, f_dev), jnp.float32)],
        compiler_params=params(14),
        cost_estimate=pl.CostEstimate(
            flops=2 * ITERS * 3 * n_rows * n_freq * n_freq,
            bytes_accessed=4 * n_freq * n_freq,
            transcendentals=0,
        ),
        name="fill",
    )(*pieces, high, low, flags)


def gather_kernel(n_in, *refs):
    out_ref, stage_ref = refs[n_in:]
    n_src, n_rows, _ = stage_ref.shape
    for src, take in arrivals(refs[:n_in]):
        stage_ref[src] = take()
    pairs = out_ref.shape[0] // 2
    per_pair = n_src // pairs
    rows = n_rows // 4
    for src in range(n_src):
        i, block = src // per_pair, src % per_pair
        for g in range(4):
            out_ref[2 * i + g // 2, g % 2, block * rows : (block + 1) * rows, :] = stage_ref[
                src, g * rows : (g + 1) * rows, :
            ]


def gather(pieces, shape):
    def body(*refs):
        gather_kernel(len(pieces), *refs)

    n_hi, n_rows, f_dev = pieces[0].shape
    return pl.pallas_call(
        body,
        in_specs=[pl.BlockSpec(memory_space=pltpu.VMEM)] * len(pieces),
        out_specs=pl.BlockSpec(memory_space=pltpu.VMEM),
        out_shape=jax.ShapeDtypeStruct(shape, jnp.float32),
        scratch_shapes=[pltpu.VMEM((2 * n_hi, n_rows, f_dev), jnp.float32)],
        compiler_params=params(14),
        name="gather",
    )(*pieces)


def make_tables(m_modes, n_tm, t_dev):
    n_time = t_dev * n_tm
    times = lax.axis_index("tm") * t_dev + jnp.arange(t_dev * FB, dtype=jnp.int32) // FB
    index = m_modes[:, None] * times[None, :] % n_time
    angle = 2.0 * math.pi / n_time * index.astype(jnp.float32)
    return jnp.concatenate([jnp.cos(angle), jnp.sin(angle)], axis=0)


def exchange(send, bit, n_tm):
    return lax.ppermute(send, "tm", [(i, i ^ bit) for i in range(n_tm)])


def make_chunks(n_units):
    sizes = [2, 2] if n_units == 4 else [1] * n_units
    return [(sum(sizes[:i]), size) for i, size in enumerate(sizes)]


def per_device(vis, beam, fg_cov, flags, m_modes):
    t_dev, f_dev, _ = vis.shape
    n_tm = lax.axis_size("tm")
    n_chan = lax.axis_size("chan")
    n_slots = m_modes.shape[0] // n_tm
    degrees = beam.shape[3]
    orders = bit_orders(n_tm)
    targets = [target_order(n_tm, bits) for bits in orders]
    n_units = f_dev // (2 * FB)
    chunks = make_chunks(n_units)
    n_chunks = len(chunks)
    n_steps = len(orders[0])
    high, low = split(fg_cov)

    parts = [None] * n_chunks
    sends = [None] * n_chunks

    def begin(chunk, tab):
        first, units = chunks[chunk]
        outs = transform(tab, vis, first * 2 * FB, units, targets, n_slots)
        parts[chunk] = [[outs[0]], [outs[2]]]
        sends[chunk] = [outs[1], outs[3]]

    def go_on(chunk, place):
        for h, bits in enumerate(orders):
            got = exchange(sends[chunk][h], bits[place], n_tm)
            parts[chunk][h].append(got)
            size = got.shape[0] // 2
            sends[chunk][h] = sum(term[size : 2 * size] for term in parts[chunk][h])

    tab = make_tables(m_modes, n_tm, t_dev)
    for chunk in range(n_chunks):
        begin(chunk, tab)
    blocks = []
    for chunk, (first, units) in enumerate(chunks):
        before = max(chunk - 1, 0)
        source = sends[-1][0] if chunk == 0 else sends[before][0]
        source, beam = lax.optimization_barrier((source, beam))
        if chunk == 0:
            sends[-1][0] = source
        else:
            sends[before][0] = source
        block = load(beam, first * 2 * FB, units * 2 * FB)
        keeps = [group[0] for group in parts[chunk]]
        *keeps, block = lax.optimization_barrier((*keeps, block))
        parts[chunk] = [[keep] for keep in keeps]
        blocks.append(block)
        go_on(chunk, 0)
    sends[-1][0], high, low = lax.optimization_barrier((sends[-1][0], high, low))
    for place in range(1, n_steps):
        for chunk in range(n_chunks):
            go_on(chunk, place)

    coeffs = []
    for chunk, (first, units) in enumerate(chunks):
        coeffs = project(
            parts[chunk], blocks[chunk], first * 2 * FB, units, n_chan, n_units, coeffs
        )
    pieces = exchange_chan(*coeffs, n_chan)
    whole = fill(pieces, high, low, flags[None, :], f_dev)
    back = exchange_chan(*whole, n_chan)
    return gather(back, (n_slots, 2, degrees, f_dev))


def solution(mesh):
    placed = (P("tm", "chan", None), P("tm", "chan", None, None, None), P(), P(), P())
    return jax.shard_map(
        per_device,
        mesh=mesh,
        in_specs=placed,
        out_specs=P("tm", None, None, "chan"),
        check_vma=False,
    )
```

```python
import math

import jax
import jax.numpy as jnp
from jax import lax
from jax.experimental import pallas as pl
from jax.experimental.pallas import tpu as pltpu
from jax.sharding import PartitionSpec as P

ITERS = 10
EPS = 1e-06
FB = 16


def params(mebibytes):
    return pltpu.CompilerParams(vmem_limit_bytes=mebibytes * 1024 * 1024)


def bit_orders(n_tm):
    bits = [1 << i for i in range(n_tm.bit_length() - 1)]
    return bits, bits[::-1]


def target_order(n_tm, bits):
    return sorted(range(n_tm), key=lambda r: [int(bool(r & b)) for b in bits])


def transform_kernel(orders, n_slots, start, units, tab_ref, vis_ref, *refs):
    outs, (held_ref, wide_ref, full_ref, sems) = refs[:-4], refs[-4:]
    _, n_dev_time, _, width = held_ref.shape
    n_tm = len(orders[0])
    n_time = n_dev_time * n_tm
    n_rows = n_tm * n_slots
    half = width // 2
    depth = n_dev_time * FB
    scale = 1.0 / math.sqrt(n_time)

    def copies(unit):
        size = n_dev_time // 2
        for piece in range(2):
            times = pl.ds(piece * size, size)
            source = vis_ref.at[times, pl.ds(start + unit * 2 * FB, 2 * FB), :]
            target = held_ref.at[unit, times]
            yield pltpu.make_async_copy(source, target, sems.at[unit, piece])

    for unit in range(units):
        for copy in copies(unit):
            copy.start()

    times = lax.broadcasted_iota(jnp.int32, (n_dev_time, depth), 0)
    lanes = lax.broadcasted_iota(jnp.int32, (n_dev_time, depth), 1)
    spread = jnp.where(lax.div(lanes, FB) == times, 1.0, 0.0).astype(jnp.bfloat16)
    wide_ref[...] = jnp.dot(tab_ref[...], spread, preferred_element_type=jnp.float32)
    me = lax.axis_index("tm")
    sub = lax.broadcasted_iota(jnp.int32, (FB, depth), 0)
    same = lax.rem(lax.broadcasted_iota(jnp.int32, (FB, depth), 1), FB) == sub
    for r in range(n_tm):
        for j in range(n_slots):
            for which in range(2):
                mode = which * n_rows + (me ^ r) * n_slots + j
                wide = jnp.broadcast_to(wide_ref[pl.ds(mode, 1), :], (FB, depth))
                at = (which * n_rows + r * n_slots + j) * FB
                full_ref[at : at + FB, :] = jnp.where(same, wide, 0.0).astype(jnp.bfloat16)

    for group in range(2 * units):
        part, place_f = group // units, group % units * FB
        order, keep, send = orders[part], outs[2 * part], outs[2 * part + 1]
        n_keep = keep.shape[0]
        if group % 2 == 0:
            for copy in copies(group // 2):
                copy.wait()
        first = group % 2 * FB
        data = held_ref[group // 2, :, first : first + FB, :].reshape(depth, width)
        prod = jnp.dot(full_ref[...], data, preferred_element_type=jnp.float32)
        cos_part, sin_part = prod[: n_rows * FB], prod[n_rows * FB :]
        real = (cos_part[:, :half] + sin_part[:, half:]) * scale
        imag = (cos_part[:, half:] - sin_part[:, :half]) * scale
        for place, r in enumerate(order):
            out = keep if place < n_keep else send
            for j in range(n_slots):
                at = (r * n_slots + j) * FB
                out[place % n_keep, j, place_f : place_f + FB, :half] = real[at : at + FB]
                out[place % n_keep, j, place_f : place_f + FB, half:] = imag[at : at + FB]


def transform(tab, vis, start, units, orders, n_slots):
    n_time, _, width = vis.shape
    n_tm = len(orders[0])
    depth = n_time * FB
    n_rows = n_tm * n_slots
    piece = jax.ShapeDtypeStruct((n_tm // 2, n_slots, units * FB, width), jnp.float32)

    def body(*refs):
        transform_kernel(orders, n_slots, start, units, *refs)

    return pl.pallas_call(
        body,
        in_specs=[
            pl.BlockSpec(memory_space=pltpu.VMEM),
            pl.BlockSpec(memory_space=pltpu.HBM),
        ],
        out_specs=[pl.BlockSpec(memory_space=pltpu.VMEM)] * 4,
        out_shape=[piece] * 4,
        scratch_shapes=[
            pltpu.VMEM((units, n_time, 2 * FB, width), jnp.bfloat16),
            pltpu.VMEM((2 * n_rows, depth), jnp.float32),
            pltpu.VMEM((2 * n_rows * FB, depth), jnp.bfloat16),
            pltpu.SemaphoreType.DMA((units, 2)),
        ],
        compiler_params=params(50),
        cost_estimate=pl.CostEstimate(
            flops=2 * 2 * n_rows * FB * depth * width * 2 * units,
            bytes_accessed=n_time * 2 * FB * units * width * 2 + 4 * 4 * piece.size,
            transcendentals=0,
        ),
        name="transform",
    )(tab, vis)


def position():
    me = lax.axis_index("chan")
    return lax.div(me, 2), lax.rem(me, 2)


def put(dst, keep_ref, send_ref, at, value):
    z, core = position()

    @pl.when(core == dst % 2)
    def _():
        keep_ref[(dst // 2) ^ z, *at] = value

    @pl.when(core != dst % 2)
    def _():
        send_ref[(dst // 2) ^ z, *at] = value


def exchange_chan(keep, send, n_chan):
    def swap(value, bits):
        return lax.ppermute(value, "chan", [(i, i ^ bits) for i in range(n_chan)])

    got = swap(send, 1)
    pairs = [(k, jnp.stack([keep[k], got[k]])) for k in reversed(range(1, n_chan // 2))]
    far = {k: swap(pair, 2 * k) for k, pair in pairs}
    return [keep, got, *(far[k] for k in range(1, n_chan // 2))]


def arrivals(refs):
    z, core = position()
    keep, got, far = refs[0], refs[1], refs[2:]
    yield 2 * z + core, lambda *at: keep[0, *at]
    yield 2 * z + 1 - core, lambda *at: got[0, *at]
    for k, ref in enumerate(far, 1):
        yield 2 * (z ^ k) + core, lambda *at, ref=ref: ref[0, *at]
        yield 2 * (z ^ k) + 1 - core, lambda *at, ref=ref: ref[1, *at]


def project_kernel(n_terms, units, *refs):
    terms = refs[: 2 * n_terms]
    beam_ref, keep_ref, send_ref, vis_ref, flat_ref = refs[2 * n_terms], *refs[-4:]
    n_slots, _, _, degrees, half = beam_ref.shape
    pairs = n_slots // 2
    pieces = [(u, i, s, h) for u in range(units) for i in range(pairs) for s in range(2) for h in range(2)]

    for at, (u, i, s, h) in enumerate(pieces):
        part, place = (2 * u + h) // units, (2 * u + h) % units * FB
        total = None
        for term in terms[part * n_terms : (part + 1) * n_terms]:
            value = term[0, 2 * i + s, place : place + FB, :]
            total = value if total is None else total + value
        real = total[:, :half].astype(jnp.bfloat16)
        imag = total[:, half:].astype(jnp.bfloat16)
        vis_ref[at, :FB, :half] = real
        vis_ref[at, FB:, :half] = imag
        vis_ref[at, :FB, half:] = -imag
        vis_ref[at, FB:, half:] = real

    dims = (((1,), (1,)), ((), ()))
    per_pair = 2 * keep_ref.shape[0] // pairs
    rows = keep_ref.shape[2]
    per_tile = 128 // degrees
    sub = lax.broadcasted_iota(jnp.int32, (8, 128), 0)
    for at, (u, i, s, h) in enumerate(pieces):
        block = beam_ref.at[2 * i + s, pl.ds((2 * u + h) * FB, FB)]
        real = block[:, 0].reshape(FB * degrees, half)
        imag = block[:, 1].reshape(FB * degrees, half)
        both = jnp.concatenate([real, imag], axis=1)
        prod = lax.dot_general(vis_ref[at], both, dims, preferred_element_type=jnp.float32)
        for p in range(2):
            for g in range(FB // 8):
                own = prod[p * FB + g * 8 : p * FB + g * 8 + 8, g * 8 * degrees : (g + 1) * 8 * degrees]
                pick = own[:, :128]
                for v in range(1, 8 // per_tile):
                    pick = jnp.where(sub // per_tile == v, own[:, v * 128 : (v + 1) * 128], pick)
                if per_tile == 2:
                    pick = jnp.where(sub % 2 == 0, pick, pltpu.roll(pick, degrees, 1))
                row = s * 4 * FB + p * 2 * FB + h * FB + g * 8
                flat_ref[row : row + 8, :] = pick
        if s == 1 and h == 1:
            turned = flat_ref[...].T[:degrees]
            for b in range(per_pair):
                put(i * per_pair + b, keep_ref, send_ref, (u,), turned[b * rows : (b + 1) * rows])


def load(beam, start, size):
    n_slots = beam.shape[0]
    pieces = [(j, f) for j in range(n_slots) for f in range(0, size, FB)]
    block = jax.ShapeDtypeStruct((n_slots, size, *beam.shape[2:]), beam.dtype)

    def body(beam_ref, out_ref, sems):
        copies = [
            pltpu.make_async_copy(
                beam_ref.at[j, pl.ds(start + f, FB)], out_ref.at[j, pl.ds(f, FB)], sems.at[at]
            )
            for at, (j, f) in enumerate(pieces)
        ]
        for copy in copies:
            copy.start()
        for copy in copies:
            copy.wait()

    return pl.pallas_call(
        body,
        in_specs=[pl.BlockSpec(memory_space=pltpu.HBM)],
        out_specs=pl.BlockSpec(memory_space=pltpu.VMEM),
        out_shape=block,
        scratch_shapes=[pltpu.SemaphoreType.DMA((len(pieces),))],
        compiler_params=params(14),
        cost_estimate=pl.CostEstimate(
            flops=0, bytes_accessed=4 * block.size, transcendentals=0
        ),
        name="load",
    )(beam)


def project(parts, beam, start, units, n_chan, n_units, buffers):
    n_slots, _, _, degrees, half = beam.shape
    n_terms = len(parts[0])
    pairs = n_slots // 2
    rows = pairs * degrees // n_chan
    terms = [term for group in parts for term in group]
    place = start // (2 * FB) // units
    n_pieces = units * n_slots * 2

    def body(*refs):
        project_kernel(n_terms, units, *refs)

    term_spec = pl.BlockSpec((1, n_slots, units * FB, 2 * half), lambda i: (0, 0, 0, 0))
    return pl.pallas_call(
        body,
        grid=(1,),
        in_specs=[term_spec] * len(terms)
        + [pl.BlockSpec(memory_space=pltpu.VMEM)]
        + [pl.BlockSpec(memory_space=pl.ANY)] * len(buffers),
        out_specs=[pl.BlockSpec((n_chan // 2, units, rows, 8 * FB), lambda i: (0, place, 0, 0))] * 2,
        out_shape=[jax.ShapeDtypeStruct((n_chan // 2, n_units, rows, 8 * FB), jnp.float32)] * 2,
        scratch_shapes=[
            pltpu.VMEM((n_pieces, 2 * FB, 2 * half), jnp.bfloat16),
            pltpu.VMEM((8 * FB, 128), jnp.float32),
        ],
        input_output_aliases={len(terms) + 1 + i: i for i in range(len(buffers))},
        compiler_params=params(14),
        cost_estimate=pl.CostEstimate(
            flops=2 * n_slots * 2 * FB * units * 2 * degrees * half * 256,
            bytes_accessed=n_slots * 2 * FB * units * 2 * degrees * half * 2,
            transcendentals=0,
        ),
        name="project",
    )(*terms, beam, *buffers)


def split_kernel(cov_ref, high_ref, low_ref):
    cov = cov_ref[...]
    high = cov.astype(jnp.bfloat16)
    high_ref[...] = high
    low_ref[...] = (cov - high.astype(jnp.float32)).astype(jnp.bfloat16)


def split(cov, n_blocks=4):
    rows, cols = cov.shape
    spec = pl.BlockSpec((rows // n_blocks, cols), lambda i: (i, 0))
    half = jax.ShapeDtypeStruct(cov.shape, jnp.bfloat16)
    return pl.pallas_call(
        split_kernel,
        grid=(n_blocks,),
        in_specs=[spec],
        out_specs=[spec, spec],
        out_shape=[half, half],
        compiler_params=params(14),
        cost_estimate=pl.CostEstimate(
            flops=4 * cov.size, bytes_accessed=8 * cov.size, transcendentals=0
        ),
        name="split",
    )(cov)


def fill_kernel(n_in, *refs):
    high_ref, low_ref, flags_ref, keep_ref, send_ref, data_ref = refs[n_in:]
    n_src, n_rows, f_dev = data_ref.shape
    _, n_units, rows, lanes = refs[0].shape
    groups = lanes // (2 * FB)
    for src, take in arrivals(refs[:n_in]):
        for u in range(n_units):
            piece = take(u)
            for g in range(groups):
                data_ref[src, g * rows : (g + 1) * rows, u * 2 * FB : (u + 1) * 2 * FB] = piece[
                    :, g * 2 * FB : (g + 1) * 2 * FB
                ]
    data = jnp.concatenate([data_ref[src] for src in range(n_src)], axis=1)
    good = 1.0 - flags_ref[...].astype(jnp.float32)

    def total(values):
        return jnp.sum(values, axis=1, keepdims=True)

    def covered(vec):
        top = vec.astype(jnp.bfloat16)
        rest = (vec - top.astype(jnp.float32)).astype(jnp.bfloat16)
        both = jnp.concatenate([top, rest], axis=0)
        wide = jnp.dot(both, high_ref[...], preferred_element_type=jnp.float32)
        thin = jnp.dot(top, low_ref[...], preferred_element_type=jnp.float32)
        return wide[:n_rows] + (wide[n_rows:] + thin)

    resid = good * data
    direc = resid
    norm_now = total(resid * resid)
    signal = jnp.zeros_like(resid)

    def advance(step, carry):
        signal, resid, direc, norm_now = carry
        image = covered(direc)
        shifted = direc + good * image
        alpha = norm_now / (total(direc * shifted) + EPS)
        signal = signal + alpha * image
        resid = resid - alpha * shifted
        norm_next = total(resid * resid)
        direc = resid + norm_next / (norm_now + EPS) * direc
        return signal, resid, direc, norm_next

    signal, resid, direc, norm_now = lax.fori_loop(
        0, ITERS, advance, (signal, resid, direc, norm_now)
    )
    data = jnp.concatenate([data_ref[src] for src in range(n_src)], axis=1)
    filled = good * data + (1.0 - good) * signal
    for dst in range(n_src):
        put(dst, keep_ref, send_ref, (), filled[:, dst * f_dev : (dst + 1) * f_dev])


def fill(pieces, high, low, flags, f_dev):
    n_hi, _, rows, lanes = pieces[0].shape
    n_rows = lanes // (2 * FB) * rows
    n_freq = high.shape[0]

    def body(*refs):
        fill_kernel(len(pieces), *refs)

    return pl.pallas_call(
        body,
        in_specs=[pl.BlockSpec(memory_space=pltpu.VMEM)] * (len(pieces) + 3),
        out_specs=[pl.BlockSpec(memory_space=pltpu.VMEM)] * 2,
        out_shape=[jax.ShapeDtypeStruct((n_hi, n_rows, f_dev), jnp.float32)] * 2,
        scratch_shapes=[pltpu.VMEM((2 * n_hi, n_rows, f_dev), jnp.float32)],
        compiler_params=params(14),
        cost_estimate=pl.CostEstimate(
            flops=2 * ITERS * 3 * n_rows * n_freq * n_freq,
            bytes_accessed=4 * n_freq * n_freq,
            transcendentals=0,
        ),
        name="fill",
    )(*pieces, high, low, flags)


def gather_kernel(n_in, *refs):
    out_ref, stage_ref = refs[n_in:]
    n_src, n_rows, _ = stage_ref.shape
    for src, take in arrivals(refs[:n_in]):
        stage_ref[src] = take()
    pairs = out_ref.shape[0] // 2
    per_pair = n_src // pairs
    rows = n_rows // 4
    for src in range(n_src):
        i, block = src // per_pair, src % per_pair
        for g in range(4):
            out_ref[2 * i + g // 2, g % 2, block * rows : (block + 1) * rows, :] = stage_ref[
                src, g * rows : (g + 1) * rows, :
            ]


def gather(pieces, shape):
    def body(*refs):
        gather_kernel(len(pieces), *refs)

    n_hi, n_rows, f_dev = pieces[0].shape
    return pl.pallas_call(
        body,
        in_specs=[pl.BlockSpec(memory_space=pltpu.VMEM)] * len(pieces),
        out_specs=pl.BlockSpec(memory_space=pltpu.VMEM),
        out_shape=jax.ShapeDtypeStruct(shape, jnp.float32),
        scratch_shapes=[pltpu.VMEM((2 * n_hi, n_rows, f_dev), jnp.float32)],
        compiler_params=params(14),
        name="gather",
    )(*pieces)


def make_tables(m_modes, n_tm, t_dev):
    n_time = t_dev * n_tm
    times = lax.axis_index("tm") * t_dev + jnp.arange(t_dev, dtype=jnp.int32)
    index = m_modes[:, None] * times[None, :] % n_time
    angle = 2.0 * math.pi / n_time * index.astype(jnp.float32)
    return jnp.concatenate([jnp.cos(angle), jnp.sin(angle)], axis=0).astype(jnp.bfloat16)


def exchange(send, bit, n_tm):
    return lax.ppermute(send, "tm", [(i, i ^ bit) for i in range(n_tm)])


def make_chunks(n_units):
    sizes = [2, 2] if n_units == 4 else [1] * n_units
    return [(sum(sizes[:i]), size) for i, size in enumerate(sizes)]


def per_device(vis, beam, fg_cov, flags, m_modes):
    t_dev, f_dev, _ = vis.shape
    n_tm = lax.axis_size("tm")
    n_chan = lax.axis_size("chan")
    n_slots = m_modes.shape[0] // n_tm
    degrees = beam.shape[3]
    orders = bit_orders(n_tm)
    targets = [target_order(n_tm, bits) for bits in orders]
    n_units = f_dev // (2 * FB)
    chunks = make_chunks(n_units)
    n_chunks = len(chunks)
    n_steps = len(orders[0])
    high, low = split(fg_cov)

    parts = [None] * n_chunks
    sends = [None] * n_chunks

    def begin(chunk, tab):
        first, units = chunks[chunk]
        outs = transform(tab, vis, first * 2 * FB, units, targets, n_slots)
        parts[chunk] = [[outs[0]], [outs[2]]]
        sends[chunk] = [outs[1], outs[3]]

    def go_on(chunk, place):
        for h, bits in enumerate(orders):
            got = exchange(sends[chunk][h], bits[place], n_tm)
            parts[chunk][h].append(got)
            size = got.shape[0] // 2
            sends[chunk][h] = sum(term[size : 2 * size] for term in parts[chunk][h])

    tab = make_tables(m_modes, n_tm, t_dev)
    for chunk in range(n_chunks):
        begin(chunk, tab)
    blocks = []
    for chunk, (first, units) in enumerate(chunks):
        before = max(chunk - 1, 0)
        source = sends[-1][0] if chunk == 0 else sends[before][0]
        source, beam = lax.optimization_barrier((source, beam))
        if chunk == 0:
            sends[-1][0] = source
        else:
            sends[before][0] = source
        block = load(beam, first * 2 * FB, units * 2 * FB)
        keeps = [group[0] for group in parts[chunk]]
        *keeps, block = lax.optimization_barrier((*keeps, block))
        parts[chunk] = [[keep] for keep in keeps]
        blocks.append(block)
        go_on(chunk, 0)
    sends[-1][0], high, low = lax.optimization_barrier((sends[-1][0], high, low))
    for place in range(1, n_steps):
        for chunk in range(n_chunks):
            if chunk:
                got = [group.pop() for group in parts[chunk - 1]]
                *got, sends[chunk][0], sends[chunk][1] = lax.optimization_barrier(
                    (*got, *sends[chunk])
                )
                for group, value in zip(parts[chunk - 1], got):
                    group.append(value)
            go_on(chunk, place)

    coeffs = []
    for chunk, (first, units) in enumerate(chunks):
        coeffs = project(
            parts[chunk], blocks[chunk], first * 2 * FB, units, n_chan, n_units, coeffs
        )
    pieces = exchange_chan(*coeffs, n_chan)
    whole = fill(pieces, high, low, flags[None, :], f_dev)
    back = exchange_chan(*whole, n_chan)
    return gather(back, (n_slots, 2, degrees, f_dev))


def solution(mesh):
    placed = (P("tm", "chan", None), P("tm", "chan", None, None, None), P(), P(), P())
    return jax.shard_map(
        per_device,
        mesh=mesh,
        in_specs=placed,
        out_specs=P("tm", None, None, "chan"),
        check_vma=False,
    )
```

```python
import math

import jax
import jax.numpy as jnp
from jax import lax
from jax.experimental import pallas as pl
from jax.experimental.pallas import tpu as pltpu
from jax.sharding import PartitionSpec as P

ITERS = 10
EPS = 1e-06
FB = 16


def params(mebibytes):
    return pltpu.CompilerParams(vmem_limit_bytes=mebibytes * 1024 * 1024)


def bit_orders(n_tm):
    bits = [1 << i for i in range(n_tm.bit_length() - 1)]
    return bits, bits[::-1]


def target_order(n_tm, bits):
    return sorted(range(n_tm), key=lambda r: [int(bool(r & b)) for b in bits])


def transform_kernel(orders, n_slots, start, units, tab_ref, vis_ref, *refs):
    outs, (held_ref, wide_ref, full_ref, sems) = refs[:-4], refs[-4:]
    _, n_dev_time, _, width = held_ref.shape
    n_tm = len(orders[0])
    n_time = n_dev_time * n_tm
    n_rows = n_tm * n_slots
    half = width // 2
    depth = n_dev_time * FB
    scale = 1.0 / math.sqrt(n_time)

    def copies(unit):
        size = n_dev_time // 2
        for piece in range(2):
            times = pl.ds(piece * size, size)
            source = vis_ref.at[times, pl.ds(start + unit * 2 * FB, 2 * FB), :]
            target = held_ref.at[unit, times]
            yield pltpu.make_async_copy(source, target, sems.at[unit, piece])

    for unit in range(units):
        for copy in copies(unit):
            copy.start()

    times = lax.broadcasted_iota(jnp.int32, (n_dev_time, depth), 0)
    lanes = lax.broadcasted_iota(jnp.int32, (n_dev_time, depth), 1)
    spread = jnp.where(lax.div(lanes, FB) == times, 1.0, 0.0).astype(jnp.bfloat16)
    wide_ref[...] = jnp.dot(tab_ref[...], spread, preferred_element_type=jnp.float32)
    me = lax.axis_index("tm")
    sub = lax.broadcasted_iota(jnp.int32, (FB, depth), 0)
    same = lax.rem(lax.broadcasted_iota(jnp.int32, (FB, depth), 1), FB) == sub
    for r in range(n_tm):
        for j in range(n_slots):
            for which in range(2):
                mode = which * n_rows + (me ^ r) * n_slots + j
                wide = jnp.broadcast_to(wide_ref[pl.ds(mode, 1), :], (FB, depth))
                at = (which * n_rows + r * n_slots + j) * FB
                full_ref[at : at + FB, :] = jnp.where(same, wide, 0.0).astype(jnp.bfloat16)

    for group in range(2 * units):
        part, place_f = group // units, group % units * FB
        order, keep, send = orders[part], outs[2 * part], outs[2 * part + 1]
        n_keep = keep.shape[0]
        if group % 2 == 0:
            for copy in copies(group // 2):
                copy.wait()
        first = group % 2 * FB
        data = held_ref[group // 2, :, first : first + FB, :].reshape(depth, width)
        prod = jnp.dot(full_ref[...], data, preferred_element_type=jnp.float32)
        cos_part, sin_part = prod[: n_rows * FB], prod[n_rows * FB :]
        real = (cos_part[:, :half] + sin_part[:, half:]) * scale
        imag = (cos_part[:, half:] - sin_part[:, :half]) * scale
        for place, r in enumerate(order):
            out = keep if place < n_keep else send
            for j in range(n_slots):
                at = (r * n_slots + j) * FB
                out[place % n_keep, j, place_f : place_f + FB, :half] = real[at : at + FB]
                out[place % n_keep, j, place_f : place_f + FB, half:] = imag[at : at + FB]


def transform(tab, vis, start, units, orders, n_slots):
    n_time, _, width = vis.shape
    n_tm = len(orders[0])
    depth = n_time * FB
    n_rows = n_tm * n_slots
    piece = jax.ShapeDtypeStruct((n_tm // 2, n_slots, units * FB, width), jnp.float32)

    def body(*refs):
        transform_kernel(orders, n_slots, start, units, *refs)

    return pl.pallas_call(
        body,
        in_specs=[
            pl.BlockSpec(memory_space=pltpu.VMEM),
            pl.BlockSpec(memory_space=pltpu.HBM),
        ],
        out_specs=[pl.BlockSpec(memory_space=pltpu.VMEM)] * 4,
        out_shape=[piece] * 4,
        scratch_shapes=[
            pltpu.VMEM((units, n_time, 2 * FB, width), jnp.bfloat16),
            pltpu.VMEM((2 * n_rows, depth), jnp.float32),
            pltpu.VMEM((2 * n_rows * FB, depth), jnp.bfloat16),
            pltpu.SemaphoreType.DMA((units, 2)),
        ],
        compiler_params=params(50),
        cost_estimate=pl.CostEstimate(
            flops=2 * 2 * n_rows * FB * depth * width * 2 * units,
            bytes_accessed=n_time * 2 * FB * units * width * 2 + 4 * 4 * piece.size,
            transcendentals=0,
        ),
        name="transform",
    )(tab, vis)


def position():
    me = lax.axis_index("chan")
    return lax.div(me, 2), lax.rem(me, 2)


def put(dst, keep_ref, send_ref, at, value):
    z, core = position()

    @pl.when(core == dst % 2)
    def _():
        keep_ref[(dst // 2) ^ z, *at] = value

    @pl.when(core != dst % 2)
    def _():
        send_ref[(dst // 2) ^ z, *at] = value


def exchange_chan(keep, send, n_chan):
    def swap(value, bits):
        return lax.ppermute(value, "chan", [(i, i ^ bits) for i in range(n_chan)])

    got = swap(send, 1)
    pairs = [(k, jnp.stack([keep[k], got[k]])) for k in reversed(range(1, n_chan // 2))]
    far = {k: swap(pair, 2 * k) for k, pair in pairs}
    return [keep, got, *(far[k] for k in range(1, n_chan // 2))]


def arrivals(refs):
    z, core = position()
    keep, got, far = refs[0], refs[1], refs[2:]
    yield 2 * z + core, lambda *at: keep[0, *at]
    yield 2 * z + 1 - core, lambda *at: got[0, *at]
    for k, ref in enumerate(far, 1):
        yield 2 * (z ^ k) + core, lambda *at, ref=ref: ref[0, *at]
        yield 2 * (z ^ k) + 1 - core, lambda *at, ref=ref: ref[1, *at]


def project_kernel(n_terms, start, units, resident, *refs):
    terms = refs[: 2 * n_terms]
    beam_ref, keep_ref, send_ref, vis_ref, flat_ref = refs[2 * n_terms], *refs[-6:-2]
    held_ref, sems = refs[-2:]
    depth = held_ref.shape[0]
    n_slots, _, _, degrees, half = beam_ref.shape
    pairs = n_slots // 2
    pieces = [(u, i, s, h) for u in range(units) for i in range(pairs) for s in range(2) for h in range(2)]

    def copy(at):
        u, i, s, h = pieces[at]
        source = beam_ref.at[2 * i + s, pl.ds(start + (2 * u + h) * FB, FB)]
        return pltpu.make_async_copy(source, held_ref.at[at % depth], sems.at[at % depth])

    if not resident:
        for at in range(depth - 1):
            copy(at).start()

    for at, (u, i, s, h) in enumerate(pieces):
        part, place = (2 * u + h) // units, (2 * u + h) % units * FB
        total = None
        for term in terms[part * n_terms : (part + 1) * n_terms]:
            value = term[0, 2 * i + s, place : place + FB, :]
            total = value if total is None else total + value
        real = total[:, :half].astype(jnp.bfloat16)
        imag = total[:, half:].astype(jnp.bfloat16)
        vis_ref[at, :FB, :half] = real
        vis_ref[at, FB:, :half] = imag
        vis_ref[at, :FB, half:] = -imag
        vis_ref[at, FB:, half:] = real

    dims = (((1,), (1,)), ((), ()))
    per_pair = 2 * keep_ref.shape[0] // pairs
    rows = keep_ref.shape[2]
    per_tile = 128 // degrees
    sub = lax.broadcasted_iota(jnp.int32, (8, 128), 0)
    for at, (u, i, s, h) in enumerate(pieces):
        if resident:
            block = beam_ref.at[2 * i + s, pl.ds((2 * u + h) * FB, FB)]
        else:
            copy(at).wait()
            if at + depth - 1 < len(pieces):
                copy(at + depth - 1).start()
            block = held_ref.at[at % depth]
        real = block[:, 0].reshape(FB * degrees, half)
        imag = block[:, 1].reshape(FB * degrees, half)
        both = jnp.concatenate([real, imag], axis=1)
        prod = lax.dot_general(vis_ref[at], both, dims, preferred_element_type=jnp.float32)
        for p in range(2):
            for g in range(FB // 8):
                own = prod[p * FB + g * 8 : p * FB + g * 8 + 8, g * 8 * degrees : (g + 1) * 8 * degrees]
                pick = own[:, :128]
                for v in range(1, 8 // per_tile):
                    pick = jnp.where(sub // per_tile == v, own[:, v * 128 : (v + 1) * 128], pick)
                if per_tile == 2:
                    pick = jnp.where(sub % 2 == 0, pick, pltpu.roll(pick, degrees, 1))
                row = s * 4 * FB + p * 2 * FB + h * FB + g * 8
                flat_ref[row : row + 8, :] = pick
        if s == 1 and h == 1:
            turned = flat_ref[...].T[:degrees]
            for b in range(per_pair):
                put(i * per_pair + b, keep_ref, send_ref, (u,), turned[b * rows : (b + 1) * rows])


def load(beam, start, size):
    n_slots = beam.shape[0]
    pieces = [(j, f) for j in range(n_slots) for f in range(0, size, FB)]
    block = jax.ShapeDtypeStruct((n_slots, size, *beam.shape[2:]), beam.dtype)

    def body(beam_ref, out_ref, sems):
        copies = [
            pltpu.make_async_copy(
                beam_ref.at[j, pl.ds(start + f, FB)], out_ref.at[j, pl.ds(f, FB)], sems.at[at]
            )
            for at, (j, f) in enumerate(pieces)
        ]
        for copy in copies:
            copy.start()
        for copy in copies:
            copy.wait()

    return pl.pallas_call(
        body,
        in_specs=[pl.BlockSpec(memory_space=pltpu.HBM)],
        out_specs=pl.BlockSpec(memory_space=pltpu.VMEM),
        out_shape=block,
        scratch_shapes=[pltpu.SemaphoreType.DMA((len(pieces),))],
        compiler_params=params(14),
        cost_estimate=pl.CostEstimate(
            flops=0, bytes_accessed=4 * block.size, transcendentals=0
        ),
        name="load",
    )(beam)


def project(parts, beam, start, units, resident, n_chan, n_units, buffers, depth=5):
    n_slots, _, _, degrees, half = beam.shape
    n_terms = len(parts[0])
    pairs = n_slots // 2
    rows = pairs * degrees // n_chan
    terms = [term for group in parts for term in group]
    place = start // (2 * FB) // units
    depth = 1 if resident else min(depth, 2 * n_slots * units)
    n_pieces = units * n_slots * 2

    def body(*refs):
        project_kernel(n_terms, start, units, resident, *refs)

    term_spec = pl.BlockSpec((1, n_slots, units * FB, 2 * half), lambda i: (0, 0, 0, 0))
    return pl.pallas_call(
        body,
        grid=(1,),
        in_specs=[term_spec] * len(terms)
        + [pl.BlockSpec(memory_space=pltpu.VMEM if resident else pltpu.HBM)]
        + [pl.BlockSpec(memory_space=pl.ANY)] * len(buffers),
        out_specs=[pl.BlockSpec((n_chan // 2, units, rows, 8 * FB), lambda i: (0, place, 0, 0))] * 2,
        out_shape=[jax.ShapeDtypeStruct((n_chan // 2, n_units, rows, 8 * FB), jnp.float32)] * 2,
        scratch_shapes=[
            pltpu.VMEM((n_pieces, 2 * FB, 2 * half), jnp.bfloat16),
            pltpu.VMEM((8 * FB, 128), jnp.float32),
            pltpu.VMEM((depth, FB, 2, degrees, half), jnp.bfloat16),
            pltpu.SemaphoreType.DMA((depth,)),
        ],
        input_output_aliases={len(terms) + 1 + i: i for i in range(len(buffers))},
        compiler_params=params(14 if resident else 32),
        cost_estimate=pl.CostEstimate(
            flops=2 * n_slots * 2 * FB * units * 2 * degrees * half * 256,
            bytes_accessed=n_slots * 2 * FB * units * 2 * degrees * half * 2,
            transcendentals=0,
        ),
        name="project",
    )(*terms, beam, *buffers)


def split_kernel(cov_ref, high_ref, low_ref):
    cov = cov_ref[...]
    high = cov.astype(jnp.bfloat16)
    high_ref[...] = high
    low_ref[...] = (cov - high.astype(jnp.float32)).astype(jnp.bfloat16)


def split(cov, n_blocks=4):
    rows, cols = cov.shape
    spec = pl.BlockSpec((rows // n_blocks, cols), lambda i: (i, 0))
    half = jax.ShapeDtypeStruct(cov.shape, jnp.bfloat16)
    return pl.pallas_call(
        split_kernel,
        grid=(n_blocks,),
        in_specs=[spec],
        out_specs=[spec, spec],
        out_shape=[half, half],
        compiler_params=params(14),
        cost_estimate=pl.CostEstimate(
            flops=4 * cov.size, bytes_accessed=8 * cov.size, transcendentals=0
        ),
        name="split",
    )(cov)


def fill_kernel(n_in, *refs):
    high_ref, low_ref, flags_ref, keep_ref, send_ref, data_ref = refs[n_in:]
    n_src, n_rows, f_dev = data_ref.shape
    _, n_units, rows, lanes = refs[0].shape
    groups = lanes // (2 * FB)
    for src, take in arrivals(refs[:n_in]):
        for u in range(n_units):
            piece = take(u)
            for g in range(groups):
                data_ref[src, g * rows : (g + 1) * rows, u * 2 * FB : (u + 1) * 2 * FB] = piece[
                    :, g * 2 * FB : (g + 1) * 2 * FB
                ]
    data = jnp.concatenate([data_ref[src] for src in range(n_src)], axis=1)
    good = 1.0 - flags_ref[...].astype(jnp.float32)

    def total(values):
        return jnp.sum(values, axis=1, keepdims=True)

    def covered(vec):
        top = vec.astype(jnp.bfloat16)
        rest = (vec - top.astype(jnp.float32)).astype(jnp.bfloat16)
        both = jnp.concatenate([top, rest], axis=0)
        wide = jnp.dot(both, high_ref[...], preferred_element_type=jnp.float32)
        thin = jnp.dot(top, low_ref[...], preferred_element_type=jnp.float32)
        return wide[:n_rows] + (wide[n_rows:] + thin)

    resid = good * data
    direc = resid
    norm_now = total(resid * resid)
    signal = jnp.zeros_like(resid)

    def advance(step, carry):
        signal, resid, direc, norm_now = carry
        image = covered(direc)
        shifted = direc + good * image
        alpha = norm_now / (total(direc * shifted) + EPS)
        signal = signal + alpha * image
        resid = resid - alpha * shifted
        norm_next = total(resid * resid)
        direc = resid + norm_next / (norm_now + EPS) * direc
        return signal, resid, direc, norm_next

    signal, resid, direc, norm_now = lax.fori_loop(
        0, ITERS, advance, (signal, resid, direc, norm_now)
    )
    data = jnp.concatenate([data_ref[src] for src in range(n_src)], axis=1)
    filled = good * data + (1.0 - good) * signal
    for dst in range(n_src):
        put(dst, keep_ref, send_ref, (), filled[:, dst * f_dev : (dst + 1) * f_dev])


def fill(pieces, high, low, flags, f_dev):
    n_hi, _, rows, lanes = pieces[0].shape
    n_rows = lanes // (2 * FB) * rows
    n_freq = high.shape[0]

    def body(*refs):
        fill_kernel(len(pieces), *refs)

    return pl.pallas_call(
        body,
        in_specs=[pl.BlockSpec(memory_space=pltpu.VMEM)] * (len(pieces) + 3),
        out_specs=[pl.BlockSpec(memory_space=pltpu.VMEM)] * 2,
        out_shape=[jax.ShapeDtypeStruct((n_hi, n_rows, f_dev), jnp.float32)] * 2,
        scratch_shapes=[pltpu.VMEM((2 * n_hi, n_rows, f_dev), jnp.float32)],
        compiler_params=params(14),
        cost_estimate=pl.CostEstimate(
            flops=2 * ITERS * 3 * n_rows * n_freq * n_freq,
            bytes_accessed=4 * n_freq * n_freq,
            transcendentals=0,
        ),
        name="fill",
    )(*pieces, high, low, flags)


def gather_kernel(n_in, *refs):
    out_ref, stage_ref = refs[n_in:]
    n_src, n_rows, _ = stage_ref.shape
    for src, take in arrivals(refs[:n_in]):
        stage_ref[src] = take()
    pairs = out_ref.shape[0] // 2
    per_pair = n_src // pairs
    rows = n_rows // 4
    for src in range(n_src):
        i, block = src // per_pair, src % per_pair
        for g in range(4):
            out_ref[2 * i + g // 2, g % 2, block * rows : (block + 1) * rows, :] = stage_ref[
                src, g * rows : (g + 1) * rows, :
            ]


def gather(pieces, shape):
    def body(*refs):
        gather_kernel(len(pieces), *refs)

    n_hi, n_rows, f_dev = pieces[0].shape
    return pl.pallas_call(
        body,
        in_specs=[pl.BlockSpec(memory_space=pltpu.VMEM)] * len(pieces),
        out_specs=pl.BlockSpec(memory_space=pltpu.VMEM),
        out_shape=jax.ShapeDtypeStruct(shape, jnp.float32),
        scratch_shapes=[pltpu.VMEM((2 * n_hi, n_rows, f_dev), jnp.float32)],
        compiler_params=params(14),
        name="gather",
    )(*pieces)


def make_tables(m_modes, n_tm, t_dev):
    n_time = t_dev * n_tm
    times = lax.axis_index("tm") * t_dev + jnp.arange(t_dev, dtype=jnp.int32)
    index = m_modes[:, None] * times[None, :] % n_time
    angle = 2.0 * math.pi / n_time * index.astype(jnp.float32)
    return jnp.concatenate([jnp.cos(angle), jnp.sin(angle)], axis=0).astype(jnp.bfloat16)


def exchange(send, bit, n_tm):
    return lax.ppermute(send, "tm", [(i, i ^ bit) for i in range(n_tm)])


def make_chunks(n_units):
    sizes = [2, 1, 1] if n_units == 4 else [1] * n_units
    return [(sum(sizes[:i]), size) for i, size in enumerate(sizes)]


def per_device(vis, beam, fg_cov, flags, m_modes):
    t_dev, f_dev, _ = vis.shape
    n_tm = lax.axis_size("tm")
    n_chan = lax.axis_size("chan")
    n_slots = m_modes.shape[0] // n_tm
    degrees = beam.shape[3]
    orders = bit_orders(n_tm)
    targets = [target_order(n_tm, bits) for bits in orders]
    n_units = f_dev // (2 * FB)
    chunks = make_chunks(n_units)
    n_chunks = len(chunks)
    n_steps = len(orders[0])
    high, low = split(fg_cov)

    parts = [None] * n_chunks
    sends = [None] * n_chunks

    def begin(chunk, tab):
        first, units = chunks[chunk]
        outs = transform(tab, vis, first * 2 * FB, units, targets, n_slots)
        parts[chunk] = [[outs[0]], [outs[2]]]
        sends[chunk] = [outs[1], outs[3]]

    def go_on(chunk, place):
        for h, bits in enumerate(orders):
            got = exchange(sends[chunk][h], bits[place], n_tm)
            parts[chunk][h].append(got)
            size = got.shape[0] // 2
            sends[chunk][h] = sum(term[size : 2 * size] for term in parts[chunk][h])

    tab = make_tables(m_modes, n_tm, t_dev)
    for chunk in range(n_chunks):
        begin(chunk, tab)
    def after(first, then):
        both = lax.optimization_barrier((*first, *then))
        return list(both[: len(first)]), list(both[len(first) :])

    go_on(0, 0)
    if n_chunks > 1:
        ready, (beam,) = after([send[0] for send in sends[1:]], [beam])
        for send, value in zip(sends[1:], ready):
            send[0] = value
    first, units = chunks[-1]
    block = load(beam, first * 2 * FB, units * 2 * FB)
    (block, high, low), sends[-1] = after([block, high, low], sends[-1])
    if n_chunks > 2:
        ready, sends[1] = after([block, *sends[-1]], sends[1])
        block, sends[-1] = ready[0], ready[1:]
    for chunk in range(1, min(n_chunks, 2)):
        go_on(chunk, 0)
    for place in range(1, n_steps):
        go_on(0, place)
    for chunk in range(1, n_chunks):
        if chunk + 1 < n_chunks:
            group = parts[chunk - 1][0]
            (group[-1],), sends[chunk + 1] = after(group[-1:], sends[chunk + 1])
            go_on(chunk + 1, 0)
        for place in range(1, n_steps):
            go_on(chunk, place)

    coeffs = []
    for chunk, (first, units) in enumerate(chunks):
        last = chunk == n_chunks - 1
        coeffs = project(
            parts[chunk], block if last else beam, first * 2 * FB, units, last, n_chan, n_units, coeffs
        )
    pieces = exchange_chan(*coeffs, n_chan)
    whole = fill(pieces, high, low, flags[None, :], f_dev)
    back = exchange_chan(*whole, n_chan)
    return gather(back, (n_slots, 2, degrees, f_dev))


def solution(mesh):
    placed = (P("tm", "chan", None), P("tm", "chan", None, None, None), P(), P(), P())
    return jax.shard_map(
        per_device,
        mesh=mesh,
        in_specs=placed,
        out_specs=P("tm", None, None, "chan"),
        check_vma=False,
    )
```

```python
import math

import jax
import jax.numpy as jnp
from jax import lax
from jax.experimental import pallas as pl
from jax.experimental.pallas import tpu as pltpu
from jax.sharding import PartitionSpec as P

ITERS = 10
EPS = 1e-06
FB = 16


def params(mebibytes):
    return pltpu.CompilerParams(vmem_limit_bytes=mebibytes * 1024 * 1024)


def bit_orders(n_tm):
    bits = [1 << i for i in range(n_tm.bit_length() - 1)]
    return bits, bits[::-1]


def target_order(n_tm, bits):
    return sorted(range(n_tm), key=lambda r: [int(bool(r & b)) for b in bits])


def transform_kernel(orders, n_slots, start, units, tab_ref, vis_ref, *refs):
    outs, (held_ref, wide_ref, full_ref, sems) = refs[:-4], refs[-4:]
    _, n_dev_time, _, width = held_ref.shape
    n_tm = len(orders[0])
    n_time = n_dev_time * n_tm
    n_rows = n_tm * n_slots
    half = width // 2
    depth = n_dev_time * FB
    scale = 1.0 / math.sqrt(n_time)

    def copies(unit):
        size = n_dev_time // 2
        for piece in range(2):
            times = pl.ds(piece * size, size)
            source = vis_ref.at[times, pl.ds(start + unit * 2 * FB, 2 * FB), :]
            target = held_ref.at[unit, times]
            yield pltpu.make_async_copy(source, target, sems.at[unit, piece])

    for unit in range(units):
        for copy in copies(unit):
            copy.start()

    times = lax.broadcasted_iota(jnp.int32, (n_dev_time, depth), 0)
    lanes = lax.broadcasted_iota(jnp.int32, (n_dev_time, depth), 1)
    spread = jnp.where(lax.div(lanes, FB) == times, 1.0, 0.0).astype(jnp.bfloat16)
    wide_ref[...] = jnp.dot(tab_ref[...], spread, preferred_element_type=jnp.float32)
    me = lax.axis_index("tm")
    sub = lax.broadcasted_iota(jnp.int32, (FB, depth), 0)
    same = lax.rem(lax.broadcasted_iota(jnp.int32, (FB, depth), 1), FB) == sub
    for r in range(n_tm):
        for j in range(n_slots):
            for which in range(2):
                mode = which * n_rows + (me ^ r) * n_slots + j
                wide = jnp.broadcast_to(wide_ref[pl.ds(mode, 1), :], (FB, depth))
                at = (which * n_rows + r * n_slots + j) * FB
                full_ref[at : at + FB, :] = jnp.where(same, wide, 0.0).astype(jnp.bfloat16)

    for group in range(2 * units):
        part, place_f = group // units, group % units * FB
        order, keep, send = orders[part], outs[2 * part], outs[2 * part + 1]
        n_keep = keep.shape[0]
        if group % 2 == 0:
            for copy in copies(group // 2):
                copy.wait()
        first = group % 2 * FB
        data = held_ref[group // 2, :, first : first + FB, :].reshape(depth, width)
        prod = jnp.dot(full_ref[...], data, preferred_element_type=jnp.float32)
        cos_part, sin_part = prod[: n_rows * FB], prod[n_rows * FB :]
        real = (cos_part[:, :half] + sin_part[:, half:]) * scale
        imag = (cos_part[:, half:] - sin_part[:, :half]) * scale
        for place, r in enumerate(order):
            out = keep if place < n_keep else send
            for j in range(n_slots):
                at = (r * n_slots + j) * FB
                out[place % n_keep, j, place_f : place_f + FB, :half] = real[at : at + FB]
                out[place % n_keep, j, place_f : place_f + FB, half:] = imag[at : at + FB]


def transform(tab, vis, start, units, orders, n_slots):
    n_time, _, width = vis.shape
    n_tm = len(orders[0])
    depth = n_time * FB
    n_rows = n_tm * n_slots
    piece = jax.ShapeDtypeStruct((n_tm // 2, n_slots, units * FB, width), jnp.float32)

    def body(*refs):
        transform_kernel(orders, n_slots, start, units, *refs)

    return pl.pallas_call(
        body,
        in_specs=[
            pl.BlockSpec(memory_space=pltpu.VMEM),
            pl.BlockSpec(memory_space=pltpu.HBM),
        ],
        out_specs=[pl.BlockSpec(memory_space=pltpu.VMEM)] * 4,
        out_shape=[piece] * 4,
        scratch_shapes=[
            pltpu.VMEM((units, n_time, 2 * FB, width), jnp.bfloat16),
            pltpu.VMEM((2 * n_rows, depth), jnp.float32),
            pltpu.VMEM((2 * n_rows * FB, depth), jnp.bfloat16),
            pltpu.SemaphoreType.DMA((units, 2)),
        ],
        compiler_params=params(50),
        cost_estimate=pl.CostEstimate(
            flops=2 * 2 * n_rows * FB * depth * width * 2 * units,
            bytes_accessed=n_time * 2 * FB * units * width * 2 + 4 * 4 * piece.size,
            transcendentals=0,
        ),
        name="transform",
    )(tab, vis)


def position():
    me = lax.axis_index("chan")
    return lax.div(me, 2), lax.rem(me, 2)


def put(dst, keep_ref, send_ref, at, value):
    z, core = position()

    @pl.when(core == dst % 2)
    def _():
        keep_ref[(dst // 2) ^ z, *at] = value

    @pl.when(core != dst % 2)
    def _():
        send_ref[(dst // 2) ^ z, *at] = value


def exchange_chan(keep, send, n_chan):
    def swap(value, bits):
        return lax.ppermute(value, "chan", [(i, i ^ bits) for i in range(n_chan)])

    got = swap(send, 1)
    pairs = [(k, jnp.stack([keep[k], got[k]])) for k in reversed(range(1, n_chan // 2))]
    far = {k: swap(pair, 2 * k) for k, pair in pairs}
    return [keep, got, *(far[k] for k in range(1, n_chan // 2))]


def arrivals(refs):
    z, core = position()
    keep, got, far = refs[0], refs[1], refs[2:]
    yield 2 * z + core, lambda *at: keep[0, *at]
    yield 2 * z + 1 - core, lambda *at: got[0, *at]
    for k, ref in enumerate(far, 1):
        yield 2 * (z ^ k) + core, lambda *at, ref=ref: ref[0, *at]
        yield 2 * (z ^ k) + 1 - core, lambda *at, ref=ref: ref[1, *at]


def project_kernel(n_terms, units, *refs):
    terms = refs[: 2 * n_terms]
    beam_ref, keep_ref, send_ref, vis_ref, flat_ref = refs[2 * n_terms], *refs[-4:]
    _, double, width = beam_ref.shape
    half, degrees = double // 2, width // FB
    n_slots = terms[0].shape[1]
    pairs = n_slots // 2
    pieces = [(u, i, s, h) for u in range(units) for i in range(pairs) for s in range(2) for h in range(2)]

    for at, (u, i, s, h) in enumerate(pieces):
        part, place = (2 * u + h) // units, (2 * u + h) % units * FB
        total = None
        for term in terms[part * n_terms : (part + 1) * n_terms]:
            value = term[0, 2 * i + s, place : place + FB, :]
            total = value if total is None else total + value
        real = total[:, :half].astype(jnp.bfloat16)
        imag = total[:, half:].astype(jnp.bfloat16)
        vis_ref[at, :FB, :half] = real
        vis_ref[at, FB:, :half] = imag
        vis_ref[at, :FB, half:] = -imag
        vis_ref[at, FB:, half:] = real

    per_pair = 2 * keep_ref.shape[0] // pairs
    rows = keep_ref.shape[2]
    per_tile = 128 // degrees
    sub = lax.broadcasted_iota(jnp.int32, (8, 128), 0)
    for at, (u, i, s, h) in enumerate(pieces):
        turned = beam_ref[(2 * i + s) * 2 * units + 2 * u + h]
        prod = jnp.dot(vis_ref[at], turned, preferred_element_type=jnp.float32)
        for p in range(2):
            for g in range(FB // 8):
                own = prod[p * FB + g * 8 : p * FB + g * 8 + 8, g * 8 * degrees : (g + 1) * 8 * degrees]
                pick = own[:, :128]
                for v in range(1, 8 // per_tile):
                    pick = jnp.where(sub // per_tile == v, own[:, v * 128 : (v + 1) * 128], pick)
                if per_tile == 2:
                    pick = jnp.where(sub % 2 == 0, pick, pltpu.roll(pick, degrees, 1))
                row = s * 4 * FB + p * 2 * FB + h * FB + g * 8
                flat_ref[row : row + 8, :] = pick
        if s == 1 and h == 1:
            coeffs = flat_ref[...].T[:degrees]
            for b in range(per_pair):
                put(i * per_pair + b, keep_ref, send_ref, (u,), coeffs[b * rows : (b + 1) * rows])


def load(beam, start, size, depth=6):
    n_slots, _, _, degrees, half = beam.shape
    per_slot = size // FB
    n_pieces = n_slots * per_slot
    depth = min(depth, n_pieces)

    def body(beam_ref, out_ref, held_ref, sems):
        def copy(at):
            f = pl.multiple_of(start + lax.rem(at, per_slot) * FB, FB)
            slot = lax.rem(at, depth)
            return pltpu.make_async_copy(
                beam_ref.at[lax.div(at, per_slot), pl.ds(f, FB)], held_ref.at[slot], sems.at[slot]
            )

        def step(at, carry):
            copy(at).wait()
            for p in range(2):
                block = held_ref[lax.rem(at, depth), :, p].reshape(FB * degrees, half)
                out_ref[at, p * half : (p + 1) * half, :] = block.T

            @pl.when(at + depth < n_pieces)
            def _():
                copy(at + depth).start()

            return carry

        for at in range(depth):
            copy(at).start()
        lax.fori_loop(0, n_pieces, step, 0)

    return pl.pallas_call(
        body,
        in_specs=[pl.BlockSpec(memory_space=pltpu.HBM)],
        out_specs=pl.BlockSpec(memory_space=pltpu.VMEM),
        out_shape=jax.ShapeDtypeStruct((n_pieces, 2 * half, FB * degrees), beam.dtype),
        scratch_shapes=[
            pltpu.VMEM((depth, FB, 2, degrees, half), beam.dtype),
            pltpu.SemaphoreType.DMA((depth,)),
        ],
        compiler_params=params(14),
        cost_estimate=pl.CostEstimate(
            flops=0, bytes_accessed=4 * n_pieces * FB * 2 * degrees * half, transcendentals=0
        ),
        name="load",
    )(beam)


def project(parts, beam, start, units, n_chan, n_units, buffers):
    _, double, width = beam.shape
    half, degrees = double // 2, width // FB
    n_slots = parts[0][0].shape[1]
    n_terms = len(parts[0])
    pairs = n_slots // 2
    rows = pairs * degrees // n_chan
    terms = [term for group in parts for term in group]
    place = start // (2 * FB) // units
    n_pieces = units * n_slots * 2

    def body(*refs):
        project_kernel(n_terms, units, *refs)

    term_spec = pl.BlockSpec((1, n_slots, units * FB, 2 * half), lambda i: (0, 0, 0, 0))
    return pl.pallas_call(
        body,
        grid=(1,),
        in_specs=[term_spec] * len(terms)
        + [pl.BlockSpec(memory_space=pltpu.VMEM)]
        + [pl.BlockSpec(memory_space=pl.ANY)] * len(buffers),
        out_specs=[pl.BlockSpec((n_chan // 2, units, rows, 8 * FB), lambda i: (0, place, 0, 0))] * 2,
        out_shape=[jax.ShapeDtypeStruct((n_chan // 2, n_units, rows, 8 * FB), jnp.float32)] * 2,
        scratch_shapes=[
            pltpu.VMEM((n_pieces, 2 * FB, 2 * half), jnp.bfloat16),
            pltpu.VMEM((8 * FB, 128), jnp.float32),
        ],
        input_output_aliases={len(terms) + 1 + i: i for i in range(len(buffers))},
        compiler_params=params(14),
        cost_estimate=pl.CostEstimate(
            flops=2 * n_slots * 2 * FB * units * 2 * degrees * half * 256,
            bytes_accessed=n_slots * 2 * FB * units * 2 * degrees * half * 2,
            transcendentals=0,
        ),
        name="project",
    )(*terms, beam, *buffers)


def split_kernel(cov_ref, high_ref, low_ref):
    cov = cov_ref[...]
    high = cov.astype(jnp.bfloat16)
    high_ref[...] = high
    low_ref[...] = (cov - high.astype(jnp.float32)).astype(jnp.bfloat16)


def split(cov, n_blocks=4):
    rows, cols = cov.shape
    spec = pl.BlockSpec((rows // n_blocks, cols), lambda i: (i, 0))
    half = jax.ShapeDtypeStruct(cov.shape, jnp.bfloat16)
    return pl.pallas_call(
        split_kernel,
        grid=(n_blocks,),
        in_specs=[spec],
        out_specs=[spec, spec],
        out_shape=[half, half],
        compiler_params=params(14),
        cost_estimate=pl.CostEstimate(
            flops=4 * cov.size, bytes_accessed=8 * cov.size, transcendentals=0
        ),
        name="split",
    )(cov)


def fill_kernel(n_in, *refs):
    high_ref, low_ref, flags_ref, keep_ref, send_ref, data_ref = refs[n_in:]
    n_src, n_rows, f_dev = data_ref.shape
    _, n_units, rows, lanes = refs[0].shape
    groups = lanes // (2 * FB)
    for src, take in arrivals(refs[:n_in]):
        for u in range(n_units):
            piece = take(u)
            for g in range(groups):
                data_ref[src, g * rows : (g + 1) * rows, u * 2 * FB : (u + 1) * 2 * FB] = piece[
                    :, g * 2 * FB : (g + 1) * 2 * FB
                ]
    data = jnp.concatenate([data_ref[src] for src in range(n_src)], axis=1)
    good = 1.0 - flags_ref[...].astype(jnp.float32)

    def total(values):
        return jnp.sum(values, axis=1, keepdims=True)

    def covered(vec):
        top = vec.astype(jnp.bfloat16)
        rest = (vec - top.astype(jnp.float32)).astype(jnp.bfloat16)
        both = jnp.concatenate([top, rest], axis=0)
        wide = jnp.dot(both, high_ref[...], preferred_element_type=jnp.float32)
        thin = jnp.dot(top, low_ref[...], preferred_element_type=jnp.float32)
        return wide[:n_rows] + (wide[n_rows:] + thin)

    resid = good * data
    direc = resid
    norm_now = total(resid * resid)
    signal = jnp.zeros_like(resid)

    def advance(step, carry):
        signal, resid, direc, norm_now = carry
        image = covered(direc)
        shifted = direc + good * image
        alpha = norm_now / (total(direc * shifted) + EPS)
        signal = signal + alpha * image
        resid = resid - alpha * shifted
        norm_next = total(resid * resid)
        direc = resid + norm_next / (norm_now + EPS) * direc
        return signal, resid, direc, norm_next

    signal, resid, direc, norm_now = lax.fori_loop(
        0, ITERS, advance, (signal, resid, direc, norm_now)
    )
    data = jnp.concatenate([data_ref[src] for src in range(n_src)], axis=1)
    filled = good * data + (1.0 - good) * signal
    for dst in range(n_src):
        put(dst, keep_ref, send_ref, (), filled[:, dst * f_dev : (dst + 1) * f_dev])


def fill(pieces, high, low, flags, f_dev):
    n_hi, _, rows, lanes = pieces[0].shape
    n_rows = lanes // (2 * FB) * rows
    n_freq = high.shape[0]

    def body(*refs):
        fill_kernel(len(pieces), *refs)

    return pl.pallas_call(
        body,
        in_specs=[pl.BlockSpec(memory_space=pltpu.VMEM)] * (len(pieces) + 3),
        out_specs=[pl.BlockSpec(memory_space=pltpu.VMEM)] * 2,
        out_shape=[jax.ShapeDtypeStruct((n_hi, n_rows, f_dev), jnp.float32)] * 2,
        scratch_shapes=[pltpu.VMEM((2 * n_hi, n_rows, f_dev), jnp.float32)],
        compiler_params=params(14),
        cost_estimate=pl.CostEstimate(
            flops=2 * ITERS * 3 * n_rows * n_freq * n_freq,
            bytes_accessed=4 * n_freq * n_freq,
            transcendentals=0,
        ),
        name="fill",
    )(*pieces, high, low, flags)


def gather_kernel(n_in, *refs):
    out_ref, stage_ref = refs[n_in:]
    n_src, n_rows, _ = stage_ref.shape
    for src, take in arrivals(refs[:n_in]):
        stage_ref[src] = take()
    pairs = out_ref.shape[0] // 2
    per_pair = n_src // pairs
    rows = n_rows // 4
    for src in range(n_src):
        i, block = src // per_pair, src % per_pair
        for g in range(4):
            out_ref[2 * i + g // 2, g % 2, block * rows : (block + 1) * rows, :] = stage_ref[
                src, g * rows : (g + 1) * rows, :
            ]


def gather(pieces, shape):
    def body(*refs):
        gather_kernel(len(pieces), *refs)

    n_hi, n_rows, f_dev = pieces[0].shape
    return pl.pallas_call(
        body,
        in_specs=[pl.BlockSpec(memory_space=pltpu.VMEM)] * len(pieces),
        out_specs=pl.BlockSpec(memory_space=pltpu.VMEM),
        out_shape=jax.ShapeDtypeStruct(shape, jnp.float32),
        scratch_shapes=[pltpu.VMEM((2 * n_hi, n_rows, f_dev), jnp.float32)],
        compiler_params=params(14),
        name="gather",
    )(*pieces)


def make_tables(m_modes, n_tm, t_dev):
    n_time = t_dev * n_tm
    times = lax.axis_index("tm") * t_dev + jnp.arange(t_dev, dtype=jnp.int32)
    index = m_modes[:, None] * times[None, :] % n_time
    angle = 2.0 * math.pi / n_time * index.astype(jnp.float32)
    return jnp.concatenate([jnp.cos(angle), jnp.sin(angle)], axis=0).astype(jnp.bfloat16)


def exchange(send, bit, n_tm):
    return lax.ppermute(send, "tm", [(i, i ^ bit) for i in range(n_tm)])


def make_chunks(n_units):
    sizes = [2, 2] if n_units == 4 else [1] * n_units
    return [(sum(sizes[:i]), size) for i, size in enumerate(sizes)]


def per_device(vis, beam, fg_cov, flags, m_modes):
    t_dev, f_dev, _ = vis.shape
    n_tm = lax.axis_size("tm")
    n_chan = lax.axis_size("chan")
    n_slots = m_modes.shape[0] // n_tm
    degrees = beam.shape[3]
    orders = bit_orders(n_tm)
    targets = [target_order(n_tm, bits) for bits in orders]
    n_units = f_dev // (2 * FB)
    chunks = make_chunks(n_units)
    n_chunks = len(chunks)
    n_steps = len(orders[0])
    high, low = split(fg_cov)

    parts = [None] * n_chunks
    sends = [None] * n_chunks

    def begin(chunk, tab):
        first, units = chunks[chunk]
        outs = transform(tab, vis, first * 2 * FB, units, targets, n_slots)
        parts[chunk] = [[outs[0]], [outs[2]]]
        sends[chunk] = [outs[1], outs[3]]

    def go_on(chunk, place):
        for h, bits in enumerate(orders):
            got = exchange(sends[chunk][h], bits[place], n_tm)
            parts[chunk][h].append(got)
            size = got.shape[0] // 2
            sends[chunk][h] = sum(term[size : 2 * size] for term in parts[chunk][h])

    tab = make_tables(m_modes, n_tm, t_dev)
    for chunk in range(n_chunks):
        begin(chunk, tab)
    blocks = []
    for chunk, (first, units) in enumerate(chunks):
        before = max(chunk - 1, 0)
        source = sends[-1][0] if chunk == 0 else sends[before][0]
        source, beam = lax.optimization_barrier((source, beam))
        if chunk == 0:
            sends[-1][0] = source
        else:
            sends[before][0] = source
        block = load(beam, first * 2 * FB, units * 2 * FB)
        keeps = [group[0] for group in parts[chunk]]
        *keeps, block = lax.optimization_barrier((*keeps, block))
        parts[chunk] = [[keep] for keep in keeps]
        blocks.append(block)
        go_on(chunk, 0)
    sends[-1][0], high, low = lax.optimization_barrier((sends[-1][0], high, low))
    for place in range(1, n_steps):
        for chunk in range(n_chunks):
            go_on(chunk, place)

    coeffs = []
    for chunk, (first, units) in enumerate(chunks):
        coeffs = project(
            parts[chunk], blocks[chunk], first * 2 * FB, units, n_chan, n_units, coeffs
        )
    pieces = exchange_chan(*coeffs, n_chan)
    whole = fill(pieces, high, low, flags[None, :], f_dev)
    back = exchange_chan(*whole, n_chan)
    return gather(back, (n_slots, 2, degrees, f_dev))


def solution(mesh):
    placed = (P("tm", "chan", None), P("tm", "chan", None, None, None), P(), P(), P())
    return jax.shard_map(
        per_device,
        mesh=mesh,
        in_specs=placed,
        out_specs=P("tm", None, None, "chan"),
        check_vma=False,
    )
```

```python
import math

import jax
import jax.numpy as jnp
from jax import lax
from jax.experimental import pallas as pl
from jax.experimental.pallas import tpu as pltpu
from jax.sharding import PartitionSpec as P

ITERS = 10
EPS = 1e-06
FB = 16


def params(mebibytes):
    return pltpu.CompilerParams(vmem_limit_bytes=mebibytes * 1024 * 1024)


def bit_orders(n_tm):
    bits = [1 << i for i in range(n_tm.bit_length() - 1)]
    return bits, bits[::-1]


def target_order(n_tm, bits):
    return sorted(range(n_tm), key=lambda r: [int(bool(r & b)) for b in bits])


def transform_kernel(orders, n_slots, start, units, tab_ref, vis_ref, *refs):
    outs, (held_ref, wide_ref, full_ref, sems) = refs[:-4], refs[-4:]
    _, n_dev_time, _, width = held_ref.shape
    n_tm = len(orders[0])
    n_time = n_dev_time * n_tm
    n_rows = n_tm * n_slots
    half = width // 2
    depth = n_dev_time * FB
    scale = 1.0 / math.sqrt(n_time)

    def copies(unit):
        size = n_dev_time // 2
        for piece in range(2):
            times = pl.ds(piece * size, size)
            source = vis_ref.at[times, pl.ds(start + unit * 2 * FB, 2 * FB), :]
            target = held_ref.at[unit, times]
            yield pltpu.make_async_copy(source, target, sems.at[unit, piece])

    for copy in copies(0):
        copy.start()

    times = lax.broadcasted_iota(jnp.int32, (n_dev_time, depth), 0)
    lanes = lax.broadcasted_iota(jnp.int32, (n_dev_time, depth), 1)
    spread = jnp.where(lax.div(lanes, FB) == times, 1.0, 0.0).astype(jnp.bfloat16)
    wide_ref[...] = jnp.dot(tab_ref[...], spread, preferred_element_type=jnp.float32)
    me = lax.axis_index("tm")
    sub = lax.broadcasted_iota(jnp.int32, (FB, depth), 0)
    same = lax.rem(lax.broadcasted_iota(jnp.int32, (FB, depth), 1), FB) == sub
    for r in range(n_tm):
        for j in range(n_slots):
            for which in range(2):
                mode = which * n_rows + (me ^ r) * n_slots + j
                wide = jnp.broadcast_to(wide_ref[pl.ds(mode, 1), :], (FB, depth))
                at = (which * n_rows + r * n_slots + j) * FB
                full_ref[at : at + FB, :] = jnp.where(same, wide, 0.0).astype(jnp.bfloat16)

    for unit in range(1, units):
        for copy in copies(unit):
            copy.start()

    for group in range(2 * units):
        part, place_f = group // units, group % units * FB
        order, keep, send = orders[part], outs[2 * part], outs[2 * part + 1]
        n_keep = keep.shape[0]
        if group % 2 == 0:
            for copy in copies(group // 2):
                copy.wait()
        first = group % 2 * FB
        data = held_ref[group // 2, :, first : first + FB, :].reshape(depth, width)
        prod = jnp.dot(full_ref[...], data, preferred_element_type=jnp.float32)
        cos_part, sin_part = prod[: n_rows * FB], prod[n_rows * FB :]
        real = (cos_part[:, :half] + sin_part[:, half:]) * scale
        imag = (cos_part[:, half:] - sin_part[:, :half]) * scale
        for place, r in enumerate(order):
            out = keep if place < n_keep else send
            for j in range(n_slots):
                at = (r * n_slots + j) * FB
                out[place % n_keep, j, place_f : place_f + FB, :half] = real[at : at + FB]
                out[place % n_keep, j, place_f : place_f + FB, half:] = imag[at : at + FB]


def transform(tab, vis, start, units, orders, n_slots):
    n_time, _, width = vis.shape
    n_tm = len(orders[0])
    depth = n_time * FB
    n_rows = n_tm * n_slots
    piece = jax.ShapeDtypeStruct((n_tm // 2, n_slots, units * FB, width), jnp.float32)

    def body(*refs):
        transform_kernel(orders, n_slots, start, units, *refs)

    return pl.pallas_call(
        body,
        in_specs=[
            pl.BlockSpec(memory_space=pltpu.VMEM),
            pl.BlockSpec(memory_space=pltpu.HBM),
        ],
        out_specs=[pl.BlockSpec(memory_space=pltpu.VMEM)] * 4,
        out_shape=[piece] * 4,
        scratch_shapes=[
            pltpu.VMEM((units, n_time, 2 * FB, width), jnp.bfloat16),
            pltpu.VMEM((2 * n_rows, depth), jnp.float32),
            pltpu.VMEM((2 * n_rows * FB, depth), jnp.bfloat16),
            pltpu.SemaphoreType.DMA((units, 2)),
        ],
        compiler_params=params(50),
        cost_estimate=pl.CostEstimate(
            flops=2 * 2 * n_rows * FB * depth * width * 2 * units,
            bytes_accessed=n_time * 2 * FB * units * width * 2 + 4 * 4 * piece.size,
            transcendentals=0,
        ),
        name="transform",
    )(tab, vis)


def position():
    me = lax.axis_index("chan")
    return lax.div(me, 2), lax.rem(me, 2)


def put(dst, keep_ref, send_ref, at, value):
    z, core = position()

    @pl.when(core == dst % 2)
    def _():
        keep_ref[(dst // 2) ^ z, *at] = value

    @pl.when(core != dst % 2)
    def _():
        send_ref[(dst // 2) ^ z, *at] = value


def exchange_chan(keep, send, n_chan):
    def swap(value, bits):
        return lax.ppermute(value, "chan", [(i, i ^ bits) for i in range(n_chan)])

    got = swap(send, 1)
    pairs = [(k, jnp.stack([keep[k], got[k]])) for k in reversed(range(1, n_chan // 2))]
    far = {k: swap(pair, 2 * k) for k, pair in pairs}
    return [keep, got, *(far[k] for k in range(1, n_chan // 2))]


def arrivals(refs):
    z, core = position()
    keep, got, far = refs[0], refs[1], refs[2:]
    yield 2 * z + core, lambda *at: keep[0, *at]
    yield 2 * z + 1 - core, lambda *at: got[0, *at]
    for k, ref in enumerate(far, 1):
        yield 2 * (z ^ k) + core, lambda *at, ref=ref: ref[0, *at]
        yield 2 * (z ^ k) + 1 - core, lambda *at, ref=ref: ref[1, *at]


def project_kernel(n_terms, units, *refs):
    terms = refs[: 2 * n_terms]
    beam_ref, keep_ref, send_ref, vis_ref, flat_ref = refs[2 * n_terms], *refs[-4:]
    _, double, width = beam_ref.shape
    half, degrees = double // 2, width // FB
    n_slots = terms[0].shape[1]
    pairs = n_slots // 2
    pieces = [(u, i, s, h) for u in range(units) for i in range(pairs) for s in range(2) for h in range(2)]

    for at, (u, i, s, h) in enumerate(pieces):
        part, place = (2 * u + h) // units, (2 * u + h) % units * FB
        total = None
        for term in terms[part * n_terms : (part + 1) * n_terms]:
            value = term[0, 2 * i + s, place : place + FB, :]
            total = value if total is None else total + value
        real = total[:, :half].astype(jnp.bfloat16)
        imag = total[:, half:].astype(jnp.bfloat16)
        vis_ref[at, :FB, :half] = real
        vis_ref[at, FB:, :half] = imag
        vis_ref[at, :FB, half:] = -imag
        vis_ref[at, FB:, half:] = real

    per_pair = 2 * keep_ref.shape[0] // pairs
    rows = keep_ref.shape[2]
    per_tile = 128 // degrees
    sub = lax.broadcasted_iota(jnp.int32, (8, 128), 0)
    for at, (u, i, s, h) in enumerate(pieces):
        turned = beam_ref[(2 * i + s) * 2 * units + 2 * u + h]
        prod = jnp.dot(vis_ref[at], turned, preferred_element_type=jnp.float32)
        for p in range(2):
            for g in range(FB // 8):
                own = prod[p * FB + g * 8 : p * FB + g * 8 + 8, g * 8 * degrees : (g + 1) * 8 * degrees]
                pick = own[:, :128]
                for v in range(1, 8 // per_tile):
                    pick = jnp.where(sub // per_tile == v, own[:, v * 128 : (v + 1) * 128], pick)
                if per_tile == 2:
                    pick = jnp.where(sub % 2 == 0, pick, pltpu.roll(pick, degrees, 1))
                row = s * 4 * FB + p * 2 * FB + h * FB + g * 8
                flat_ref[row : row + 8, :] = pick
        if s == 1 and h == 1:
            coeffs = flat_ref[...].T[:degrees]
            for b in range(per_pair):
                put(i * per_pair + b, keep_ref, send_ref, (u,), coeffs[b * rows : (b + 1) * rows])


def load(beam, start, size, depth=6):
    n_slots, _, _, degrees, half = beam.shape
    per_slot = size // FB
    n_pieces = n_slots * per_slot
    depth = min(depth, n_pieces)

    def body(beam_ref, out_ref, held_ref, sems):
        def copy(at):
            f = pl.multiple_of(start + lax.rem(at, per_slot) * FB, FB)
            slot = lax.rem(at, depth)
            return pltpu.make_async_copy(
                beam_ref.at[lax.div(at, per_slot), pl.ds(f, FB)], held_ref.at[slot], sems.at[slot]
            )

        def step(at, carry):
            copy(at).wait()
            for p in range(2):
                block = held_ref[lax.rem(at, depth), :, p].reshape(FB * degrees, half)
                out_ref[at, p * half : (p + 1) * half, :] = block.T

            @pl.when(at + depth < n_pieces)
            def _():
                copy(at + depth).start()

            return carry

        for at in range(depth):
            copy(at).start()
        lax.fori_loop(0, n_pieces, step, 0)

    return pl.pallas_call(
        body,
        in_specs=[pl.BlockSpec(memory_space=pltpu.HBM)],
        out_specs=pl.BlockSpec(memory_space=pltpu.VMEM),
        out_shape=jax.ShapeDtypeStruct((n_pieces, 2 * half, FB * degrees), beam.dtype),
        scratch_shapes=[
            pltpu.VMEM((depth, FB, 2, degrees, half), beam.dtype),
            pltpu.SemaphoreType.DMA((depth,)),
        ],
        compiler_params=params(14),
        cost_estimate=pl.CostEstimate(
            flops=0, bytes_accessed=4 * n_pieces * FB * 2 * degrees * half, transcendentals=0
        ),
        name="load",
    )(beam)


def project(parts, beam, start, units, n_chan, n_units, buffers):
    _, double, width = beam.shape
    half, degrees = double // 2, width // FB
    n_slots = parts[0][0].shape[1]
    n_terms = len(parts[0])
    pairs = n_slots // 2
    rows = pairs * degrees // n_chan
    terms = [term for group in parts for term in group]
    place = start // (2 * FB) // units
    n_pieces = units * n_slots * 2

    def body(*refs):
        project_kernel(n_terms, units, *refs)

    term_spec = pl.BlockSpec((1, n_slots, units * FB, 2 * half), lambda i: (0, 0, 0, 0))
    return pl.pallas_call(
        body,
        grid=(1,),
        in_specs=[term_spec] * len(terms)
        + [pl.BlockSpec(memory_space=pltpu.VMEM)]
        + [pl.BlockSpec(memory_space=pl.ANY)] * len(buffers),
        out_specs=[pl.BlockSpec((n_chan // 2, units, rows, 8 * FB), lambda i: (0, place, 0, 0))] * 2,
        out_shape=[jax.ShapeDtypeStruct((n_chan // 2, n_units, rows, 8 * FB), jnp.float32)] * 2,
        scratch_shapes=[
            pltpu.VMEM((n_pieces, 2 * FB, 2 * half), jnp.bfloat16),
            pltpu.VMEM((8 * FB, 128), jnp.float32),
        ],
        input_output_aliases={len(terms) + 1 + i: i for i in range(len(buffers))},
        compiler_params=params(14),
        cost_estimate=pl.CostEstimate(
            flops=2 * n_slots * 2 * FB * units * 2 * degrees * half * 256,
            bytes_accessed=n_slots * 2 * FB * units * 2 * degrees * half * 2,
            transcendentals=0,
        ),
        name="project",
    )(*terms, beam, *buffers)


def split_kernel(cov_ref, high_ref, low_ref):
    cov = cov_ref[...]
    high = cov.astype(jnp.bfloat16)
    high_ref[...] = high
    low_ref[...] = (cov - high.astype(jnp.float32)).astype(jnp.bfloat16)


def split(cov, n_blocks=4):
    rows, cols = cov.shape
    spec = pl.BlockSpec((rows // n_blocks, cols), lambda i: (i, 0))
    half = jax.ShapeDtypeStruct(cov.shape, jnp.bfloat16)
    return pl.pallas_call(
        split_kernel,
        grid=(n_blocks,),
        in_specs=[spec],
        out_specs=[spec, spec],
        out_shape=[half, half],
        compiler_params=params(14),
        cost_estimate=pl.CostEstimate(
            flops=4 * cov.size, bytes_accessed=8 * cov.size, transcendentals=0
        ),
        name="split",
    )(cov)


def fill_kernel(n_in, *refs):
    high_ref, low_ref, flags_ref, keep_ref, send_ref, data_ref = refs[n_in:]
    n_src, n_rows, f_dev = data_ref.shape
    _, n_units, rows, lanes = refs[0].shape
    groups = lanes // (2 * FB)
    for src, take in arrivals(refs[:n_in]):
        for u in range(n_units):
            piece = take(u)
            for g in range(groups):
                data_ref[src, g * rows : (g + 1) * rows, u * 2 * FB : (u + 1) * 2 * FB] = piece[
                    :, g * 2 * FB : (g + 1) * 2 * FB
                ]
    data = jnp.concatenate([data_ref[src] for src in range(n_src)], axis=1)
    good = 1.0 - flags_ref[...].astype(jnp.float32)

    n_freq = n_src * f_dev
    halves = [slice(at, at + n_freq // 2) for at in (0, n_freq // 2)]

    def total(values):
        return jnp.sum(values, axis=1, keepdims=True)

    resid = good * data
    direc = resid
    norm_now = total(resid * resid)
    signal = jnp.zeros_like(resid)

    def advance(step, carry):
        signal, resid, direc, norm_now = carry
        top = direc.astype(jnp.bfloat16)
        rest = (direc - top.astype(jnp.float32)).astype(jnp.bfloat16)
        both = jnp.concatenate([top, rest], axis=0)
        images, shifts, curves = [], [], []
        for cols in halves:
            wide = jnp.dot(both, high_ref[:, cols], preferred_element_type=jnp.float32)
            thin = jnp.dot(top, low_ref[:, cols], preferred_element_type=jnp.float32)
            image = wide[:n_rows] + (wide[n_rows:] + thin)
            shift = direc[:, cols] + good[:, cols] * image
            images.append(image)
            shifts.append(shift)
            curves.append(direc[:, cols] * shift)
        image, shifted = jnp.concatenate(images, axis=1), jnp.concatenate(shifts, axis=1)
        alpha = norm_now / (total(curves[0] + curves[1]) + EPS)
        signal = signal + alpha * image
        resid = resid - alpha * shifted
        norm_next = total(resid * resid)
        direc = resid + norm_next / (norm_now + EPS) * direc
        return signal, resid, direc, norm_next

    signal, resid, direc, norm_now = lax.fori_loop(
        0, ITERS, advance, (signal, resid, direc, norm_now)
    )
    data = jnp.concatenate([data_ref[src] for src in range(n_src)], axis=1)
    filled = good * data + (1.0 - good) * signal
    for dst in range(n_src):
        put(dst, keep_ref, send_ref, (), filled[:, dst * f_dev : (dst + 1) * f_dev])


def fill(pieces, high, low, flags, f_dev):
    n_hi, _, rows, lanes = pieces[0].shape
    n_rows = lanes // (2 * FB) * rows
    n_freq = high.shape[0]

    def body(*refs):
        fill_kernel(len(pieces), *refs)

    return pl.pallas_call(
        body,
        in_specs=[pl.BlockSpec(memory_space=pltpu.VMEM)] * (len(pieces) + 3),
        out_specs=[pl.BlockSpec(memory_space=pltpu.VMEM)] * 2,
        out_shape=[jax.ShapeDtypeStruct((n_hi, n_rows, f_dev), jnp.float32)] * 2,
        scratch_shapes=[pltpu.VMEM((2 * n_hi, n_rows, f_dev), jnp.float32)],
        compiler_params=params(14),
        cost_estimate=pl.CostEstimate(
            flops=2 * ITERS * 3 * n_rows * n_freq * n_freq,
            bytes_accessed=4 * n_freq * n_freq,
            transcendentals=0,
        ),
        name="fill",
    )(*pieces, high, low, flags)


def gather_kernel(n_in, *refs):
    out_ref, stage_ref = refs[n_in:]
    n_src, n_rows, _ = stage_ref.shape
    for src, take in arrivals(refs[:n_in]):
        stage_ref[src] = take()
    pairs = out_ref.shape[0] // 2
    per_pair = n_src // pairs
    rows = n_rows // 4
    for src in range(n_src):
        i, block = src // per_pair, src % per_pair
        for g in range(4):
            out_ref[2 * i + g // 2, g % 2, block * rows : (block + 1) * rows, :] = stage_ref[
                src, g * rows : (g + 1) * rows, :
            ]


def gather(pieces, shape):
    def body(*refs):
        gather_kernel(len(pieces), *refs)

    n_hi, n_rows, f_dev = pieces[0].shape
    return pl.pallas_call(
        body,
        in_specs=[pl.BlockSpec(memory_space=pltpu.VMEM)] * len(pieces),
        out_specs=pl.BlockSpec(memory_space=pltpu.VMEM),
        out_shape=jax.ShapeDtypeStruct(shape, jnp.float32),
        scratch_shapes=[pltpu.VMEM((2 * n_hi, n_rows, f_dev), jnp.float32)],
        compiler_params=params(14),
        name="gather",
    )(*pieces)


def make_tables(m_modes, n_tm, t_dev):
    n_time = t_dev * n_tm
    times = lax.axis_index("tm") * t_dev + jnp.arange(t_dev, dtype=jnp.int32)
    index = m_modes[:, None] * times[None, :] % n_time
    angle = 2.0 * math.pi / n_time * index.astype(jnp.float32)
    return jnp.concatenate([jnp.cos(angle), jnp.sin(angle)], axis=0).astype(jnp.bfloat16)


def exchange(send, bit, n_tm):
    return lax.ppermute(send, "tm", [(i, i ^ bit) for i in range(n_tm)])


def make_chunks(n_units):
    sizes = [2, 2] if n_units == 4 else [1] * n_units
    return [(sum(sizes[:i]), size) for i, size in enumerate(sizes)]


def per_device(vis, beam, fg_cov, flags, m_modes):
    t_dev, f_dev, _ = vis.shape
    n_tm = lax.axis_size("tm")
    n_chan = lax.axis_size("chan")
    n_slots = m_modes.shape[0] // n_tm
    degrees = beam.shape[3]
    orders = bit_orders(n_tm)
    targets = [target_order(n_tm, bits) for bits in orders]
    n_units = f_dev // (2 * FB)
    chunks = make_chunks(n_units)
    n_chunks = len(chunks)
    n_steps = len(orders[0])
    high, low = split(fg_cov)

    parts = [None] * n_chunks
    sends = [None] * n_chunks

    def begin(chunk, tab):
        first, units = chunks[chunk]
        outs = transform(tab, vis, first * 2 * FB, units, targets, n_slots)
        parts[chunk] = [[outs[0]], [outs[2]]]
        sends[chunk] = [outs[1], outs[3]]

    def go_on(chunk, place):
        for h, bits in enumerate(orders):
            got = exchange(sends[chunk][h], bits[place], n_tm)
            parts[chunk][h].append(got)
            size = got.shape[0] // 2
            sends[chunk][h] = sum(term[size : 2 * size] for term in parts[chunk][h])

    tab = make_tables(m_modes, n_tm, t_dev)
    for chunk in range(n_chunks):
        begin(chunk, tab)
    blocks = []
    for chunk, (first, units) in enumerate(chunks):
        before = max(chunk - 1, 0)
        source = sends[-1][0] if chunk == 0 else sends[before][0]
        source, beam = lax.optimization_barrier((source, beam))
        if chunk == 0:
            sends[-1][0] = source
        else:
            sends[before][0] = source
        block = load(beam, first * 2 * FB, units * 2 * FB)
        keeps = [group[0] for group in parts[chunk]]
        *keeps, block = lax.optimization_barrier((*keeps, block))
        parts[chunk] = [[keep] for keep in keeps]
        blocks.append(block)
        go_on(chunk, 0)
    sends[-1][0], high, low = lax.optimization_barrier((sends[-1][0], high, low))
    for place in range(1, n_steps):
        for chunk in range(n_chunks):
            go_on(chunk, place)

    coeffs = []
    for chunk, (first, units) in enumerate(chunks):
        coeffs = project(
            parts[chunk], blocks[chunk], first * 2 * FB, units, n_chan, n_units, coeffs
        )
    pieces = exchange_chan(*coeffs, n_chan)
    whole = fill(pieces, high, low, flags[None, :], f_dev)
    back = exchange_chan(*whole, n_chan)
    return gather(back, (n_slots, 2, degrees, f_dev))


def solution(mesh):
    placed = (P("tm", "chan", None), P("tm", "chan", None, None, None), P(), P(), P())
    return jax.shard_map(
        per_device,
        mesh=mesh,
        in_specs=placed,
        out_specs=P("tm", None, None, "chan"),
        check_vma=False,
    )
```

```python
import math

import jax
import jax.numpy as jnp
from jax import lax
from jax.experimental import pallas as pl
from jax.experimental.pallas import tpu as pltpu
from jax.sharding import PartitionSpec as P

ITERS = 10
EPS = 1e-06
FB = 16


def params(mebibytes):
    return pltpu.CompilerParams(vmem_limit_bytes=mebibytes * 1024 * 1024)


def bit_orders(n_tm):
    bits = [1 << i for i in range(n_tm.bit_length() - 1)]
    return bits, bits[::-1]


def target_order(n_tm, bits):
    return sorted(range(n_tm), key=lambda r: [int(bool(r & b)) for b in bits])


def transform_kernel(orders, n_slots, start, units, tab_ref, vis_ref, *refs):
    outs, (held_ref, wide_ref, full_ref, sems) = refs[:-4], refs[-4:]
    _, n_dev_time, _, width = held_ref.shape
    n_tm = len(orders[0])
    n_time = n_dev_time * n_tm
    n_rows = n_tm * n_slots
    half = width // 2
    depth = n_dev_time * FB
    scale = 1.0 / math.sqrt(n_time)

    def copies(unit):
        size = n_dev_time // 2
        for piece in range(2):
            times = pl.ds(piece * size, size)
            source = vis_ref.at[times, pl.ds(start + unit * 2 * FB, 2 * FB), :]
            target = held_ref.at[unit, times]
            yield pltpu.make_async_copy(source, target, sems.at[unit, piece])

    for unit in range(units):
        for copy in copies(unit):
            copy.start()

    times = lax.broadcasted_iota(jnp.int32, (n_dev_time, depth), 0)
    lanes = lax.broadcasted_iota(jnp.int32, (n_dev_time, depth), 1)
    spread = jnp.where(lax.div(lanes, FB) == times, 1.0, 0.0).astype(jnp.bfloat16)
    wide_ref[...] = jnp.dot(tab_ref[...], spread, preferred_element_type=jnp.float32)
    me = lax.axis_index("tm")
    sub = lax.broadcasted_iota(jnp.int32, (FB, depth), 0)
    same = lax.rem(lax.broadcasted_iota(jnp.int32, (FB, depth), 1), FB) == sub
    for r in range(n_tm):
        for j in range(n_slots):
            for which in range(2):
                mode = which * n_rows + (me ^ r) * n_slots + j
                wide = jnp.broadcast_to(wide_ref[pl.ds(mode, 1), :], (FB, depth))
                at = (which * n_rows + r * n_slots + j) * FB
                full_ref[at : at + FB, :] = jnp.where(same, wide, 0.0).astype(jnp.bfloat16)

    for group in range(2 * units):
        part, place_f = group // units, group % units * FB
        order, keep, send = orders[part], outs[2 * part], outs[2 * part + 1]
        n_keep = keep.shape[0]
        if group % 2 == 0:
            for copy in copies(group // 2):
                copy.wait()
        first = group % 2 * FB
        data = held_ref[group // 2, :, first : first + FB, :].reshape(depth, width)
        prod = jnp.dot(full_ref[...], data, preferred_element_type=jnp.float32)
        cos_part, sin_part = prod[: n_rows * FB], prod[n_rows * FB :]
        real = (cos_part[:, :half] + sin_part[:, half:]) * scale
        imag = (cos_part[:, half:] - sin_part[:, :half]) * scale
        for place, r in enumerate(order):
            out = keep if place < n_keep else send
            for j in range(n_slots):
                at = (r * n_slots + j) * FB
                out[place % n_keep, j, place_f : place_f + FB, :half] = real[at : at + FB]
                out[place % n_keep, j, place_f : place_f + FB, half:] = imag[at : at + FB]


def transform(tab, vis, start, units, orders, n_slots):
    n_time, _, width = vis.shape
    n_tm = len(orders[0])
    depth = n_time * FB
    n_rows = n_tm * n_slots
    piece = jax.ShapeDtypeStruct((n_tm // 2, n_slots, units * FB, width), jnp.float32)

    def body(*refs):
        transform_kernel(orders, n_slots, start, units, *refs)

    return pl.pallas_call(
        body,
        in_specs=[
            pl.BlockSpec(memory_space=pltpu.VMEM),
            pl.BlockSpec(memory_space=pltpu.HBM),
        ],
        out_specs=[pl.BlockSpec(memory_space=pltpu.VMEM)] * 4,
        out_shape=[piece] * 4,
        scratch_shapes=[
            pltpu.VMEM((units, n_time, 2 * FB, width), jnp.bfloat16),
            pltpu.VMEM((2 * n_rows, depth), jnp.float32),
            pltpu.VMEM((2 * n_rows * FB, depth), jnp.bfloat16),
            pltpu.SemaphoreType.DMA((units, 2)),
        ],
        compiler_params=params(50),
        cost_estimate=pl.CostEstimate(
            flops=2 * 2 * n_rows * FB * depth * width * 2 * units,
            bytes_accessed=n_time * 2 * FB * units * width * 2 + 4 * 4 * piece.size,
            transcendentals=0,
        ),
        name="transform",
    )(tab, vis)


def position():
    me = lax.axis_index("chan")
    return lax.div(me, 2), lax.rem(me, 2)


def put(dst, keep_ref, send_ref, at, value):
    _, core = position()

    @pl.when(core == dst % 2)
    def _():
        keep_ref[dst // 2, *at] = value

    @pl.when(core != dst % 2)
    def _():
        send_ref[dst // 2, *at] = value


def exchange_chan(keep, send, n_chan):
    got = lax.ppermute(send, "chan", [(i, i ^ 1) for i in range(n_chan)])
    groups = [list(range(core, n_chan, 2)) for core in range(2)]
    both = jnp.stack([keep, got], axis=1)
    return [lax.all_to_all(both, "chan", 0, 0, axis_index_groups=groups, tiled=True)]


def arrivals(refs):
    _, core = position()
    for z in range(refs[0].shape[0]):
        yield 2 * z + core, lambda *at, z=z: refs[0][z, 0, *at]
        yield 2 * z + 1 - core, lambda *at, z=z: refs[0][z, 1, *at]


def project_kernel(n_terms, units, *refs):
    terms = refs[: 2 * n_terms]
    beam_ref, keep_ref, send_ref, vis_ref, flat_ref = refs[2 * n_terms], *refs[-4:]
    _, double, width = beam_ref.shape
    half, degrees = double // 2, width // FB
    n_slots = terms[0].shape[1]
    pairs = n_slots // 2
    pieces = [(u, i, s, h) for u in range(units) for i in range(pairs) for s in range(2) for h in range(2)]

    for at, (u, i, s, h) in enumerate(pieces):
        part, place = (2 * u + h) // units, (2 * u + h) % units * FB
        total = None
        for term in terms[part * n_terms : (part + 1) * n_terms]:
            value = term[0, 2 * i + s, place : place + FB, :]
            total = value if total is None else total + value
        real = total[:, :half].astype(jnp.bfloat16)
        imag = total[:, half:].astype(jnp.bfloat16)
        vis_ref[at, :FB, :half] = real
        vis_ref[at, FB:, :half] = imag
        vis_ref[at, :FB, half:] = -imag
        vis_ref[at, FB:, half:] = real

    per_pair = 2 * keep_ref.shape[0] // pairs
    rows = keep_ref.shape[2]
    per_tile = 128 // degrees
    sub = lax.broadcasted_iota(jnp.int32, (8, 128), 0)
    for at, (u, i, s, h) in enumerate(pieces):
        turned = beam_ref[(2 * i + s) * 2 * units + 2 * u + h]
        prod = jnp.dot(vis_ref[at], turned, preferred_element_type=jnp.float32)
        for p in range(2):
            for g in range(FB // 8):
                own = prod[p * FB + g * 8 : p * FB + g * 8 + 8, g * 8 * degrees : (g + 1) * 8 * degrees]
                pick = own[:, :128]
                for v in range(1, 8 // per_tile):
                    pick = jnp.where(sub // per_tile == v, own[:, v * 128 : (v + 1) * 128], pick)
                if per_tile == 2:
                    pick = jnp.where(sub % 2 == 0, pick, pltpu.roll(pick, degrees, 1))
                row = s * 4 * FB + p * 2 * FB + h * FB + g * 8
                flat_ref[row : row + 8, :] = pick
        if s == 1 and h == 1:
            coeffs = flat_ref[...].T[:degrees]
            for b in range(per_pair):
                put(i * per_pair + b, keep_ref, send_ref, (u,), coeffs[b * rows : (b + 1) * rows])


def load(beam, start, size, depth=6):
    n_slots, _, _, degrees, half = beam.shape
    per_slot = size // FB
    n_pieces = n_slots * per_slot
    depth = min(depth, n_pieces)

    def body(beam_ref, out_ref, held_ref, sems):
        def copy(at):
            f = pl.multiple_of(start + lax.rem(at, per_slot) * FB, FB)
            slot = lax.rem(at, depth)
            return pltpu.make_async_copy(
                beam_ref.at[lax.div(at, per_slot), pl.ds(f, FB)], held_ref.at[slot], sems.at[slot]
            )

        def step(at, carry):
            copy(at).wait()
            for p in range(2):
                block = held_ref[lax.rem(at, depth), :, p].reshape(FB * degrees, half)
                out_ref[at, p * half : (p + 1) * half, :] = block.T

            @pl.when(at + depth < n_pieces)
            def _():
                copy(at + depth).start()

            return carry

        for at in range(depth):
            copy(at).start()
        lax.fori_loop(0, n_pieces, step, 0)

    return pl.pallas_call(
        body,
        in_specs=[pl.BlockSpec(memory_space=pltpu.HBM)],
        out_specs=pl.BlockSpec(memory_space=pltpu.VMEM),
        out_shape=jax.ShapeDtypeStruct((n_pieces, 2 * half, FB * degrees), beam.dtype),
        scratch_shapes=[
            pltpu.VMEM((depth, FB, 2, degrees, half), beam.dtype),
            pltpu.SemaphoreType.DMA((depth,)),
        ],
        compiler_params=params(14),
        cost_estimate=pl.CostEstimate(
            flops=0, bytes_accessed=4 * n_pieces * FB * 2 * degrees * half, transcendentals=0
        ),
        name="load",
    )(beam)


def project(parts, beam, start, units, n_chan, n_units, buffers):
    _, double, width = beam.shape
    half, degrees = double // 2, width // FB
    n_slots = parts[0][0].shape[1]
    n_terms = len(parts[0])
    pairs = n_slots // 2
    rows = pairs * degrees // n_chan
    terms = [term for group in parts for term in group]
    place = start // (2 * FB) // units
    n_pieces = units * n_slots * 2

    def body(*refs):
        project_kernel(n_terms, units, *refs)

    term_spec = pl.BlockSpec((1, n_slots, units * FB, 2 * half), lambda i: (0, 0, 0, 0))
    return pl.pallas_call(
        body,
        grid=(1,),
        in_specs=[term_spec] * len(terms)
        + [pl.BlockSpec(memory_space=pltpu.VMEM)]
        + [pl.BlockSpec(memory_space=pl.ANY)] * len(buffers),
        out_specs=[pl.BlockSpec((n_chan // 2, units, rows, 8 * FB), lambda i: (0, place, 0, 0))] * 2,
        out_shape=[jax.ShapeDtypeStruct((n_chan // 2, n_units, rows, 8 * FB), jnp.float32)] * 2,
        scratch_shapes=[
            pltpu.VMEM((n_pieces, 2 * FB, 2 * half), jnp.bfloat16),
            pltpu.VMEM((8 * FB, 128), jnp.float32),
        ],
        input_output_aliases={len(terms) + 1 + i: i for i in range(len(buffers))},
        compiler_params=params(14),
        cost_estimate=pl.CostEstimate(
            flops=2 * n_slots * 2 * FB * units * 2 * degrees * half * 256,
            bytes_accessed=n_slots * 2 * FB * units * 2 * degrees * half * 2,
            transcendentals=0,
        ),
        name="project",
    )(*terms, beam, *buffers)


def split_kernel(cov_ref, high_ref, low_ref):
    cov = cov_ref[...]
    high = cov.astype(jnp.bfloat16)
    high_ref[...] = high
    low_ref[...] = (cov - high.astype(jnp.float32)).astype(jnp.bfloat16)


def split(cov, n_blocks=4):
    rows, cols = cov.shape
    spec = pl.BlockSpec((rows // n_blocks, cols), lambda i: (i, 0))
    half = jax.ShapeDtypeStruct(cov.shape, jnp.bfloat16)
    return pl.pallas_call(
        split_kernel,
        grid=(n_blocks,),
        in_specs=[spec],
        out_specs=[spec, spec],
        out_shape=[half, half],
        compiler_params=params(14),
        cost_estimate=pl.CostEstimate(
            flops=4 * cov.size, bytes_accessed=8 * cov.size, transcendentals=0
        ),
        name="split",
    )(cov)


def fill_kernel(n_in, *refs):
    high_ref, low_ref, flags_ref, keep_ref, send_ref, data_ref = refs[n_in:]
    n_src, n_rows, f_dev = data_ref.shape
    _, _, n_units, rows, lanes = refs[0].shape
    groups = lanes // (2 * FB)
    for src, take in arrivals(refs[:n_in]):
        for u in range(n_units):
            piece = take(u)
            for g in range(groups):
                data_ref[src, g * rows : (g + 1) * rows, u * 2 * FB : (u + 1) * 2 * FB] = piece[
                    :, g * 2 * FB : (g + 1) * 2 * FB
                ]
    data = jnp.concatenate([data_ref[src] for src in range(n_src)], axis=1)
    good = 1.0 - flags_ref[...].astype(jnp.float32)

    def total(values):
        return jnp.sum(values, axis=1, keepdims=True)

    def covered(vec):
        top = vec.astype(jnp.bfloat16)
        rest = (vec - top.astype(jnp.float32)).astype(jnp.bfloat16)
        both = jnp.concatenate([top, rest], axis=0)
        wide = jnp.dot(both, high_ref[...], preferred_element_type=jnp.float32)
        thin = jnp.dot(top, low_ref[...], preferred_element_type=jnp.float32)
        return wide[:n_rows] + (wide[n_rows:] + thin)

    resid = good * data
    direc = resid
    norm_now = total(resid * resid)
    signal = jnp.zeros_like(resid)

    def advance(step, carry):
        signal, resid, direc, norm_now = carry
        image = covered(direc)
        shifted = direc + good * image
        alpha = norm_now / (total(direc * shifted) + EPS)
        signal = signal + alpha * image
        resid = resid - alpha * shifted
        norm_next = total(resid * resid)
        direc = resid + norm_next / (norm_now + EPS) * direc
        return signal, resid, direc, norm_next

    signal, resid, direc, norm_now = lax.fori_loop(
        0, ITERS, advance, (signal, resid, direc, norm_now)
    )
    data = jnp.concatenate([data_ref[src] for src in range(n_src)], axis=1)
    filled = good * data + (1.0 - good) * signal
    for dst in range(n_src):
        put(dst, keep_ref, send_ref, (), filled[:, dst * f_dev : (dst + 1) * f_dev])


def fill(pieces, high, low, flags, f_dev):
    n_hi, _, _, rows, lanes = pieces[0].shape
    n_rows = lanes // (2 * FB) * rows
    n_freq = high.shape[0]

    def body(*refs):
        fill_kernel(len(pieces), *refs)

    return pl.pallas_call(
        body,
        in_specs=[pl.BlockSpec(memory_space=pltpu.VMEM)] * (len(pieces) + 3),
        out_specs=[pl.BlockSpec(memory_space=pltpu.VMEM)] * 2,
        out_shape=[jax.ShapeDtypeStruct((n_hi, n_rows, f_dev), jnp.float32)] * 2,
        scratch_shapes=[pltpu.VMEM((2 * n_hi, n_rows, f_dev), jnp.float32)],
        compiler_params=params(14),
        cost_estimate=pl.CostEstimate(
            flops=2 * ITERS * 3 * n_rows * n_freq * n_freq,
            bytes_accessed=4 * n_freq * n_freq,
            transcendentals=0,
        ),
        name="fill",
    )(*pieces, high, low, flags)


def gather_kernel(n_in, *refs):
    out_ref, stage_ref = refs[n_in:]
    n_src, n_rows, _ = stage_ref.shape
    for src, take in arrivals(refs[:n_in]):
        stage_ref[src] = take()
    pairs = out_ref.shape[0] // 2
    per_pair = n_src // pairs
    rows = n_rows // 4
    for src in range(n_src):
        i, block = src // per_pair, src % per_pair
        for g in range(4):
            out_ref[2 * i + g // 2, g % 2, block * rows : (block + 1) * rows, :] = stage_ref[
                src, g * rows : (g + 1) * rows, :
            ]


def gather(pieces, shape):
    def body(*refs):
        gather_kernel(len(pieces), *refs)

    n_hi, _, n_rows, f_dev = pieces[0].shape
    return pl.pallas_call(
        body,
        in_specs=[pl.BlockSpec(memory_space=pltpu.VMEM)] * len(pieces),
        out_specs=pl.BlockSpec(memory_space=pltpu.VMEM),
        out_shape=jax.ShapeDtypeStruct(shape, jnp.float32),
        scratch_shapes=[pltpu.VMEM((2 * n_hi, n_rows, f_dev), jnp.float32)],
        compiler_params=params(14),
        name="gather",
    )(*pieces)


def make_tables(m_modes, n_tm, t_dev):
    n_time = t_dev * n_tm
    times = lax.axis_index("tm") * t_dev + jnp.arange(t_dev, dtype=jnp.int32)
    index = m_modes[:, None] * times[None, :] % n_time
    angle = 2.0 * math.pi / n_time * index.astype(jnp.float32)
    return jnp.concatenate([jnp.cos(angle), jnp.sin(angle)], axis=0).astype(jnp.bfloat16)


def exchange(send, bit, n_tm):
    return lax.ppermute(send, "tm", [(i, i ^ bit) for i in range(n_tm)])


def make_chunks(n_units):
    sizes = [2, 2] if n_units == 4 else [1] * n_units
    return [(sum(sizes[:i]), size) for i, size in enumerate(sizes)]


def per_device(vis, beam, fg_cov, flags, m_modes):
    t_dev, f_dev, _ = vis.shape
    n_tm = lax.axis_size("tm")
    n_chan = lax.axis_size("chan")
    n_slots = m_modes.shape[0] // n_tm
    degrees = beam.shape[3]
    orders = bit_orders(n_tm)
    targets = [target_order(n_tm, bits) for bits in orders]
    n_units = f_dev // (2 * FB)
    chunks = make_chunks(n_units)
    n_chunks = len(chunks)
    n_steps = len(orders[0])
    high, low = split(fg_cov)

    parts = [None] * n_chunks
    sends = [None] * n_chunks

    def begin(chunk, tab):
        first, units = chunks[chunk]
        outs = transform(tab, vis, first * 2 * FB, units, targets, n_slots)
        parts[chunk] = [[outs[0]], [outs[2]]]
        sends[chunk] = [outs[1], outs[3]]

    def go_on(chunk, place):
        for h, bits in enumerate(orders):
            got = exchange(sends[chunk][h], bits[place], n_tm)
            parts[chunk][h].append(got)
            size = got.shape[0] // 2
            sends[chunk][h] = sum(term[size : 2 * size] for term in parts[chunk][h])

    tab = make_tables(m_modes, n_tm, t_dev)
    for chunk in range(n_chunks):
        begin(chunk, tab)
    blocks = []
    for chunk, (first, units) in enumerate(chunks):
        before = max(chunk - 1, 0)
        source = sends[-1][0] if chunk == 0 else sends[before][0]
        source, beam = lax.optimization_barrier((source, beam))
        if chunk == 0:
            sends[-1][0] = source
        else:
            sends[before][0] = source
        block = load(beam, first * 2 * FB, units * 2 * FB)
        keeps = [group[0] for group in parts[chunk]]
        *keeps, block = lax.optimization_barrier((*keeps, block))
        parts[chunk] = [[keep] for keep in keeps]
        blocks.append(block)
        go_on(chunk, 0)
    sends[-1][0], high, low = lax.optimization_barrier((sends[-1][0], high, low))
    for place in range(1, n_steps):
        for chunk in range(n_chunks):
            go_on(chunk, place)

    coeffs = []
    for chunk, (first, units) in enumerate(chunks):
        coeffs = project(
            parts[chunk], blocks[chunk], first * 2 * FB, units, n_chan, n_units, coeffs
        )
    pieces = exchange_chan(*coeffs, n_chan)
    whole = fill(pieces, high, low, flags[None, :], f_dev)
    back = exchange_chan(*whole, n_chan)
    return gather(back, (n_slots, 2, degrees, f_dev))


def solution(mesh):
    placed = (P("tm", "chan", None), P("tm", "chan", None, None, None), P(), P(), P())
    return jax.shard_map(
        per_device,
        mesh=mesh,
        in_specs=placed,
        out_specs=P("tm", None, None, "chan"),
        check_vma=False,
    )
```

```python
import math

import jax
import jax.numpy as jnp
from jax import lax
from jax.experimental import pallas as pl
from jax.experimental.pallas import tpu as pltpu
from jax.sharding import PartitionSpec as P

ITERS = 10
EPS = 1e-06
FB = 16


def params(mebibytes):
    return pltpu.CompilerParams(vmem_limit_bytes=mebibytes * 1024 * 1024)


def bit_orders(n_tm):
    bits = [1 << i for i in range(n_tm.bit_length() - 1)]
    return bits, bits[::-1]


def target_order(n_tm, bits):
    return sorted(range(n_tm), key=lambda r: [int(bool(r & b)) for b in bits])


def transform_kernel(orders, n_slots, start, units, tab_ref, vis_ref, *refs):
    outs, (held_ref, wide_ref, full_ref, sems) = refs[:-4], refs[-4:]
    _, n_dev_time, _, width = held_ref.shape
    n_tm = len(orders[0])
    n_time = n_dev_time * n_tm
    n_rows = n_tm * n_slots
    half = width // 2
    depth = n_dev_time * FB
    scale = 1.0 / math.sqrt(n_time)

    def copies(unit):
        size = n_dev_time // 2
        for piece in range(2):
            times = pl.ds(piece * size, size)
            source = vis_ref.at[times, pl.ds(start + unit * 2 * FB, 2 * FB), :]
            target = held_ref.at[unit, times]
            yield pltpu.make_async_copy(source, target, sems.at[unit, piece])

    for unit in range(units):
        for copy in copies(unit):
            copy.start()

    times = lax.broadcasted_iota(jnp.int32, (n_dev_time, depth), 0)
    lanes = lax.broadcasted_iota(jnp.int32, (n_dev_time, depth), 1)
    spread = jnp.where(lax.div(lanes, FB) == times, 1.0, 0.0).astype(jnp.bfloat16)
    wide_ref[...] = jnp.dot(tab_ref[...], spread, preferred_element_type=jnp.float32)
    me = lax.axis_index("tm")
    sub = lax.broadcasted_iota(jnp.int32, (FB, depth), 0)
    same = lax.rem(lax.broadcasted_iota(jnp.int32, (FB, depth), 1), FB) == sub
    for r in range(n_tm):
        for j in range(n_slots):
            for which in range(2):
                mode = which * n_rows + (me ^ r) * n_slots + j
                wide = jnp.broadcast_to(wide_ref[pl.ds(mode, 1), :], (FB, depth))
                at = (which * n_rows + r * n_slots + j) * FB
                full_ref[at : at + FB, :] = jnp.where(same, wide, 0.0).astype(jnp.bfloat16)

    for group in range(2 * units):
        part, place_f = group // units, group % units * FB
        order, keep, send = orders[part], outs[2 * part], outs[2 * part + 1]
        n_keep = keep.shape[0]
        if group % 2 == 0:
            for copy in copies(group // 2):
                copy.wait()
        first = group % 2 * FB
        data = held_ref[group // 2, :, first : first + FB, :].reshape(depth, width)
        prod = jnp.dot(full_ref[...], data, preferred_element_type=jnp.float32)
        cos_part, sin_part = prod[: n_rows * FB], prod[n_rows * FB :]
        real = (cos_part[:, :half] + sin_part[:, half:]) * scale
        imag = (cos_part[:, half:] - sin_part[:, :half]) * scale
        for place, r in enumerate(order):
            out = keep if place < n_keep else send
            for j in range(n_slots):
                at = (r * n_slots + j) * FB
                out[place % n_keep, j, place_f : place_f + FB, :half] = real[at : at + FB]
                out[place % n_keep, j, place_f : place_f + FB, half:] = imag[at : at + FB]


def transform(tab, vis, start, units, orders, n_slots):
    n_time, _, width = vis.shape
    n_tm = len(orders[0])
    depth = n_time * FB
    n_rows = n_tm * n_slots
    piece = jax.ShapeDtypeStruct((n_tm // 2, n_slots, units * FB, width), jnp.float32)

    def body(*refs):
        transform_kernel(orders, n_slots, start, units, *refs)

    return pl.pallas_call(
        body,
        in_specs=[
            pl.BlockSpec(memory_space=pltpu.VMEM),
            pl.BlockSpec(memory_space=pltpu.HBM),
        ],
        out_specs=[pl.BlockSpec(memory_space=pltpu.VMEM)] * 4,
        out_shape=[piece] * 4,
        scratch_shapes=[
            pltpu.VMEM((units, n_time, 2 * FB, width), jnp.bfloat16),
            pltpu.VMEM((2 * n_rows, depth), jnp.float32),
            pltpu.VMEM((2 * n_rows * FB, depth), jnp.bfloat16),
            pltpu.SemaphoreType.DMA((units, 2)),
        ],
        compiler_params=params(50),
        cost_estimate=pl.CostEstimate(
            flops=2 * 2 * n_rows * FB * depth * width * 2 * units,
            bytes_accessed=n_time * 2 * FB * units * width * 2 + 4 * 4 * piece.size,
            transcendentals=0,
        ),
        name="transform",
    )(tab, vis)


def position():
    me = lax.axis_index("chan")
    return lax.div(me, 2), lax.rem(me, 2)


def put(dst, keep_ref, send_ref, at, value):
    z, core = position()

    @pl.when(core == dst % 2)
    def _():
        keep_ref[(dst // 2) ^ z, *at] = value

    @pl.when(core != dst % 2)
    def _():
        send_ref[(dst // 2) ^ z, *at] = value


def exchange_chan(keep, send, n_chan):
    def swap(value, bits):
        return lax.ppermute(value, "chan", [(i, i ^ bits) for i in range(n_chan)])

    got = swap(send, 1)
    pairs = [(k, jnp.stack([keep[k], got[k]])) for k in reversed(range(1, n_chan // 2))]
    far = {k: swap(pair, 2 * k) for k, pair in pairs}
    return [keep, got, *(far[k] for k in range(1, n_chan // 2))]


def arrivals(refs):
    z, core = position()
    keep, got, far = refs[0], refs[1], refs[2:]
    yield 2 * z + core, lambda *at: keep[0, *at]
    yield 2 * z + 1 - core, lambda *at: got[0, *at]
    for k, ref in enumerate(far, 1):
        yield 2 * (z ^ k) + core, lambda *at, ref=ref: ref[0, *at]
        yield 2 * (z ^ k) + 1 - core, lambda *at, ref=ref: ref[1, *at]


def project_kernel(halves, unit, units, n_terms, *refs):
    beam_ref, keep_ref, send_ref, vis_ref, flat_ref = refs[n_terms], *refs[-4:]
    _, double, width = beam_ref.shape
    half, degrees = double // 2, width // FB
    n_slots = refs[0].shape[1]
    pairs = n_slots // 2
    pieces = [(i, s, h) for i in range(pairs) for s in range(2) for h in range(2)]

    for at, (i, s, h) in enumerate(pieces):
        terms, place = halves[h]
        total = None
        for term in terms:
            value = refs[term][0, 2 * i + s, place : place + FB, :]
            total = value if total is None else total + value
        real = total[:, :half].astype(jnp.bfloat16)
        imag = total[:, half:].astype(jnp.bfloat16)
        vis_ref[at, :FB, :half] = real
        vis_ref[at, FB:, :half] = imag
        vis_ref[at, :FB, half:] = -imag
        vis_ref[at, FB:, half:] = real

    per_pair = 2 * keep_ref.shape[0] // pairs
    rows = keep_ref.shape[1]
    per_tile = 128 // degrees
    sub = lax.broadcasted_iota(jnp.int32, (8, 128), 0)
    for at, (i, s, h) in enumerate(pieces):
        turned = beam_ref[((2 * i + s) * units + unit) * 2 + h]
        prod = jnp.dot(vis_ref[at], turned, preferred_element_type=jnp.float32)
        for p in range(2):
            for g in range(FB // 8):
                own = prod[p * FB + g * 8 : p * FB + g * 8 + 8, g * 8 * degrees : (g + 1) * 8 * degrees]
                pick = own[:, :128]
                for v in range(1, 8 // per_tile):
                    pick = jnp.where(sub // per_tile == v, own[:, v * 128 : (v + 1) * 128], pick)
                if per_tile == 2:
                    pick = jnp.where(sub % 2 == 0, pick, pltpu.roll(pick, degrees, 1))
                row = s * 4 * FB + p * 2 * FB + h * FB + g * 8
                flat_ref[row : row + 8, :] = pick
        if s == 1 and h == 1:
            coeffs = flat_ref[...].T[:degrees]
            for b in range(per_pair):
                put(i * per_pair + b, keep_ref, send_ref, (), coeffs[b * rows : (b + 1) * rows])


def load(beam, start, size, depth=6):
    n_slots, _, _, degrees, half = beam.shape
    per_slot = size // FB
    n_pieces = n_slots * per_slot
    depth = min(depth, n_pieces)

    def body(beam_ref, out_ref, held_ref, sems):
        def copy(at):
            f = pl.multiple_of(start + lax.rem(at, per_slot) * FB, FB)
            slot = lax.rem(at, depth)
            return pltpu.make_async_copy(
                beam_ref.at[lax.div(at, per_slot), pl.ds(f, FB)], held_ref.at[slot], sems.at[slot]
            )

        def step(at, carry):
            copy(at).wait()
            for p in range(2):
                block = held_ref[lax.rem(at, depth), :, p].reshape(FB * degrees, half)
                out_ref[at, p * half : (p + 1) * half, :] = block.T

            @pl.when(at + depth < n_pieces)
            def _():
                copy(at + depth).start()

            return carry

        for at in range(depth):
            copy(at).start()
        lax.fori_loop(0, n_pieces, step, 0)

    return pl.pallas_call(
        body,
        in_specs=[pl.BlockSpec(memory_space=pltpu.HBM)],
        out_specs=pl.BlockSpec(memory_space=pltpu.VMEM),
        out_shape=jax.ShapeDtypeStruct((n_pieces, 2 * half, FB * degrees), beam.dtype),
        scratch_shapes=[
            pltpu.VMEM((depth, FB, 2, degrees, half), beam.dtype),
            pltpu.SemaphoreType.DMA((depth,)),
        ],
        compiler_params=params(10),
        cost_estimate=pl.CostEstimate(
            flops=0, bytes_accessed=4 * n_pieces * FB * 2 * degrees * half, transcendentals=0
        ),
        name="load",
    )(beam)


def project(parts, beam, unit, units, place, n_chan, n_units, buffers):
    _, double, width = beam.shape
    half, degrees = double // 2, width // FB
    n_slots = parts[0][0].shape[1]
    pairs = n_slots // 2
    rows = pairs * degrees // n_chan
    terms, halves = [], []
    for h in range(2):
        part, at = (2 * unit + h) // units, (2 * unit + h) % units * FB
        if not halves or part != (2 * unit) // units:
            terms += parts[part]
        halves.append((range(len(terms) - len(parts[part]), len(terms)), at))
    n_terms = len(terms)
    n_pieces = n_slots * 2

    def body(*refs):
        project_kernel(halves, unit, units, n_terms, *refs)

    term_spec = pl.BlockSpec((1, n_slots, units * FB, 2 * half), lambda i: (0, 0, 0, 0))
    return pl.pallas_call(
        body,
        grid=(1,),
        in_specs=[term_spec] * n_terms
        + [pl.BlockSpec(memory_space=pltpu.VMEM)]
        + [pl.BlockSpec(memory_space=pl.ANY)] * len(buffers),
        out_specs=[pl.BlockSpec((n_chan // 2, None, rows, 8 * FB), lambda i: (0, place, 0, 0))] * 2,
        out_shape=[jax.ShapeDtypeStruct((n_chan // 2, n_units, rows, 8 * FB), jnp.float32)] * 2,
        scratch_shapes=[
            pltpu.VMEM((n_pieces, 2 * FB, 2 * half), jnp.bfloat16),
            pltpu.VMEM((8 * FB, 128), jnp.float32),
        ],
        input_output_aliases={n_terms + 1 + i: i for i in range(len(buffers))},
        compiler_params=params(6),
        cost_estimate=pl.CostEstimate(
            flops=2 * n_slots * 2 * FB * 2 * degrees * half * 256,
            bytes_accessed=n_slots * 2 * FB * 2 * degrees * half * 2,
            transcendentals=0,
        ),
        name="project",
    )(*terms, beam, *buffers)


def split_kernel(cov_ref, high_ref, low_ref):
    cov = cov_ref[...]
    high = cov.astype(jnp.bfloat16)
    high_ref[...] = high
    low_ref[...] = (cov - high.astype(jnp.float32)).astype(jnp.bfloat16)


def split(cov, n_blocks=4):
    rows, cols = cov.shape
    spec = pl.BlockSpec((rows // n_blocks, cols), lambda i: (i, 0))
    half = jax.ShapeDtypeStruct(cov.shape, jnp.bfloat16)
    return pl.pallas_call(
        split_kernel,
        grid=(n_blocks,),
        in_specs=[spec],
        out_specs=[spec, spec],
        out_shape=[half, half],
        compiler_params=params(10),
        cost_estimate=pl.CostEstimate(
            flops=4 * cov.size, bytes_accessed=8 * cov.size, transcendentals=0
        ),
        name="split",
    )(cov)


def fill_kernel(n_in, *refs):
    high_ref, low_ref, flags_ref, keep_ref, send_ref, data_ref = refs[n_in:]
    n_src, n_rows, f_dev = data_ref.shape
    _, n_units, rows, lanes = refs[0].shape
    groups = lanes // (2 * FB)
    for src, take in arrivals(refs[:n_in]):
        for u in range(n_units):
            piece = take(u)
            for g in range(groups):
                data_ref[src, g * rows : (g + 1) * rows, u * 2 * FB : (u + 1) * 2 * FB] = piece[
                    :, g * 2 * FB : (g + 1) * 2 * FB
                ]
    data = jnp.concatenate([data_ref[src] for src in range(n_src)], axis=1)
    good = 1.0 - flags_ref[...].astype(jnp.float32)

    def total(values):
        return jnp.sum(values, axis=1, keepdims=True)

    def covered(vec):
        top = vec.astype(jnp.bfloat16)
        rest = (vec - top.astype(jnp.float32)).astype(jnp.bfloat16)
        both = jnp.concatenate([top, rest], axis=0)
        wide = jnp.dot(both, high_ref[...], preferred_element_type=jnp.float32)
        thin = jnp.dot(top, low_ref[...], preferred_element_type=jnp.float32)
        return wide[:n_rows] + (wide[n_rows:] + thin)

    resid = good * data
    direc = resid
    norm_now = total(resid * resid)
    signal = jnp.zeros_like(resid)

    def advance(step, carry):
        signal, resid, direc, norm_now = carry
        image = covered(direc)
        shifted = direc + good * image
        alpha = norm_now / (total(direc * shifted) + EPS)
        signal = signal + alpha * image
        resid = resid - alpha * shifted
        norm_next = total(resid * resid)
        direc = resid + norm_next / (norm_now + EPS) * direc
        return signal, resid, direc, norm_next

    signal, resid, direc, norm_now = lax.fori_loop(
        0, ITERS, advance, (signal, resid, direc, norm_now)
    )
    data = jnp.concatenate([data_ref[src] for src in range(n_src)], axis=1)
    filled = good * data + (1.0 - good) * signal
    for dst in range(n_src):
        put(dst, keep_ref, send_ref, (), filled[:, dst * f_dev : (dst + 1) * f_dev])


def fill(pieces, high, low, flags, f_dev):
    n_hi, _, rows, lanes = pieces[0].shape
    n_rows = lanes // (2 * FB) * rows
    n_freq = high.shape[0]

    def body(*refs):
        fill_kernel(len(pieces), *refs)

    return pl.pallas_call(
        body,
        in_specs=[pl.BlockSpec(memory_space=pltpu.VMEM)] * (len(pieces) + 3),
        out_specs=[pl.BlockSpec(memory_space=pltpu.VMEM)] * 2,
        out_shape=[jax.ShapeDtypeStruct((n_hi, n_rows, f_dev), jnp.float32)] * 2,
        scratch_shapes=[pltpu.VMEM((2 * n_hi, n_rows, f_dev), jnp.float32)],
        compiler_params=params(8),
        cost_estimate=pl.CostEstimate(
            flops=2 * ITERS * 3 * n_rows * n_freq * n_freq,
            bytes_accessed=4 * n_freq * n_freq,
            transcendentals=0,
        ),
        name="fill",
    )(*pieces, high, low, flags)


def gather_kernel(n_in, *refs):
    out_ref, stage_ref = refs[n_in:]
    n_src, n_rows, _ = stage_ref.shape
    for src, take in arrivals(refs[:n_in]):
        stage_ref[src] = take()
    pairs = out_ref.shape[0] // 2
    per_pair = n_src // pairs
    rows = n_rows // 4
    for src in range(n_src):
        i, block = src // per_pair, src % per_pair
        for g in range(4):
            out_ref[2 * i + g // 2, g % 2, block * rows : (block + 1) * rows, :] = stage_ref[
                src, g * rows : (g + 1) * rows, :
            ]


def gather(pieces, shape):
    def body(*refs):
        gather_kernel(len(pieces), *refs)

    n_hi, n_rows, f_dev = pieces[0].shape
    return pl.pallas_call(
        body,
        in_specs=[pl.BlockSpec(memory_space=pltpu.VMEM)] * len(pieces),
        out_specs=pl.BlockSpec(memory_space=pltpu.VMEM),
        out_shape=jax.ShapeDtypeStruct(shape, jnp.float32),
        scratch_shapes=[pltpu.VMEM((2 * n_hi, n_rows, f_dev), jnp.float32)],
        compiler_params=params(4),
        name="gather",
    )(*pieces)


def make_tables(m_modes, n_tm, t_dev):
    n_time = t_dev * n_tm
    times = lax.axis_index("tm") * t_dev + jnp.arange(t_dev, dtype=jnp.int32)
    index = m_modes[:, None] * times[None, :] % n_time
    angle = 2.0 * math.pi / n_time * index.astype(jnp.float32)
    return jnp.concatenate([jnp.cos(angle), jnp.sin(angle)], axis=0).astype(jnp.bfloat16)


def exchange(send, bit, n_tm):
    return lax.ppermute(send, "tm", [(i, i ^ bit) for i in range(n_tm)])


def make_chunks(n_units):
    sizes = [2, 2] if n_units == 4 else [1] * n_units
    return [(sum(sizes[:i]), size) for i, size in enumerate(sizes)]


def per_device(vis, beam, fg_cov, flags, m_modes):
    t_dev, f_dev, _ = vis.shape
    n_tm = lax.axis_size("tm")
    n_chan = lax.axis_size("chan")
    n_slots = m_modes.shape[0] // n_tm
    degrees = beam.shape[3]
    orders = bit_orders(n_tm)
    targets = [target_order(n_tm, bits) for bits in orders]
    n_units = f_dev // (2 * FB)
    chunks = make_chunks(n_units)
    n_chunks = len(chunks)
    n_steps = len(orders[0])
    high, low = split(fg_cov)

    parts = [None] * n_chunks
    sends = [None] * n_chunks

    def begin(chunk, tab):
        first, units = chunks[chunk]
        outs = transform(tab, vis, first * 2 * FB, units, targets, n_slots)
        parts[chunk] = [[outs[0]], [outs[2]]]
        sends[chunk] = [outs[1], outs[3]]

    def go_on(chunk, place):
        for h, bits in enumerate(orders):
            got = exchange(sends[chunk][h], bits[place], n_tm)
            parts[chunk][h].append(got)
            size = got.shape[0] // 2
            sends[chunk][h] = sum(term[size : 2 * size] for term in parts[chunk][h])

    tab = make_tables(m_modes, n_tm, t_dev)
    for chunk in range(n_chunks):
        begin(chunk, tab)
    blocks = []
    for chunk, (first, units) in enumerate(chunks):
        before = max(chunk - 1, 0)
        source = sends[-1][0] if chunk == 0 else sends[before][0]
        source, beam = lax.optimization_barrier((source, beam))
        if chunk == 0:
            sends[-1][0] = source
        else:
            sends[before][0] = source
        block = load(beam, first * 2 * FB, units * 2 * FB)
        keeps = [group[0] for group in parts[chunk]]
        *keeps, block = lax.optimization_barrier((*keeps, block))
        parts[chunk] = [[keep] for keep in keeps]
        blocks.append(block)
        go_on(chunk, 0)
    sends[-1][0], high, low = lax.optimization_barrier((sends[-1][0], high, low))
    for place in range(1, n_steps):
        for chunk in range(n_chunks):
            go_on(chunk, place)

    coeffs = []
    for chunk, (first, units) in enumerate(chunks):
        for unit in reversed(range(units)):
            coeffs = project(
                parts[chunk], blocks[chunk], unit, units, first + unit, n_chan, n_units, coeffs
            )
    pieces = exchange_chan(*coeffs, n_chan)
    whole = fill(pieces, high, low, flags[None, :], f_dev)
    back = exchange_chan(*whole, n_chan)
    return gather(back, (n_slots, 2, degrees, f_dev))


def solution(mesh):
    placed = (P("tm", "chan", None), P("tm", "chan", None, None, None), P(), P(), P())
    return jax.shard_map(
        per_device,
        mesh=mesh,
        in_specs=placed,
        out_specs=P("tm", None, None, "chan"),
        check_vma=False,
    )
```

```python
import math

import jax
import jax.numpy as jnp
from jax import lax
from jax.experimental import pallas as pl
from jax.experimental.pallas import tpu as pltpu
from jax.sharding import PartitionSpec as P

ITERS = 10
EPS = 1e-06
FB = 16
PIECES = 8


def params(mebibytes):
    return pltpu.CompilerParams(vmem_limit_bytes=mebibytes * 1024 * 1024)


def bit_orders(n_tm):
    bits = [1 << i for i in range(n_tm.bit_length() - 1)]
    return bits, bits[::-1]


def target_order(n_tm, bits):
    return sorted(range(n_tm), key=lambda r: [int(bool(r & b)) for b in bits])


def transform_kernel(orders, n_slots, start, units, tab_ref, vis_ref, *refs):
    outs, (held_ref, wide_ref, full_ref, sems) = refs[:-4], refs[-4:]
    _, n_dev_time, _, width = held_ref.shape
    n_tm = len(orders[0])
    n_time = n_dev_time * n_tm
    n_rows = n_tm * n_slots
    half = width // 2
    depth = n_dev_time * FB
    scale = 1.0 / math.sqrt(n_time)

    def copies(unit):
        size = n_dev_time // PIECES
        for piece in range(PIECES):
            times = pl.ds(piece * size, size)
            source = vis_ref.at[times, pl.ds(start + unit * 2 * FB, 2 * FB), :]
            target = held_ref.at[unit, times]
            yield pltpu.make_async_copy(source, target, sems.at[unit, piece])

    for unit in range(units):
        for copy in copies(unit):
            copy.start()

    times = lax.broadcasted_iota(jnp.int32, (n_dev_time, depth), 0)
    lanes = lax.broadcasted_iota(jnp.int32, (n_dev_time, depth), 1)
    spread = jnp.where(lax.div(lanes, FB) == times, 1.0, 0.0).astype(jnp.bfloat16)
    wide_ref[...] = jnp.dot(tab_ref[...], spread, preferred_element_type=jnp.float32)
    me = lax.axis_index("tm")
    sub = lax.broadcasted_iota(jnp.int32, (FB, depth), 0)
    same = lax.rem(lax.broadcasted_iota(jnp.int32, (FB, depth), 1), FB) == sub
    for r in range(n_tm):
        for j in range(n_slots):
            for which in range(2):
                mode = which * n_rows + (me ^ r) * n_slots + j
                wide = jnp.broadcast_to(wide_ref[pl.ds(mode, 1), :], (FB, depth))
                at = (which * n_rows + r * n_slots + j) * FB
                full_ref[at : at + FB, :] = jnp.where(same, wide, 0.0).astype(jnp.bfloat16)

    for group in range(2 * units):
        part, place_f = group // units, group % units * FB
        order, keep, send = orders[part], outs[2 * part], outs[2 * part + 1]
        n_keep = keep.shape[0]
        if group % 2 == 0:
            for copy in copies(group // 2):
                copy.wait()
        first = group % 2 * FB
        data = held_ref[group // 2, :, first : first + FB, :].reshape(depth, width)
        prod = jnp.dot(full_ref[...], data, preferred_element_type=jnp.float32)
        cos_part, sin_part = prod[: n_rows * FB], prod[n_rows * FB :]
        real = (cos_part[:, :half] + sin_part[:, half:]) * scale
        imag = (cos_part[:, half:] - sin_part[:, :half]) * scale
        for place, r in enumerate(order):
            out = keep if place < n_keep else send
            for j in range(n_slots):
                at = (r * n_slots + j) * FB
                out[place % n_keep, j, place_f : place_f + FB, :half] = real[at : at + FB]
                out[place % n_keep, j, place_f : place_f + FB, half:] = imag[at : at + FB]


def transform(tab, vis, start, units, orders, n_slots):
    n_time, _, width = vis.shape
    n_tm = len(orders[0])
    depth = n_time * FB
    n_rows = n_tm * n_slots
    piece = jax.ShapeDtypeStruct((n_tm // 2, n_slots, units * FB, width), jnp.float32)

    def body(*refs):
        transform_kernel(orders, n_slots, start, units, *refs)

    return pl.pallas_call(
        body,
        in_specs=[
            pl.BlockSpec(memory_space=pltpu.VMEM),
            pl.BlockSpec(memory_space=pltpu.HBM),
        ],
        out_specs=[pl.BlockSpec(memory_space=pltpu.VMEM)] * 4,
        out_shape=[piece] * 4,
        scratch_shapes=[
            pltpu.VMEM((units, n_time, 2 * FB, width), jnp.bfloat16),
            pltpu.VMEM((2 * n_rows, depth), jnp.float32),
            pltpu.VMEM((2 * n_rows * FB, depth), jnp.bfloat16),
            pltpu.SemaphoreType.DMA((units, PIECES)),
        ],
        compiler_params=params(50),
        cost_estimate=pl.CostEstimate(
            flops=2 * 2 * n_rows * FB * depth * width * 2 * units,
            bytes_accessed=n_time * 2 * FB * units * width * 2 + 4 * 4 * piece.size,
            transcendentals=0,
        ),
        name="transform",
    )(tab, vis)


def position():
    me = lax.axis_index("chan")
    return lax.div(me, 2), lax.rem(me, 2)


def put(dst, keep_ref, send_ref, at, value):
    z, core = position()

    @pl.when(core == dst % 2)
    def _():
        keep_ref[(dst // 2) ^ z, *at] = value

    @pl.when(core != dst % 2)
    def _():
        send_ref[(dst // 2) ^ z, *at] = value


def exchange_chan(keep, send, n_chan):
    def swap(value, bits):
        return lax.ppermute(value, "chan", [(i, i ^ bits) for i in range(n_chan)])

    got = swap(send, 1)
    pairs = [(k, jnp.stack([keep[k], got[k]])) for k in reversed(range(1, n_chan // 2))]
    far = {k: swap(pair, 2 * k) for k, pair in pairs}
    return [keep, got, *(far[k] for k in range(1, n_chan // 2))]


def arrivals(refs):
    z, core = position()
    keep, got, far = refs[0], refs[1], refs[2:]
    yield 2 * z + core, lambda *at: keep[0, *at]
    yield 2 * z + 1 - core, lambda *at: got[0, *at]
    for k, ref in enumerate(far, 1):
        yield 2 * (z ^ k) + core, lambda *at, ref=ref: ref[0, *at]
        yield 2 * (z ^ k) + 1 - core, lambda *at, ref=ref: ref[1, *at]


def project_kernel(n_terms, units, *refs):
    terms = refs[: 2 * n_terms]
    beam_ref, keep_ref, send_ref, vis_ref, flat_ref = refs[2 * n_terms], *refs[-4:]
    _, double, width = beam_ref.shape
    half, degrees = double // 2, width // FB
    n_slots = terms[0].shape[1]
    pairs = n_slots // 2
    pieces = [(u, i, s, h) for u in range(units) for i in range(pairs) for s in range(2) for h in range(2)]

    for at, (u, i, s, h) in enumerate(pieces):
        part, place = (2 * u + h) // units, (2 * u + h) % units * FB
        total = None
        for term in terms[part * n_terms : (part + 1) * n_terms]:
            value = term[0, 2 * i + s, place : place + FB, :]
            total = value if total is None else total + value
        real = total[:, :half].astype(jnp.bfloat16)
        imag = total[:, half:].astype(jnp.bfloat16)
        vis_ref[at, :FB, :half] = real
        vis_ref[at, FB:, :half] = imag
        vis_ref[at, :FB, half:] = -imag
        vis_ref[at, FB:, half:] = real

    per_pair = 2 * keep_ref.shape[0] // pairs
    rows = keep_ref.shape[2]
    per_tile = 128 // degrees
    sub = lax.broadcasted_iota(jnp.int32, (8, 128), 0)
    for at, (u, i, s, h) in enumerate(pieces):
        turned = beam_ref[(2 * i + s) * 2 * units + 2 * u + h]
        prod = jnp.dot(vis_ref[at], turned, preferred_element_type=jnp.float32)
        for p in range(2):
            for g in range(FB // 8):
                own = prod[p * FB + g * 8 : p * FB + g * 8 + 8, g * 8 * degrees : (g + 1) * 8 * degrees]
                pick = own[:, :128]
                for v in range(1, 8 // per_tile):
                    pick = jnp.where(sub // per_tile == v, own[:, v * 128 : (v + 1) * 128], pick)
                if per_tile == 2:
                    pick = jnp.where(sub % 2 == 0, pick, pltpu.roll(pick, degrees, 1))
                row = s * 4 * FB + p * 2 * FB + h * FB + g * 8
                flat_ref[row : row + 8, :] = pick
        if s == 1 and h == 1:
            coeffs = flat_ref[...].T[:degrees]
            for b in range(per_pair):
                put(i * per_pair + b, keep_ref, send_ref, (u,), coeffs[b * rows : (b + 1) * rows])


def load(beam, start, size, depth=6):
    n_slots, _, _, degrees, half = beam.shape
    per_slot = size // FB
    n_pieces = n_slots * per_slot
    depth = min(depth, n_pieces)

    def body(beam_ref, out_ref, held_ref, sems):
        def copy(at):
            f = pl.multiple_of(start + lax.rem(at, per_slot) * FB, FB)
            slot = lax.rem(at, depth)
            return pltpu.make_async_copy(
                beam_ref.at[lax.div(at, per_slot), pl.ds(f, FB)], held_ref.at[slot], sems.at[slot]
            )

        def step(at, carry):
            copy(at).wait()
            for p in range(2):
                block = held_ref[lax.rem(at, depth), :, p].reshape(FB * degrees, half)
                out_ref[at, p * half : (p + 1) * half, :] = block.T

            @pl.when(at + depth < n_pieces)
            def _():
                copy(at + depth).start()

            return carry

        for at in range(depth):
            copy(at).start()
        lax.fori_loop(0, n_pieces, step, 0)

    return pl.pallas_call(
        body,
        in_specs=[pl.BlockSpec(memory_space=pltpu.HBM)],
        out_specs=pl.BlockSpec(memory_space=pltpu.VMEM),
        out_shape=jax.ShapeDtypeStruct((n_pieces, 2 * half, FB * degrees), beam.dtype),
        scratch_shapes=[
            pltpu.VMEM((depth, FB, 2, degrees, half), beam.dtype),
            pltpu.SemaphoreType.DMA((depth,)),
        ],
        compiler_params=params(14),
        cost_estimate=pl.CostEstimate(
            flops=0, bytes_accessed=4 * n_pieces * FB * 2 * degrees * half, transcendentals=0
        ),
        name="load",
    )(beam)


def project(parts, beam, start, units, n_chan, n_units, buffers):
    _, double, width = beam.shape
    half, degrees = double // 2, width // FB
    n_slots = parts[0][0].shape[1]
    n_terms = len(parts[0])
    pairs = n_slots // 2
    rows = pairs * degrees // n_chan
    terms = [term for group in parts for term in group]
    place = start // (2 * FB) // units
    n_pieces = units * n_slots * 2

    def body(*refs):
        project_kernel(n_terms, units, *refs)

    term_spec = pl.BlockSpec((1, n_slots, units * FB, 2 * half), lambda i: (0, 0, 0, 0))
    return pl.pallas_call(
        body,
        grid=(1,),
        in_specs=[term_spec] * len(terms)
        + [pl.BlockSpec(memory_space=pltpu.VMEM)]
        + [pl.BlockSpec(memory_space=pl.ANY)] * len(buffers),
        out_specs=[pl.BlockSpec((n_chan // 2, units, rows, 8 * FB), lambda i: (0, place, 0, 0))] * 2,
        out_shape=[jax.ShapeDtypeStruct((n_chan // 2, n_units, rows, 8 * FB), jnp.float32)] * 2,
        scratch_shapes=[
            pltpu.VMEM((n_pieces, 2 * FB, 2 * half), jnp.bfloat16),
            pltpu.VMEM((8 * FB, 128), jnp.float32),
        ],
        input_output_aliases={len(terms) + 1 + i: i for i in range(len(buffers))},
        compiler_params=params(14),
        cost_estimate=pl.CostEstimate(
            flops=2 * n_slots * 2 * FB * units * 2 * degrees * half * 256,
            bytes_accessed=n_slots * 2 * FB * units * 2 * degrees * half * 2,
            transcendentals=0,
        ),
        name="project",
    )(*terms, beam, *buffers)


def split_kernel(cov_ref, high_ref, low_ref):
    cov = cov_ref[...]
    high = cov.astype(jnp.bfloat16)
    high_ref[...] = high
    low_ref[...] = (cov - high.astype(jnp.float32)).astype(jnp.bfloat16)


def split(cov, n_blocks=4):
    rows, cols = cov.shape
    spec = pl.BlockSpec((rows // n_blocks, cols), lambda i: (i, 0))
    half = jax.ShapeDtypeStruct(cov.shape, jnp.bfloat16)
    return pl.pallas_call(
        split_kernel,
        grid=(n_blocks,),
        in_specs=[spec],
        out_specs=[spec, spec],
        out_shape=[half, half],
        compiler_params=params(14),
        cost_estimate=pl.CostEstimate(
            flops=4 * cov.size, bytes_accessed=8 * cov.size, transcendentals=0
        ),
        name="split",
    )(cov)


def fill_kernel(n_in, *refs):
    high_ref, low_ref, flags_ref, keep_ref, send_ref, data_ref = refs[n_in:]
    n_src, n_rows, f_dev = data_ref.shape
    _, n_units, rows, lanes = refs[0].shape
    groups = lanes // (2 * FB)
    for src, take in arrivals(refs[:n_in]):
        for u in range(n_units):
            piece = take(u)
            for g in range(groups):
                data_ref[src, g * rows : (g + 1) * rows, u * 2 * FB : (u + 1) * 2 * FB] = piece[
                    :, g * 2 * FB : (g + 1) * 2 * FB
                ]
    data = jnp.concatenate([data_ref[src] for src in range(n_src)], axis=1)
    good = 1.0 - flags_ref[...].astype(jnp.float32)

    def total(values):
        return jnp.sum(values, axis=1, keepdims=True)

    def covered(vec):
        top = vec.astype(jnp.bfloat16)
        rest = (vec - top.astype(jnp.float32)).astype(jnp.bfloat16)
        both = jnp.concatenate([top, rest], axis=0)
        wide = jnp.dot(both, high_ref[...], preferred_element_type=jnp.float32)
        thin = jnp.dot(top, low_ref[...], preferred_element_type=jnp.float32)
        return wide[:n_rows] + (wide[n_rows:] + thin)

    resid = good * data
    direc = resid
    norm_now = total(resid * resid)
    signal = jnp.zeros_like(resid)

    def advance(step, carry):
        signal, resid, direc, norm_now = carry
        image = covered(direc)
        shifted = direc + good * image
        alpha = norm_now / (total(direc * shifted) + EPS)
        signal = signal + alpha * image
        resid = resid - alpha * shifted
        norm_next = total(resid * resid)
        direc = resid + norm_next / (norm_now + EPS) * direc
        return signal, resid, direc, norm_next

    signal, resid, direc, norm_now = lax.fori_loop(
        0, ITERS, advance, (signal, resid, direc, norm_now), unroll=2
    )
    data = jnp.concatenate([data_ref[src] for src in range(n_src)], axis=1)
    filled = good * data + (1.0 - good) * signal
    for dst in range(n_src):
        put(dst, keep_ref, send_ref, (), filled[:, dst * f_dev : (dst + 1) * f_dev])


def fill(pieces, high, low, flags, f_dev):
    n_hi, _, rows, lanes = pieces[0].shape
    n_rows = lanes // (2 * FB) * rows
    n_freq = high.shape[0]

    def body(*refs):
        fill_kernel(len(pieces), *refs)

    return pl.pallas_call(
        body,
        in_specs=[pl.BlockSpec(memory_space=pltpu.VMEM)] * (len(pieces) + 3),
        out_specs=[pl.BlockSpec(memory_space=pltpu.VMEM)] * 2,
        out_shape=[jax.ShapeDtypeStruct((n_hi, n_rows, f_dev), jnp.float32)] * 2,
        scratch_shapes=[pltpu.VMEM((2 * n_hi, n_rows, f_dev), jnp.float32)],
        compiler_params=params(14),
        cost_estimate=pl.CostEstimate(
            flops=2 * ITERS * 3 * n_rows * n_freq * n_freq,
            bytes_accessed=4 * n_freq * n_freq,
            transcendentals=0,
        ),
        name="fill",
    )(*pieces, high, low, flags)


def gather_kernel(n_in, *refs):
    out_ref, stage_ref = refs[n_in:]
    n_src, n_rows, _ = stage_ref.shape
    for src, take in arrivals(refs[:n_in]):
        stage_ref[src] = take()
    pairs = out_ref.shape[0] // 2
    per_pair = n_src // pairs
    rows = n_rows // 4
    for src in range(n_src):
        i, block = src // per_pair, src % per_pair
        for g in range(4):
            out_ref[2 * i + g // 2, g % 2, block * rows : (block + 1) * rows, :] = stage_ref[
                src, g * rows : (g + 1) * rows, :
            ]


def gather(pieces, shape):
    def body(*refs):
        gather_kernel(len(pieces), *refs)

    n_hi, n_rows, f_dev = pieces[0].shape
    return pl.pallas_call(
        body,
        in_specs=[pl.BlockSpec(memory_space=pltpu.VMEM)] * len(pieces),
        out_specs=pl.BlockSpec(memory_space=pltpu.VMEM),
        out_shape=jax.ShapeDtypeStruct(shape, jnp.float32),
        scratch_shapes=[pltpu.VMEM((2 * n_hi, n_rows, f_dev), jnp.float32)],
        compiler_params=params(14),
        name="gather",
    )(*pieces)


def make_tables(m_modes, n_tm, t_dev):
    n_time = t_dev * n_tm
    times = lax.axis_index("tm") * t_dev + jnp.arange(t_dev, dtype=jnp.int32)
    index = m_modes[:, None] * times[None, :] % n_time
    angle = 2.0 * math.pi / n_time * index.astype(jnp.float32)
    return jnp.concatenate([jnp.cos(angle), jnp.sin(angle)], axis=0).astype(jnp.bfloat16)


def exchange(send, bit, n_tm):
    return lax.ppermute(send, "tm", [(i, i ^ bit) for i in range(n_tm)])


def make_chunks(n_units):
    sizes = [2, 2] if n_units == 4 else [1] * n_units
    return [(sum(sizes[:i]), size) for i, size in enumerate(sizes)]


def per_device(vis, beam, fg_cov, flags, m_modes):
    t_dev, f_dev, _ = vis.shape
    n_tm = lax.axis_size("tm")
    n_chan = lax.axis_size("chan")
    n_slots = m_modes.shape[0] // n_tm
    degrees = beam.shape[3]
    orders = bit_orders(n_tm)
    targets = [target_order(n_tm, bits) for bits in orders]
    n_units = f_dev // (2 * FB)
    chunks = make_chunks(n_units)
    n_chunks = len(chunks)
    n_steps = len(orders[0])
    high, low = split(fg_cov)

    parts = [None] * n_chunks
    sends = [None] * n_chunks

    def begin(chunk, tab):
        first, units = chunks[chunk]
        outs = transform(tab, vis, first * 2 * FB, units, targets, n_slots)
        parts[chunk] = [[outs[0]], [outs[2]]]
        sends[chunk] = [outs[1], outs[3]]

    def go_on(chunk, place):
        for h, bits in enumerate(orders):
            got = exchange(sends[chunk][h], bits[place], n_tm)
            parts[chunk][h].append(got)
            size = got.shape[0] // 2
            sends[chunk][h] = sum(term[size : 2 * size] for term in parts[chunk][h])

    tab = make_tables(m_modes, n_tm, t_dev)
    for chunk in range(n_chunks):
        begin(chunk, tab)
    blocks = []
    for chunk, (first, units) in enumerate(chunks):
        before = max(chunk - 1, 0)
        source = sends[-1][0] if chunk == 0 else sends[before][0]
        source, beam = lax.optimization_barrier((source, beam))
        if chunk == 0:
            sends[-1][0] = source
        else:
            sends[before][0] = source
        block = load(beam, first * 2 * FB, units * 2 * FB)
        keeps = [group[0] for group in parts[chunk]]
        *keeps, block = lax.optimization_barrier((*keeps, block))
        parts[chunk] = [[keep] for keep in keeps]
        blocks.append(block)
        go_on(chunk, 0)
    sends[-1][0], high, low = lax.optimization_barrier((sends[-1][0], high, low))
    for place in range(1, n_steps):
        for chunk in range(n_chunks):
            go_on(chunk, place)

    coeffs = []
    for chunk, (first, units) in enumerate(chunks):
        coeffs = project(
            parts[chunk], blocks[chunk], first * 2 * FB, units, n_chan, n_units, coeffs
        )
    pieces = exchange_chan(*coeffs, n_chan)
    whole = fill(pieces, high, low, flags[None, :], f_dev)
    back = exchange_chan(*whole, n_chan)
    return gather(back, (n_slots, 2, degrees, f_dev))


def solution(mesh):
    placed = (P("tm", "chan", None), P("tm", "chan", None, None, None), P(), P(), P())
    return jax.shard_map(
        per_device,
        mesh=mesh,
        in_specs=placed,
        out_specs=P("tm", None, None, "chan"),
        check_vma=False,
    )
```

```python
import math

import jax
import jax.numpy as jnp
from jax import lax
from jax.experimental import pallas as pl
from jax.experimental.pallas import tpu as pltpu
from jax.sharding import PartitionSpec as P

ITERS = 10
EPS = 1e-06
FB = 16
PIECES = 4


def params(mebibytes):
    return pltpu.CompilerParams(vmem_limit_bytes=mebibytes * 1024 * 1024)


def bit_orders(n_tm):
    bits = [1 << i for i in range(n_tm.bit_length() - 1)]
    return bits, bits[::-1]


def target_order(n_tm, bits):
    return sorted(range(n_tm), key=lambda r: [int(bool(r & b)) for b in bits])


def transform_kernel(orders, n_slots, start, units, tab_ref, vis_ref, *refs):
    outs, (held_ref, wide_ref, full_ref, sems) = refs[:-4], refs[-4:]
    _, n_dev_time, _, width = held_ref.shape
    n_tm = len(orders[0])
    n_time = n_dev_time * n_tm
    n_rows = n_tm * n_slots
    half = width // 2
    depth = n_dev_time * FB
    scale = 1.0 / math.sqrt(n_time)

    def copies(group):
        size = n_dev_time // PIECES
        for piece in range(PIECES):
            times = pl.ds(piece * size, size)
            source = vis_ref.at[times, pl.ds(start + group * FB, FB), :]
            target = held_ref.at[group, times]
            yield pltpu.make_async_copy(source, target, sems.at[group, piece])

    for group in range(2):
        for copy in copies(group):
            copy.start()

    times = lax.broadcasted_iota(jnp.int32, (n_dev_time, depth), 0)
    lanes = lax.broadcasted_iota(jnp.int32, (n_dev_time, depth), 1)
    spread = jnp.where(lax.div(lanes, FB) == times, 1.0, 0.0).astype(jnp.bfloat16)
    wide_ref[...] = jnp.dot(tab_ref[...], spread, preferred_element_type=jnp.float32)
    me = lax.axis_index("tm")
    sub = lax.broadcasted_iota(jnp.int32, (FB, depth), 0)
    same = lax.rem(lax.broadcasted_iota(jnp.int32, (FB, depth), 1), FB) == sub
    for r in range(n_tm):
        for j in range(n_slots):
            for which in range(2):
                mode = which * n_rows + (me ^ r) * n_slots + j
                wide = jnp.broadcast_to(wide_ref[pl.ds(mode, 1), :], (FB, depth))
                at = (which * n_rows + r * n_slots + j) * FB
                full_ref[at : at + FB, :] = jnp.where(same, wide, 0.0).astype(jnp.bfloat16)

    for group in range(2, 2 * units):
        for copy in copies(group):
            copy.start()

    for group in range(2 * units):
        part, place_f = group // units, group % units * FB
        order, keep, send = orders[part], outs[2 * part], outs[2 * part + 1]
        n_keep = keep.shape[0]
        for copy in copies(group):
            copy.wait()
        data = held_ref[group].reshape(depth, width)
        prod = jnp.dot(full_ref[...], data, preferred_element_type=jnp.float32)
        cos_part, sin_part = prod[: n_rows * FB], prod[n_rows * FB :]
        real = (cos_part[:, :half] + sin_part[:, half:]) * scale
        imag = (cos_part[:, half:] - sin_part[:, :half]) * scale
        for place, r in enumerate(order):
            out = keep if place < n_keep else send
            for j in range(n_slots):
                at = (r * n_slots + j) * FB
                out[place % n_keep, j, place_f : place_f + FB, :half] = real[at : at + FB]
                out[place % n_keep, j, place_f : place_f + FB, half:] = imag[at : at + FB]


def transform(tab, vis, start, units, orders, n_slots):
    n_time, _, width = vis.shape
    n_tm = len(orders[0])
    depth = n_time * FB
    n_rows = n_tm * n_slots
    piece = jax.ShapeDtypeStruct((n_tm // 2, n_slots, units * FB, width), jnp.float32)

    def body(*refs):
        transform_kernel(orders, n_slots, start, units, *refs)

    return pl.pallas_call(
        body,
        in_specs=[
            pl.BlockSpec(memory_space=pltpu.VMEM),
            pl.BlockSpec(memory_space=pltpu.HBM),
        ],
        out_specs=[pl.BlockSpec(memory_space=pltpu.VMEM)] * 4,
        out_shape=[piece] * 4,
        scratch_shapes=[
            pltpu.VMEM((2 * units, n_time, FB, width), jnp.bfloat16),
            pltpu.VMEM((2 * n_rows, depth), jnp.float32),
            pltpu.VMEM((2 * n_rows * FB, depth), jnp.bfloat16),
            pltpu.SemaphoreType.DMA((2 * units, PIECES)),
        ],
        compiler_params=params(50),
        cost_estimate=pl.CostEstimate(
            flops=2 * 2 * n_rows * FB * depth * width * 2 * units,
            bytes_accessed=n_time * 2 * FB * units * width * 2 + 4 * 4 * piece.size,
            transcendentals=0,
        ),
        name="transform",
    )(tab, vis)


def position():
    me = lax.axis_index("chan")
    return lax.div(me, 2), lax.rem(me, 2)


def put(dst, keep_ref, send_ref, at, value):
    z, core = position()

    @pl.when(core == dst % 2)
    def _():
        keep_ref[(dst // 2) ^ z, *at] = value

    @pl.when(core != dst % 2)
    def _():
        send_ref[(dst // 2) ^ z, *at] = value


def exchange_chan(keep, send, n_chan):
    def swap(value, bits):
        return lax.ppermute(value, "chan", [(i, i ^ bits) for i in range(n_chan)])

    got = swap(send, 1)
    pairs = [(k, jnp.stack([keep[k], got[k]])) for k in reversed(range(1, n_chan // 2))]
    far = {k: swap(pair, 2 * k) for k, pair in pairs}
    return [keep, got, *(far[k] for k in range(1, n_chan // 2))]


def arrivals(refs):
    z, core = position()
    keep, got, far = refs[0], refs[1], refs[2:]
    yield 2 * z + core, lambda *at: keep[0, *at]
    yield 2 * z + 1 - core, lambda *at: got[0, *at]
    for k, ref in enumerate(far, 1):
        yield 2 * (z ^ k) + core, lambda *at, ref=ref: ref[0, *at]
        yield 2 * (z ^ k) + 1 - core, lambda *at, ref=ref: ref[1, *at]


def project_kernel(n_terms, units, *refs):
    terms = refs[: 2 * n_terms]
    beam_ref, keep_ref, send_ref, vis_ref, flat_ref = refs[2 * n_terms], *refs[-4:]
    _, double, width = beam_ref.shape
    half, degrees = double // 2, width // FB
    n_slots = terms[0].shape[1]
    pairs = n_slots // 2
    pieces = [(u, i, s, h) for u in range(units) for i in range(pairs) for s in range(2) for h in range(2)]

    for at, (u, i, s, h) in enumerate(pieces):
        part, place = (2 * u + h) // units, (2 * u + h) % units * FB
        total = None
        for term in terms[part * n_terms : (part + 1) * n_terms]:
            value = term[0, 2 * i + s, place : place + FB, :]
            total = value if total is None else total + value
        real = total[:, :half].astype(jnp.bfloat16)
        imag = total[:, half:].astype(jnp.bfloat16)
        vis_ref[at, :FB, :half] = real
        vis_ref[at, FB:, :half] = imag
        vis_ref[at, :FB, half:] = -imag
        vis_ref[at, FB:, half:] = real

    per_pair = 2 * keep_ref.shape[0] // pairs
    rows = keep_ref.shape[2]
    per_tile = 128 // degrees
    sub = lax.broadcasted_iota(jnp.int32, (8, 128), 0)
    for at, (u, i, s, h) in enumerate(pieces):
        turned = beam_ref[(2 * i + s) * 2 * units + 2 * u + h]
        prod = jnp.dot(vis_ref[at], turned, preferred_element_type=jnp.float32)
        for p in range(2):
            for g in range(FB // 8):
                own = prod[p * FB + g * 8 : p * FB + g * 8 + 8, g * 8 * degrees : (g + 1) * 8 * degrees]
                pick = own[:, :128]
                for v in range(1, 8 // per_tile):
                    pick = jnp.where(sub // per_tile == v, own[:, v * 128 : (v + 1) * 128], pick)
                if per_tile == 2:
                    pick = jnp.where(sub % 2 == 0, pick, pltpu.roll(pick, degrees, 1))
                row = s * 4 * FB + p * 2 * FB + h * FB + g * 8
                flat_ref[row : row + 8, :] = pick
        if s == 1 and h == 1:
            coeffs = flat_ref[...].T[:degrees]
            for b in range(per_pair):
                put(i * per_pair + b, keep_ref, send_ref, (u,), coeffs[b * rows : (b + 1) * rows])


def load(beam, start, size, depth=6):
    n_slots, _, _, degrees, half = beam.shape
    per_slot = size // FB
    n_pieces = n_slots * per_slot
    depth = min(depth, n_pieces)

    def body(beam_ref, out_ref, held_ref, sems):
        def copy(at):
            f = pl.multiple_of(start + lax.rem(at, per_slot) * FB, FB)
            slot = lax.rem(at, depth)
            return pltpu.make_async_copy(
                beam_ref.at[lax.div(at, per_slot), pl.ds(f, FB)], held_ref.at[slot], sems.at[slot]
            )

        def step(at, carry):
            copy(at).wait()
            for p in range(2):
                block = held_ref[lax.rem(at, depth), :, p].reshape(FB * degrees, half)
                out_ref[at, p * half : (p + 1) * half, :] = block.T

            @pl.when(at + depth < n_pieces)
            def _():
                copy(at + depth).start()

            return carry

        for at in range(depth):
            copy(at).start()
        lax.fori_loop(0, n_pieces, step, 0)

    return pl.pallas_call(
        body,
        in_specs=[pl.BlockSpec(memory_space=pltpu.HBM)],
        out_specs=pl.BlockSpec(memory_space=pltpu.VMEM),
        out_shape=jax.ShapeDtypeStruct((n_pieces, 2 * half, FB * degrees), beam.dtype),
        scratch_shapes=[
            pltpu.VMEM((depth, FB, 2, degrees, half), beam.dtype),
            pltpu.SemaphoreType.DMA((depth,)),
        ],
        compiler_params=params(14),
        cost_estimate=pl.CostEstimate(
            flops=0, bytes_accessed=4 * n_pieces * FB * 2 * degrees * half, transcendentals=0
        ),
        name="load",
    )(beam)


def project(parts, beam, start, units, n_chan, n_units, buffers):
    _, double, width = beam.shape
    half, degrees = double // 2, width // FB
    n_slots = parts[0][0].shape[1]
    n_terms = len(parts[0])
    pairs = n_slots // 2
    rows = pairs * degrees // n_chan
    terms = [term for group in parts for term in group]
    place = start // (2 * FB) // units
    n_pieces = units * n_slots * 2

    def body(*refs):
        project_kernel(n_terms, units, *refs)

    term_spec = pl.BlockSpec((1, n_slots, units * FB, 2 * half), lambda i: (0, 0, 0, 0))
    return pl.pallas_call(
        body,
        grid=(1,),
        in_specs=[term_spec] * len(terms)
        + [pl.BlockSpec(memory_space=pltpu.VMEM)]
        + [pl.BlockSpec(memory_space=pl.ANY)] * len(buffers),
        out_specs=[pl.BlockSpec((n_chan // 2, units, rows, 8 * FB), lambda i: (0, place, 0, 0))] * 2,
        out_shape=[jax.ShapeDtypeStruct((n_chan // 2, n_units, rows, 8 * FB), jnp.float32)] * 2,
        scratch_shapes=[
            pltpu.VMEM((n_pieces, 2 * FB, 2 * half), jnp.bfloat16),
            pltpu.VMEM((8 * FB, 128), jnp.float32),
        ],
        input_output_aliases={len(terms) + 1 + i: i for i in range(len(buffers))},
        compiler_params=params(14),
        cost_estimate=pl.CostEstimate(
            flops=2 * n_slots * 2 * FB * units * 2 * degrees * half * 256,
            bytes_accessed=n_slots * 2 * FB * units * 2 * degrees * half * 2,
            transcendentals=0,
        ),
        name="project",
    )(*terms, beam, *buffers)


def split_kernel(cov_ref, high_ref, low_ref):
    cov = cov_ref[...]
    high = cov.astype(jnp.bfloat16)
    high_ref[...] = high
    low_ref[...] = (cov - high.astype(jnp.float32)).astype(jnp.bfloat16)


def split(cov, n_blocks=4):
    rows, cols = cov.shape
    spec = pl.BlockSpec((rows // n_blocks, cols), lambda i: (i, 0))
    half = jax.ShapeDtypeStruct(cov.shape, jnp.bfloat16)
    return pl.pallas_call(
        split_kernel,
        grid=(n_blocks,),
        in_specs=[spec],
        out_specs=[spec, spec],
        out_shape=[half, half],
        compiler_params=params(14),
        cost_estimate=pl.CostEstimate(
            flops=4 * cov.size, bytes_accessed=8 * cov.size, transcendentals=0
        ),
        name="split",
    )(cov)


def fill_kernel(n_in, *refs):
    high_ref, low_ref, flags_ref, keep_ref, send_ref, data_ref = refs[n_in:]
    n_src, n_rows, f_dev = data_ref.shape
    _, n_units, rows, lanes = refs[0].shape
    groups = lanes // (2 * FB)
    for src, take in arrivals(refs[:n_in]):
        for u in range(n_units):
            piece = take(u)
            for g in range(groups):
                data_ref[src, g * rows : (g + 1) * rows, u * 2 * FB : (u + 1) * 2 * FB] = piece[
                    :, g * 2 * FB : (g + 1) * 2 * FB
                ]
    data = jnp.concatenate([data_ref[src] for src in range(n_src)], axis=1)
    good = 1.0 - flags_ref[...].astype(jnp.float32)

    def total(values):
        return jnp.sum(values, axis=1, keepdims=True)

    def covered(vec):
        top = vec.astype(jnp.bfloat16)
        rest = (vec - top.astype(jnp.float32)).astype(jnp.bfloat16)
        both = jnp.concatenate([top, rest], axis=0)
        wide = jnp.dot(both, high_ref[...], preferred_element_type=jnp.float32)
        thin = jnp.dot(top, low_ref[...], preferred_element_type=jnp.float32)
        return wide[:n_rows] + (wide[n_rows:] + thin)

    resid = good * data
    direc = resid
    norm_now = total(resid * resid)
    signal = jnp.zeros_like(resid)

    def advance(step, carry):
        signal, resid, direc, norm_now = carry
        image = covered(direc)
        shifted = direc + good * image
        alpha = norm_now / (total(direc * shifted) + EPS)
        signal = signal + alpha * image
        resid = resid - alpha * shifted
        norm_next = total(resid * resid)
        direc = resid + norm_next / (norm_now + EPS) * direc
        return signal, resid, direc, norm_next

    signal, resid, direc, norm_now = lax.fori_loop(
        0, ITERS, advance, (signal, resid, direc, norm_now), unroll=5
    )
    data = jnp.concatenate([data_ref[src] for src in range(n_src)], axis=1)
    filled = good * data + (1.0 - good) * signal
    for dst in range(n_src):
        put(dst, keep_ref, send_ref, (), filled[:, dst * f_dev : (dst + 1) * f_dev])


def fill(pieces, high, low, flags, f_dev):
    n_hi, _, rows, lanes = pieces[0].shape
    n_rows = lanes // (2 * FB) * rows
    n_freq = high.shape[0]

    def body(*refs):
        fill_kernel(len(pieces), *refs)

    return pl.pallas_call(
        body,
        in_specs=[pl.BlockSpec(memory_space=pltpu.VMEM)] * (len(pieces) + 3),
        out_specs=[pl.BlockSpec(memory_space=pltpu.VMEM)] * 2,
        out_shape=[jax.ShapeDtypeStruct((n_hi, n_rows, f_dev), jnp.float32)] * 2,
        scratch_shapes=[pltpu.VMEM((2 * n_hi, n_rows, f_dev), jnp.float32)],
        compiler_params=params(14),
        cost_estimate=pl.CostEstimate(
            flops=2 * ITERS * 3 * n_rows * n_freq * n_freq,
            bytes_accessed=4 * n_freq * n_freq,
            transcendentals=0,
        ),
        name="fill",
    )(*pieces, high, low, flags)


def gather_kernel(n_in, *refs):
    out_ref, stage_ref = refs[n_in:]
    n_src, n_rows, _ = stage_ref.shape
    pairs = out_ref.shape[0] // 2
    per_pair = n_src // pairs
    rows = n_rows // 4
    if rows % 8 == 0:
        for src, take in arrivals(refs[:n_in]):
            i, block = lax.div(src, per_pair), lax.rem(src, per_pair)
            at = pl.ds(pl.multiple_of(block * rows, rows), rows)
            value = take()
            for g in range(4):
                out_ref[2 * i + g // 2, g % 2, at, :] = value[g * rows : (g + 1) * rows, :]
        return
    for src, take in arrivals(refs[:n_in]):
        stage_ref[src] = take()
    for src in range(n_src):
        i, block = src // per_pair, src % per_pair
        for g in range(4):
            out_ref[2 * i + g // 2, g % 2, block * rows : (block + 1) * rows, :] = stage_ref[
                src, g * rows : (g + 1) * rows, :
            ]


def gather(pieces, shape):
    def body(*refs):
        gather_kernel(len(pieces), *refs)

    n_hi, n_rows, f_dev = pieces[0].shape
    return pl.pallas_call(
        body,
        in_specs=[pl.BlockSpec(memory_space=pltpu.VMEM)] * len(pieces),
        out_specs=pl.BlockSpec(memory_space=pltpu.VMEM),
        out_shape=jax.ShapeDtypeStruct(shape, jnp.float32),
        scratch_shapes=[pltpu.VMEM((2 * n_hi, n_rows, f_dev), jnp.float32)],
        compiler_params=params(14),
        name="gather",
    )(*pieces)


def make_tables(m_modes, n_tm, t_dev):
    n_time = t_dev * n_tm
    times = lax.axis_index("tm") * t_dev + jnp.arange(t_dev, dtype=jnp.int32)
    index = m_modes[:, None] * times[None, :] % n_time
    angle = 2.0 * math.pi / n_time * index.astype(jnp.float32)
    return jnp.concatenate([jnp.cos(angle), jnp.sin(angle)], axis=0).astype(jnp.bfloat16)


def exchange(send, bit, n_tm):
    return lax.ppermute(send, "tm", [(i, i ^ bit) for i in range(n_tm)])


def make_chunks(n_units):
    sizes = [2, 2] if n_units == 4 else [1] * n_units
    return [(sum(sizes[:i]), size) for i, size in enumerate(sizes)]


def per_device(vis, beam, fg_cov, flags, m_modes):
    t_dev, f_dev, _ = vis.shape
    n_tm = lax.axis_size("tm")
    n_chan = lax.axis_size("chan")
    n_slots = m_modes.shape[0] // n_tm
    degrees = beam.shape[3]
    orders = bit_orders(n_tm)
    targets = [target_order(n_tm, bits) for bits in orders]
    n_units = f_dev // (2 * FB)
    chunks = make_chunks(n_units)
    n_chunks = len(chunks)
    n_steps = len(orders[0])
    high, low = split(fg_cov)

    parts = [None] * n_chunks
    sends = [None] * n_chunks

    def begin(chunk, tab):
        first, units = chunks[chunk]
        outs = transform(tab, vis, first * 2 * FB, units, targets, n_slots)
        parts[chunk] = [[outs[0]], [outs[2]]]
        sends[chunk] = [outs[1], outs[3]]

    def go_on(chunk, place):
        for h, bits in enumerate(orders):
            got = exchange(sends[chunk][h], bits[place], n_tm)
            parts[chunk][h].append(got)
            size = got.shape[0] // 2
            sends[chunk][h] = sum(term[size : 2 * size] for term in parts[chunk][h])

    tab = make_tables(m_modes, n_tm, t_dev)
    for chunk in range(n_chunks):
        begin(chunk, tab)
    blocks = []
    for chunk, (first, units) in enumerate(chunks):
        before = max(chunk - 1, 0)
        source = sends[-1][0] if chunk == 0 else sends[before][0]
        source, beam = lax.optimization_barrier((source, beam))
        if chunk == 0:
            sends[-1][0] = source
        else:
            sends[before][0] = source
        block = load(beam, first * 2 * FB, units * 2 * FB)
        keeps = [group[0] for group in parts[chunk]]
        *keeps, block = lax.optimization_barrier((*keeps, block))
        parts[chunk] = [[keep] for keep in keeps]
        blocks.append(block)
        go_on(chunk, 0)
    sends[-1][0], high, low = lax.optimization_barrier((sends[-1][0], high, low))
    for place in range(1, n_steps):
        for chunk in range(n_chunks):
            go_on(chunk, place)

    coeffs = []
    for chunk, (first, units) in enumerate(chunks):
        coeffs = project(
            parts[chunk], blocks[chunk], first * 2 * FB, units, n_chan, n_units, coeffs
        )
    pieces = exchange_chan(*coeffs, n_chan)
    whole = fill(pieces, high, low, flags[None, :], f_dev)
    back = exchange_chan(*whole, n_chan)
    return gather(back, (n_slots, 2, degrees, f_dev))


def solution(mesh):
    placed = (P("tm", "chan", None), P("tm", "chan", None, None, None), P(), P(), P())
    return jax.shard_map(
        per_device,
        mesh=mesh,
        in_specs=placed,
        out_specs=P("tm", None, None, "chan"),
        check_vma=False,
    )
```

```python
import math

import jax
import jax.numpy as jnp
from jax import lax
from jax.experimental import pallas as pl
from jax.experimental.pallas import tpu as pltpu
from jax.sharding import PartitionSpec as P

ITERS = 10
EPS = 1e-06
FB = 16
PIECES = 8


def params(mebibytes):
    return pltpu.CompilerParams(vmem_limit_bytes=mebibytes * 1024 * 1024)


def bit_orders(n_tm):
    bits = [1 << i for i in range(n_tm.bit_length() - 1)]
    return bits, bits[::-1]


def target_order(n_tm, bits):
    return sorted(range(n_tm), key=lambda r: [int(bool(r & b)) for b in bits])


def transform_kernel(orders, n_slots, start, units, tab_ref, vis_ref, *refs):
    outs, (held_ref, wide_ref, full_ref, sems) = refs[:-4], refs[-4:]
    _, n_dev_time, _, width = held_ref.shape
    n_tm = len(orders[0])
    n_time = n_dev_time * n_tm
    n_rows = n_tm * n_slots
    half = width // 2
    depth = n_dev_time * FB
    scale = 1.0 / math.sqrt(n_time)

    def copies(unit):
        size = n_dev_time // PIECES
        for piece in range(PIECES):
            times = pl.ds(piece * size, size)
            source = vis_ref.at[times, pl.ds(start + unit * 2 * FB, 2 * FB), :]
            target = held_ref.at[unit, times]
            yield pltpu.make_async_copy(source, target, sems.at[unit, piece])

    for unit in range(units):
        for copy in copies(unit):
            copy.start()

    times = lax.broadcasted_iota(jnp.int32, (n_dev_time, depth), 0)
    lanes = lax.broadcasted_iota(jnp.int32, (n_dev_time, depth), 1)
    spread = jnp.where(lax.div(lanes, FB) == times, 1.0, 0.0).astype(jnp.bfloat16)
    wide_ref[...] = jnp.dot(tab_ref[...], spread, preferred_element_type=jnp.float32)
    me = lax.axis_index("tm")
    sub = lax.broadcasted_iota(jnp.int32, (FB, depth), 0)
    same = lax.rem(lax.broadcasted_iota(jnp.int32, (FB, depth), 1), FB) == sub
    for r in range(n_tm):
        for j in range(n_slots):
            for which in range(2):
                mode = which * n_rows + (me ^ r) * n_slots + j
                wide = jnp.broadcast_to(wide_ref[pl.ds(mode, 1), :], (FB, depth))
                at = (which * n_rows + r * n_slots + j) * FB
                full_ref[at : at + FB, :] = jnp.where(same, wide, 0.0).astype(jnp.bfloat16)

    for group in range(2 * units):
        part, place_f = group // units, group % units * FB
        order, keep, send = orders[part], outs[2 * part], outs[2 * part + 1]
        n_keep = keep.shape[0]
        if group % 2 == 0:
            for copy in copies(group // 2):
                copy.wait()
        first = group % 2 * FB
        data = held_ref[group // 2, :, first : first + FB, :].reshape(depth, width)
        prod = jnp.dot(full_ref[...], data, preferred_element_type=jnp.float32)
        cos_part, sin_part = prod[: n_rows * FB], prod[n_rows * FB :]
        real = (cos_part[:, :half] + sin_part[:, half:]) * scale
        imag = (cos_part[:, half:] - sin_part[:, :half]) * scale
        for place, r in enumerate(order):
            out = keep if place < n_keep else send
            for j in range(n_slots):
                at = (r * n_slots + j) * FB
                out[place % n_keep, j, place_f : place_f + FB, :half] = real[at : at + FB]
                out[place % n_keep, j, place_f : place_f + FB, half:] = imag[at : at + FB]


def transform(tab, vis, start, units, orders, n_slots):
    n_time, _, width = vis.shape
    n_tm = len(orders[0])
    depth = n_time * FB
    n_rows = n_tm * n_slots
    piece = jax.ShapeDtypeStruct((n_tm // 2, n_slots, units * FB, width), jnp.float32)

    def body(*refs):
        transform_kernel(orders, n_slots, start, units, *refs)

    return pl.pallas_call(
        body,
        in_specs=[
            pl.BlockSpec(memory_space=pltpu.VMEM),
            pl.BlockSpec(memory_space=pltpu.HBM),
        ],
        out_specs=[pl.BlockSpec(memory_space=pltpu.VMEM)] * 4,
        out_shape=[piece] * 4,
        scratch_shapes=[
            pltpu.VMEM((units, n_time, 2 * FB, width), jnp.bfloat16),
            pltpu.VMEM((2 * n_rows, depth), jnp.float32),
            pltpu.VMEM((2 * n_rows * FB, depth), jnp.bfloat16),
            pltpu.SemaphoreType.DMA((units, PIECES)),
        ],
        compiler_params=params(50),
        cost_estimate=pl.CostEstimate(
            flops=2 * 2 * n_rows * FB * depth * width * 2 * units,
            bytes_accessed=n_time * 2 * FB * units * width * 2 + 4 * 4 * piece.size,
            transcendentals=0,
        ),
        name="transform",
    )(tab, vis)


def position():
    me = lax.axis_index("chan")
    return lax.div(me, 2), lax.rem(me, 2)


def put(dst, keep_ref, send_ref, at, value):
    z, core = position()

    @pl.when(core == dst % 2)
    def _():
        keep_ref[(dst // 2) ^ z, *at] = value

    @pl.when(core != dst % 2)
    def _():
        send_ref[(dst // 2) ^ z, *at] = value


def exchange_chan(keep, send, n_chan):
    def swap(value, bits):
        return lax.ppermute(value, "chan", [(i, i ^ bits) for i in range(n_chan)])

    got = swap(send, 1)
    pairs = [(k, jnp.stack([keep[k], got[k]])) for k in reversed(range(1, n_chan // 2))]
    far = {k: swap(pair, 2 * k) for k, pair in pairs}
    return [keep, got, *(far[k] for k in reversed(range(1, n_chan // 2)))]


def arrivals(refs):
    z, core = position()
    keep, got, far = refs[0], refs[1], refs[2:]
    yield 2 * z + core, lambda *at: keep[0, *at]
    yield 2 * z + 1 - core, lambda *at: got[0, *at]
    for k, ref in enumerate(reversed(far), 1):
        yield 2 * (z ^ k) + core, lambda *at, ref=ref: ref[0, *at]
        yield 2 * (z ^ k) + 1 - core, lambda *at, ref=ref: ref[1, *at]


def project_kernel(n_terms, units, *refs):
    terms = refs[: 2 * n_terms]
    beam_ref, keep_ref, send_ref, vis_ref, flat_ref = refs[2 * n_terms], *refs[-4:]
    _, double, width = beam_ref.shape
    half, degrees = double // 2, width // FB
    n_slots = terms[0].shape[1]
    pairs = n_slots // 2
    pieces = [(u, i, s, h) for u in range(units) for i in range(pairs) for s in range(2) for h in range(2)]

    for at, (u, i, s, h) in enumerate(pieces):
        part, place = (2 * u + h) // units, (2 * u + h) % units * FB
        total = None
        for term in terms[part * n_terms : (part + 1) * n_terms]:
            value = term[0, 2 * i + s, place : place + FB, :]
            total = value if total is None else total + value
        real = total[:, :half].astype(jnp.bfloat16)
        imag = total[:, half:].astype(jnp.bfloat16)
        vis_ref[at, :FB, :half] = real
        vis_ref[at, FB:, :half] = imag
        vis_ref[at, :FB, half:] = -imag
        vis_ref[at, FB:, half:] = real

    per_pair = 2 * keep_ref.shape[0] // pairs
    rows = keep_ref.shape[2]
    per_tile = 128 // degrees
    sub = lax.broadcasted_iota(jnp.int32, (8, 128), 0)
    for at, (u, i, s, h) in enumerate(pieces):
        turned = beam_ref[(2 * i + s) * 2 * units + 2 * u + h]
        prod = jnp.dot(vis_ref[at], turned, preferred_element_type=jnp.float32)
        for p in range(2):
            for g in range(FB // 8):
                own = prod[p * FB + g * 8 : p * FB + g * 8 + 8, g * 8 * degrees : (g + 1) * 8 * degrees]
                pick = own[:, :128]
                for v in range(1, 8 // per_tile):
                    pick = jnp.where(sub // per_tile == v, own[:, v * 128 : (v + 1) * 128], pick)
                if per_tile == 2:
                    pick = jnp.where(sub % 2 == 0, pick, pltpu.roll(pick, degrees, 1))
                row = s * 4 * FB + p * 2 * FB + h * FB + g * 8
                flat_ref[row : row + 8, :] = pick
        if s == 1 and h == 1:
            coeffs = flat_ref[...].T[:degrees]
            for b in range(per_pair):
                put(i * per_pair + b, keep_ref, send_ref, (u,), coeffs[b * rows : (b + 1) * rows])


def load(beam, start, size, depth=6):
    n_slots, _, _, degrees, half = beam.shape
    per_slot = size // FB
    n_pieces = n_slots * per_slot
    depth = min(depth, n_pieces)

    def body(beam_ref, out_ref, held_ref, sems):
        def copy(at):
            f = pl.multiple_of(start + lax.rem(at, per_slot) * FB, FB)
            slot = lax.rem(at, depth)
            return pltpu.make_async_copy(
                beam_ref.at[lax.div(at, per_slot), pl.ds(f, FB)], held_ref.at[slot], sems.at[slot]
            )

        def step(at, carry):
            copy(at).wait()
            for p in range(2):
                block = held_ref[lax.rem(at, depth), :, p].reshape(FB * degrees, half)
                out_ref[at, p * half : (p + 1) * half, :] = block.T

            @pl.when(at + depth < n_pieces)
            def _():
                copy(at + depth).start()

            return carry

        for at in range(depth):
            copy(at).start()
        lax.fori_loop(0, n_pieces, step, 0)

    return pl.pallas_call(
        body,
        in_specs=[pl.BlockSpec(memory_space=pltpu.HBM)],
        out_specs=pl.BlockSpec(memory_space=pltpu.VMEM),
        out_shape=jax.ShapeDtypeStruct((n_pieces, 2 * half, FB * degrees), beam.dtype),
        scratch_shapes=[
            pltpu.VMEM((depth, FB, 2, degrees, half), beam.dtype),
            pltpu.SemaphoreType.DMA((depth,)),
        ],
        compiler_params=params(14),
        cost_estimate=pl.CostEstimate(
            flops=0, bytes_accessed=4 * n_pieces * FB * 2 * degrees * half, transcendentals=0
        ),
        name="load",
    )(beam)


def project(parts, beam, start, units, n_chan, n_units, buffers):
    _, double, width = beam.shape
    half, degrees = double // 2, width // FB
    n_slots = parts[0][0].shape[1]
    n_terms = len(parts[0])
    pairs = n_slots // 2
    rows = pairs * degrees // n_chan
    terms = [term for group in parts for term in group]
    place = start // (2 * FB) // units
    n_pieces = units * n_slots * 2

    def body(*refs):
        project_kernel(n_terms, units, *refs)

    term_spec = pl.BlockSpec((1, n_slots, units * FB, 2 * half), lambda i: (0, 0, 0, 0))
    return pl.pallas_call(
        body,
        grid=(1,),
        in_specs=[term_spec] * len(terms)
        + [pl.BlockSpec(memory_space=pltpu.VMEM)]
        + [pl.BlockSpec(memory_space=pl.ANY)] * len(buffers),
        out_specs=[pl.BlockSpec((n_chan // 2, units, rows, 8 * FB), lambda i: (0, place, 0, 0))] * 2,
        out_shape=[jax.ShapeDtypeStruct((n_chan // 2, n_units, rows, 8 * FB), jnp.float32)] * 2,
        scratch_shapes=[
            pltpu.VMEM((n_pieces, 2 * FB, 2 * half), jnp.bfloat16),
            pltpu.VMEM((8 * FB, 128), jnp.float32),
        ],
        input_output_aliases={len(terms) + 1 + i: i for i in range(len(buffers))},
        compiler_params=params(14),
        cost_estimate=pl.CostEstimate(
            flops=2 * n_slots * 2 * FB * units * 2 * degrees * half * 256,
            bytes_accessed=n_slots * 2 * FB * units * 2 * degrees * half * 2,
            transcendentals=0,
        ),
        name="project",
    )(*terms, beam, *buffers)


def split_kernel(cov_ref, high_ref, low_ref):
    cov = cov_ref[...]
    high = cov.astype(jnp.bfloat16)
    high_ref[...] = high
    low_ref[...] = (cov - high.astype(jnp.float32)).astype(jnp.bfloat16)


def split(cov, n_blocks=4):
    rows, cols = cov.shape
    spec = pl.BlockSpec((rows // n_blocks, cols), lambda i: (i, 0))
    half = jax.ShapeDtypeStruct(cov.shape, jnp.bfloat16)
    return pl.pallas_call(
        split_kernel,
        grid=(n_blocks,),
        in_specs=[spec],
        out_specs=[spec, spec],
        out_shape=[half, half],
        compiler_params=params(14),
        cost_estimate=pl.CostEstimate(
            flops=4 * cov.size, bytes_accessed=8 * cov.size, transcendentals=0
        ),
        name="split",
    )(cov)


def fill_kernel(n_in, *refs):
    high_ref, low_ref, flags_ref, keep_ref, send_ref, data_ref = refs[n_in:]
    n_src, n_rows, f_dev = data_ref.shape
    _, n_units, rows, lanes = refs[0].shape
    groups = lanes // (2 * FB)
    for src, take in arrivals(refs[:n_in]):
        for u in range(n_units):
            piece = take(u)
            for g in range(groups):
                data_ref[src, g * rows : (g + 1) * rows, u * 2 * FB : (u + 1) * 2 * FB] = piece[
                    :, g * 2 * FB : (g + 1) * 2 * FB
                ]
    data = jnp.concatenate([data_ref[src] for src in range(n_src)], axis=1)
    good = 1.0 - flags_ref[...].astype(jnp.float32)

    def total(values):
        return jnp.sum(values, axis=1, keepdims=True)

    def covered(vec):
        top = vec.astype(jnp.bfloat16)
        rest = (vec - top.astype(jnp.float32)).astype(jnp.bfloat16)
        both = jnp.concatenate([top, rest], axis=0)
        wide = jnp.dot(both, high_ref[...], preferred_element_type=jnp.float32)
        thin = jnp.dot(top, low_ref[...], preferred_element_type=jnp.float32)
        return wide[:n_rows] + (wide[n_rows:] + thin)

    resid = good * data
    direc = resid
    norm_now = total(resid * resid)
    signal = jnp.zeros_like(resid)

    def advance(step, carry):
        signal, resid, direc, norm_now = carry
        image = covered(direc)
        shifted = direc + good * image
        alpha = norm_now / (total(direc * shifted) + EPS)
        signal = signal + alpha * image
        resid = resid - alpha * shifted
        norm_next = total(resid * resid)
        direc = resid + norm_next / (norm_now + EPS) * direc
        return signal, resid, direc, norm_next

    signal, resid, direc, norm_now = lax.fori_loop(
        0, ITERS, advance, (signal, resid, direc, norm_now), unroll=True
    )
    data = jnp.concatenate([data_ref[src] for src in range(n_src)], axis=1)
    filled = good * data + (1.0 - good) * signal
    for dst in range(n_src):
        put(dst, keep_ref, send_ref, (), filled[:, dst * f_dev : (dst + 1) * f_dev])


def fill(pieces, high, low, flags, f_dev):
    n_hi, _, rows, lanes = pieces[0].shape
    n_rows = lanes // (2 * FB) * rows
    n_freq = high.shape[0]

    def body(*refs):
        fill_kernel(len(pieces), *refs)

    return pl.pallas_call(
        body,
        in_specs=[pl.BlockSpec(memory_space=pltpu.VMEM)] * (len(pieces) + 3),
        out_specs=[pl.BlockSpec(memory_space=pltpu.VMEM)] * 2,
        out_shape=[jax.ShapeDtypeStruct((n_hi, n_rows, f_dev), jnp.float32)] * 2,
        scratch_shapes=[pltpu.VMEM((2 * n_hi, n_rows, f_dev), jnp.float32)],
        compiler_params=params(14),
        cost_estimate=pl.CostEstimate(
            flops=2 * ITERS * 3 * n_rows * n_freq * n_freq,
            bytes_accessed=4 * n_freq * n_freq,
            transcendentals=0,
        ),
        name="fill",
    )(*pieces, high, low, flags)


def gather_kernel(n_in, *refs):
    out_ref, stage_ref = refs[n_in:]
    n_src, n_rows, _ = stage_ref.shape
    for src, take in arrivals(refs[:n_in]):
        stage_ref[src] = take()
    pairs = out_ref.shape[0] // 2
    per_pair = n_src // pairs
    rows = n_rows // 4
    for src in range(n_src):
        i, block = src // per_pair, src % per_pair
        for g in range(4):
            out_ref[2 * i + g // 2, g % 2, block * rows : (block + 1) * rows, :] = stage_ref[
                src, g * rows : (g + 1) * rows, :
            ]


def gather(pieces, shape):
    def body(*refs):
        gather_kernel(len(pieces), *refs)

    n_hi, n_rows, f_dev = pieces[0].shape
    return pl.pallas_call(
        body,
        in_specs=[pl.BlockSpec(memory_space=pltpu.VMEM)] * len(pieces),
        out_specs=pl.BlockSpec(memory_space=pltpu.VMEM),
        out_shape=jax.ShapeDtypeStruct(shape, jnp.float32),
        scratch_shapes=[pltpu.VMEM((2 * n_hi, n_rows, f_dev), jnp.float32)],
        compiler_params=params(14),
        name="gather",
    )(*pieces)


def make_tables(m_modes, n_tm, t_dev):
    n_time = t_dev * n_tm
    times = lax.axis_index("tm") * t_dev + jnp.arange(t_dev, dtype=jnp.int32)
    index = m_modes[:, None] * times[None, :] % n_time
    angle = 2.0 * math.pi / n_time * index.astype(jnp.float32)
    return jnp.concatenate([jnp.cos(angle), jnp.sin(angle)], axis=0).astype(jnp.bfloat16)


def exchange(send, bit, n_tm):
    return lax.ppermute(send, "tm", [(i, i ^ bit) for i in range(n_tm)])


def make_chunks(n_units):
    sizes = [2, 2] if n_units == 4 else [1] * n_units
    return [(sum(sizes[:i]), size) for i, size in enumerate(sizes)]


def per_device(vis, beam, fg_cov, flags, m_modes):
    t_dev, f_dev, _ = vis.shape
    n_tm = lax.axis_size("tm")
    n_chan = lax.axis_size("chan")
    n_slots = m_modes.shape[0] // n_tm
    degrees = beam.shape[3]
    orders = bit_orders(n_tm)
    targets = [target_order(n_tm, bits) for bits in orders]
    n_units = f_dev // (2 * FB)
    chunks = make_chunks(n_units)
    n_chunks = len(chunks)
    n_steps = len(orders[0])

    parts = [None] * n_chunks
    sends = [None] * n_chunks

    def begin(chunk, tab):
        first, units = chunks[chunk]
        outs = transform(tab, vis, first * 2 * FB, units, targets, n_slots)
        parts[chunk] = [[outs[0]], [outs[2]]]
        sends[chunk] = [outs[1], outs[3]]

    def go_on(chunk, place):
        for h, bits in enumerate(orders):
            got = exchange(sends[chunk][h], bits[place], n_tm)
            parts[chunk][h].append(got)
            size = got.shape[0] // 2
            sends[chunk][h] = sum(term[size : 2 * size] for term in parts[chunk][h])

    tab = make_tables(m_modes, n_tm, t_dev)
    for chunk in range(n_chunks):
        begin(chunk, tab)
    blocks = []
    for chunk, (first, units) in enumerate(chunks):
        before = max(chunk - 1, 0)
        source = sends[-1][0] if chunk == 0 else sends[before][0]
        source, beam = lax.optimization_barrier((source, beam))
        if chunk == 0:
            sends[-1][0] = source
        else:
            sends[before][0] = source
        block = load(beam, first * 2 * FB, units * 2 * FB)
        keeps = [group[0] for group in parts[chunk]]
        *keeps, block = lax.optimization_barrier((*keeps, block))
        parts[chunk] = [[keep] for keep in keeps]
        blocks.append(block)
        go_on(chunk, 0)
    *sends[-1], fg_cov = lax.optimization_barrier((*sends[-1], fg_cov))
    high, low = split(fg_cov)
    for place in range(1, n_steps):
        for chunk in range(n_chunks):
            go_on(chunk, place)

    coeffs = []
    for chunk, (first, units) in enumerate(chunks):
        coeffs = project(
            parts[chunk], blocks[chunk], first * 2 * FB, units, n_chan, n_units, coeffs
        )
    pieces = exchange_chan(*coeffs, n_chan)
    whole = fill(pieces, high, low, flags[None, :], f_dev)
    back = exchange_chan(*whole, n_chan)
    return gather(back, (n_slots, 2, degrees, f_dev))


def solution(mesh):
    placed = (P("tm", "chan", None), P("tm", "chan", None, None, None), P(), P(), P())
    return jax.shard_map(
        per_device,
        mesh=mesh,
        in_specs=placed,
        out_specs=P("tm", None, None, "chan"),
        check_vma=False,
    )
```

```python
import math

import jax
import jax.numpy as jnp
from jax import lax
from jax.experimental import pallas as pl
from jax.experimental.pallas import tpu as pltpu
from jax.sharding import PartitionSpec as P

ITERS = 10
EPS = 1e-06
FB = 16
PIECES = 8


def params(mebibytes):
    return pltpu.CompilerParams(vmem_limit_bytes=mebibytes * 1024 * 1024)


def bit_orders(n_tm):
    bits = [1 << i for i in range(n_tm.bit_length() - 1)]
    return bits, bits[::-1]


def target_order(n_tm, bits):
    return sorted(range(n_tm), key=lambda r: [int(bool(r & b)) for b in bits])


def transform_kernel(orders, n_slots, start, units, tab_ref, vis_ref, *refs):
    outs, (held_ref, wide_ref, full_ref, sems) = refs[:-4], refs[-4:]
    _, n_dev_time, _, width = held_ref.shape
    n_tm = len(orders[0])
    n_time = n_dev_time * n_tm
    n_rows = n_tm * n_slots
    half = width // 2
    depth = n_dev_time * FB
    scale = 1.0 / math.sqrt(n_time)

    def copies(unit):
        size = n_dev_time // PIECES
        for piece in range(PIECES):
            times = pl.ds(piece * size, size)
            source = vis_ref.at[times, pl.ds(start + unit * 2 * FB, 2 * FB), :]
            target = held_ref.at[unit, times]
            yield pltpu.make_async_copy(source, target, sems.at[unit, piece])

    for unit in range(units):
        for copy in copies(unit):
            copy.start()

    times = lax.broadcasted_iota(jnp.int32, (n_dev_time, depth), 0)
    lanes = lax.broadcasted_iota(jnp.int32, (n_dev_time, depth), 1)
    spread = jnp.where(lax.div(lanes, FB) == times, 1.0, 0.0).astype(jnp.bfloat16)
    wide_ref[...] = jnp.dot(tab_ref[...], spread, preferred_element_type=jnp.float32)
    me = lax.axis_index("tm")
    sub = lax.broadcasted_iota(jnp.int32, (FB, depth), 0)
    same = lax.rem(lax.broadcasted_iota(jnp.int32, (FB, depth), 1), FB) == sub
    for r in range(n_tm):
        for j in range(n_slots):
            for which in range(2):
                mode = which * n_rows + (me ^ r) * n_slots + j
                wide = jnp.broadcast_to(wide_ref[pl.ds(mode, 1), :], (FB, depth))
                at = (which * n_rows + r * n_slots + j) * FB
                full_ref[at : at + FB, :] = jnp.where(same, wide, 0.0).astype(jnp.bfloat16)

    for group in range(2 * units):
        part, place_f = group // units, group % units * FB
        order, keep, send = orders[part], outs[2 * part], outs[2 * part + 1]
        n_keep = keep.shape[0]
        if group % 2 == 0:
            for copy in copies(group // 2):
                copy.wait()
        first = group % 2 * FB
        data = held_ref[group // 2, :, first : first + FB, :].reshape(depth, width)
        prod = jnp.dot(full_ref[...], data, preferred_element_type=jnp.float32)
        cos_part, sin_part = prod[: n_rows * FB], prod[n_rows * FB :]
        real = (cos_part[:, :half] + sin_part[:, half:]) * scale
        imag = (cos_part[:, half:] - sin_part[:, :half]) * scale
        for place, r in enumerate(order):
            out = keep if place < n_keep else send
            for j in range(n_slots):
                at = (r * n_slots + j) * FB
                out[place % n_keep, j, place_f : place_f + FB, :half] = real[at : at + FB]
                out[place % n_keep, j, place_f : place_f + FB, half:] = imag[at : at + FB]


def transform(tab, vis, start, units, orders, n_slots):
    n_time, _, width = vis.shape
    n_tm = len(orders[0])
    depth = n_time * FB
    n_rows = n_tm * n_slots
    piece = jax.ShapeDtypeStruct((n_tm // 2, n_slots, units * FB, width), jnp.float32)

    def body(*refs):
        transform_kernel(orders, n_slots, start, units, *refs)

    return pl.pallas_call(
        body,
        in_specs=[
            pl.BlockSpec(memory_space=pltpu.VMEM),
            pl.BlockSpec(memory_space=pltpu.HBM),
        ],
        out_specs=[pl.BlockSpec(memory_space=pltpu.VMEM)] * 4,
        out_shape=[piece] * 4,
        scratch_shapes=[
            pltpu.VMEM((units, n_time, 2 * FB, width), jnp.bfloat16),
            pltpu.VMEM((2 * n_rows, depth), jnp.float32),
            pltpu.VMEM((2 * n_rows * FB, depth), jnp.bfloat16),
            pltpu.SemaphoreType.DMA((units, PIECES)),
        ],
        compiler_params=params(50),
        cost_estimate=pl.CostEstimate(
            flops=2 * 2 * n_rows * FB * depth * width * 2 * units,
            bytes_accessed=n_time * 2 * FB * units * width * 2 + 4 * 4 * piece.size,
            transcendentals=0,
        ),
        name="transform",
    )(tab, vis)


def position():
    me = lax.axis_index("chan")
    return lax.div(me, 2), lax.rem(me, 2)


def put(dst, keep_ref, send_ref, at, value):
    z, core = position()

    @pl.when(core == dst % 2)
    def _():
        keep_ref[(dst // 2) ^ z, *at] = value

    @pl.when(core != dst % 2)
    def _():
        send_ref[(dst // 2) ^ z, *at] = value


def exchange_chan(keep, send, n_chan):
    def swap(value, bits):
        return lax.ppermute(value, "chan", [(i, i ^ bits) for i in range(n_chan)])

    got = swap(send, 1)
    pairs = [(k, jnp.stack([keep[k], got[k]])) for k in reversed(range(1, n_chan // 2))]
    far = {k: swap(pair, 2 * k) for k, pair in pairs}
    return [keep, got, *(far[k] for k in range(1, n_chan // 2))]


def arrivals(refs):
    z, core = position()
    keep, got, far = refs[0], refs[1], refs[2:]
    yield 2 * z + core, lambda *at: keep[0, *at]
    yield 2 * z + 1 - core, lambda *at: got[0, *at]
    for k, ref in enumerate(far, 1):
        yield 2 * (z ^ k) + core, lambda *at, ref=ref: ref[0, *at]
        yield 2 * (z ^ k) + 1 - core, lambda *at, ref=ref: ref[1, *at]


def project_kernel(halves, unit, units, n_terms, *refs):
    beam_ref, keep_ref, send_ref, vis_ref, flat_ref = refs[n_terms], *refs[-4:]
    _, double, width = beam_ref.shape
    half, degrees = double // 2, width // FB
    n_slots = refs[0].shape[1]
    pairs = n_slots // 2
    pieces = [(i, s, h) for i in range(pairs) for s in range(2) for h in range(2)]

    for at, (i, s, h) in enumerate(pieces):
        terms, place = halves[h]
        total = None
        for term in terms:
            value = refs[term][0, 2 * i + s, place : place + FB, :]
            total = value if total is None else total + value
        real = total[:, :half].astype(jnp.bfloat16)
        imag = total[:, half:].astype(jnp.bfloat16)
        vis_ref[at, :FB, :half] = real
        vis_ref[at, FB:, :half] = imag
        vis_ref[at, :FB, half:] = -imag
        vis_ref[at, FB:, half:] = real

    per_pair = 2 * keep_ref.shape[0] // pairs
    rows = keep_ref.shape[1]
    per_tile = 128 // degrees
    sub = lax.broadcasted_iota(jnp.int32, (8, 128), 0)
    for at, (i, s, h) in enumerate(pieces):
        turned = beam_ref[((2 * i + s) * units + unit) * 2 + h]
        prod = jnp.dot(vis_ref[at], turned, preferred_element_type=jnp.float32)
        for p in range(2):
            for g in range(FB // 8):
                own = prod[p * FB + g * 8 : p * FB + g * 8 + 8, g * 8 * degrees : (g + 1) * 8 * degrees]
                pick = own[:, :128]
                for v in range(1, 8 // per_tile):
                    pick = jnp.where(sub // per_tile == v, own[:, v * 128 : (v + 1) * 128], pick)
                if per_tile == 2:
                    pick = jnp.where(sub % 2 == 0, pick, pltpu.roll(pick, degrees, 1))
                row = s * 4 * FB + p * 2 * FB + h * FB + g * 8
                flat_ref[row : row + 8, :] = pick
        if s == 1 and h == 1:
            coeffs = flat_ref[...].T[:degrees]
            for b in range(per_pair):
                put(i * per_pair + b, keep_ref, send_ref, (), coeffs[b * rows : (b + 1) * rows])


def load(beam, start, size, depth=6):
    n_slots, _, _, degrees, half = beam.shape
    per_slot = size // FB
    n_pieces = n_slots * per_slot
    depth = min(depth, n_pieces)

    def body(beam_ref, out_ref, held_ref, sems):
        def copy(at):
            f = pl.multiple_of(start + lax.rem(at, per_slot) * FB, FB)
            slot = lax.rem(at, depth)
            return pltpu.make_async_copy(
                beam_ref.at[lax.div(at, per_slot), pl.ds(f, FB)], held_ref.at[slot], sems.at[slot]
            )

        def step(at, carry):
            copy(at).wait()
            for p in range(2):
                block = held_ref[lax.rem(at, depth), :, p].reshape(FB * degrees, half)
                out_ref[at, p * half : (p + 1) * half, :] = block.T

            @pl.when(at + depth < n_pieces)
            def _():
                copy(at + depth).start()

            return carry

        for at in range(depth):
            copy(at).start()
        lax.fori_loop(0, n_pieces, step, 0)

    return pl.pallas_call(
        body,
        in_specs=[pl.BlockSpec(memory_space=pltpu.HBM)],
        out_specs=pl.BlockSpec(memory_space=pltpu.VMEM),
        out_shape=jax.ShapeDtypeStruct((n_pieces, 2 * half, FB * degrees), beam.dtype),
        scratch_shapes=[
            pltpu.VMEM((depth, FB, 2, degrees, half), beam.dtype),
            pltpu.SemaphoreType.DMA((depth,)),
        ],
        compiler_params=params(10),
        cost_estimate=pl.CostEstimate(
            flops=0, bytes_accessed=4 * n_pieces * FB * 2 * degrees * half, transcendentals=0
        ),
        name="load",
    )(beam)


def project(parts, beam, unit, units, place, n_chan, n_units, buffers):
    _, double, width = beam.shape
    half, degrees = double // 2, width // FB
    n_slots = parts[0][0].shape[1]
    pairs = n_slots // 2
    rows = pairs * degrees // n_chan
    terms, halves = [], []
    for h in range(2):
        part, at = (2 * unit + h) // units, (2 * unit + h) % units * FB
        if not halves or part != (2 * unit) // units:
            terms += parts[part]
        halves.append((range(len(terms) - len(parts[part]), len(terms)), at))
    n_terms = len(terms)
    n_pieces = n_slots * 2

    def body(*refs):
        project_kernel(halves, unit, units, n_terms, *refs)

    term_spec = pl.BlockSpec((1, n_slots, units * FB, 2 * half), lambda i: (0, 0, 0, 0))
    return pl.pallas_call(
        body,
        grid=(1,),
        in_specs=[term_spec] * n_terms
        + [pl.BlockSpec(memory_space=pltpu.VMEM)]
        + [pl.BlockSpec(memory_space=pl.ANY)] * len(buffers),
        out_specs=[pl.BlockSpec((n_chan // 2, None, rows, 8 * FB), lambda i: (0, place, 0, 0))] * 2,
        out_shape=[jax.ShapeDtypeStruct((n_chan // 2, n_units, rows, 8 * FB), jnp.float32)] * 2,
        scratch_shapes=[
            pltpu.VMEM((n_pieces, 2 * FB, 2 * half), jnp.bfloat16),
            pltpu.VMEM((8 * FB, 128), jnp.float32),
        ],
        input_output_aliases={n_terms + 1 + i: i for i in range(len(buffers))},
        compiler_params=params(6),
        cost_estimate=pl.CostEstimate(
            flops=2 * n_slots * 2 * FB * 2 * degrees * half * 256,
            bytes_accessed=n_slots * 2 * FB * 2 * degrees * half * 2,
            transcendentals=0,
        ),
        name="project",
    )(*terms, beam, *buffers)


def split_kernel(cov_ref, high_ref, low_ref):
    cov = cov_ref[...]
    high = cov.astype(jnp.bfloat16)
    high_ref[...] = high
    low_ref[...] = (cov - high.astype(jnp.float32)).astype(jnp.bfloat16)


def split(cov, n_blocks=4):
    rows, cols = cov.shape
    spec = pl.BlockSpec((rows // n_blocks, cols), lambda i: (i, 0))
    half = jax.ShapeDtypeStruct(cov.shape, jnp.bfloat16)
    return pl.pallas_call(
        split_kernel,
        grid=(n_blocks,),
        in_specs=[spec],
        out_specs=[spec, spec],
        out_shape=[half, half],
        compiler_params=params(10),
        cost_estimate=pl.CostEstimate(
            flops=4 * cov.size, bytes_accessed=8 * cov.size, transcendentals=0
        ),
        name="split",
    )(cov)


def fill_kernel(n_in, *refs):
    high_ref, low_ref, flags_ref, keep_ref, send_ref, data_ref = refs[n_in:]
    n_src, n_rows, f_dev = data_ref.shape
    _, n_units, rows, lanes = refs[0].shape
    groups = lanes // (2 * FB)
    for src, take in arrivals(refs[:n_in]):
        for u in range(n_units):
            piece = take(u)
            for g in range(groups):
                data_ref[src, g * rows : (g + 1) * rows, u * 2 * FB : (u + 1) * 2 * FB] = piece[
                    :, g * 2 * FB : (g + 1) * 2 * FB
                ]
    data = jnp.concatenate([data_ref[src] for src in range(n_src)], axis=1)
    good = 1.0 - flags_ref[...].astype(jnp.float32)

    def total(values):
        return jnp.sum(values, axis=1, keepdims=True)

    def covered(vec):
        top = vec.astype(jnp.bfloat16)
        rest = (vec - top.astype(jnp.float32)).astype(jnp.bfloat16)
        both = jnp.concatenate([top, rest], axis=0)
        wide = jnp.dot(both, high_ref[...], preferred_element_type=jnp.float32)
        thin = jnp.dot(top, low_ref[...], preferred_element_type=jnp.float32)
        return wide[:n_rows] + (wide[n_rows:] + thin)

    resid = good * data
    direc = resid
    norm_now = total(resid * resid)
    signal = jnp.zeros_like(resid)

    def advance(step, carry):
        signal, resid, direc, norm_now = carry
        image = covered(direc)
        shifted = direc + good * image
        alpha = norm_now / (total(direc * shifted) + EPS)
        signal = signal + alpha * image
        resid = resid - alpha * shifted
        norm_next = total(resid * resid)
        direc = resid + norm_next / (norm_now + EPS) * direc
        return signal, resid, direc, norm_next

    signal, resid, direc, norm_now = lax.fori_loop(
        0, ITERS, advance, (signal, resid, direc, norm_now), unroll=True
    )
    data = jnp.concatenate([data_ref[src] for src in range(n_src)], axis=1)
    filled = good * data + (1.0 - good) * signal
    for dst in range(n_src):
        put(dst, keep_ref, send_ref, (), filled[:, dst * f_dev : (dst + 1) * f_dev])


def fill(pieces, high, low, flags, f_dev):
    n_hi, _, rows, lanes = pieces[0].shape
    n_rows = lanes // (2 * FB) * rows
    n_freq = high.shape[0]

    def body(*refs):
        fill_kernel(len(pieces), *refs)

    return pl.pallas_call(
        body,
        in_specs=[pl.BlockSpec(memory_space=pltpu.VMEM)] * (len(pieces) + 3),
        out_specs=[pl.BlockSpec(memory_space=pltpu.VMEM)] * 2,
        out_shape=[jax.ShapeDtypeStruct((n_hi, n_rows, f_dev), jnp.float32)] * 2,
        scratch_shapes=[pltpu.VMEM((2 * n_hi, n_rows, f_dev), jnp.float32)],
        compiler_params=params(8),
        cost_estimate=pl.CostEstimate(
            flops=2 * ITERS * 3 * n_rows * n_freq * n_freq,
            bytes_accessed=4 * n_freq * n_freq,
            transcendentals=0,
        ),
        name="fill",
    )(*pieces, high, low, flags)


def gather_kernel(n_in, *refs):
    out_ref, stage_ref = refs[n_in:]
    n_src, n_rows, _ = stage_ref.shape
    for src, take in arrivals(refs[:n_in]):
        stage_ref[src] = take()
    pairs = out_ref.shape[0] // 2
    per_pair = n_src // pairs
    rows = n_rows // 4
    for src in range(n_src):
        i, block = src // per_pair, src % per_pair
        for g in range(4):
            out_ref[2 * i + g // 2, g % 2, block * rows : (block + 1) * rows, :] = stage_ref[
                src, g * rows : (g + 1) * rows, :
            ]


def gather(pieces, shape):
    def body(*refs):
        gather_kernel(len(pieces), *refs)

    n_hi, n_rows, f_dev = pieces[0].shape
    return pl.pallas_call(
        body,
        in_specs=[pl.BlockSpec(memory_space=pltpu.VMEM)] * len(pieces),
        out_specs=pl.BlockSpec(memory_space=pltpu.VMEM),
        out_shape=jax.ShapeDtypeStruct(shape, jnp.float32),
        scratch_shapes=[pltpu.VMEM((2 * n_hi, n_rows, f_dev), jnp.float32)],
        compiler_params=params(4),
        name="gather",
    )(*pieces)


def make_tables(m_modes, n_tm, t_dev):
    n_time = t_dev * n_tm
    times = lax.axis_index("tm") * t_dev + jnp.arange(t_dev, dtype=jnp.int32)
    index = m_modes[:, None] * times[None, :] % n_time
    angle = 2.0 * math.pi / n_time * index.astype(jnp.float32)
    return jnp.concatenate([jnp.cos(angle), jnp.sin(angle)], axis=0).astype(jnp.bfloat16)


def exchange(send, bit, n_tm):
    return lax.ppermute(send, "tm", [(i, i ^ bit) for i in range(n_tm)])


def make_chunks(n_units):
    sizes = [2, 2] if n_units == 4 else [1] * n_units
    return [(sum(sizes[:i]), size) for i, size in enumerate(sizes)]


def per_device(vis, beam, fg_cov, flags, m_modes):
    t_dev, f_dev, _ = vis.shape
    n_tm = lax.axis_size("tm")
    n_chan = lax.axis_size("chan")
    n_slots = m_modes.shape[0] // n_tm
    degrees = beam.shape[3]
    orders = bit_orders(n_tm)
    targets = [target_order(n_tm, bits) for bits in orders]
    n_units = f_dev // (2 * FB)
    chunks = make_chunks(n_units)
    n_chunks = len(chunks)
    n_steps = len(orders[0])

    parts = [None] * n_chunks
    sends = [None] * n_chunks

    def begin(chunk, tab):
        first, units = chunks[chunk]
        outs = transform(tab, vis, first * 2 * FB, units, targets, n_slots)
        parts[chunk] = [[outs[0]], [outs[2]]]
        sends[chunk] = [outs[1], outs[3]]

    def go_on(chunk, place):
        for h, bits in enumerate(orders):
            got = exchange(sends[chunk][h], bits[place], n_tm)
            parts[chunk][h].append(got)
            size = got.shape[0] // 2
            sends[chunk][h] = sum(term[size : 2 * size] for term in parts[chunk][h])

    tab = make_tables(m_modes, n_tm, t_dev)
    for chunk in range(n_chunks):
        begin(chunk, tab)
    blocks = []
    for chunk, (first, units) in enumerate(chunks):
        before = max(chunk - 1, 0)
        source = sends[-1][0] if chunk == 0 else sends[before][0]
        source, beam = lax.optimization_barrier((source, beam))
        if chunk == 0:
            sends[-1][0] = source
        else:
            sends[before][0] = source
        block = load(beam, first * 2 * FB, units * 2 * FB)
        keeps = [group[0] for group in parts[chunk]]
        *keeps, block = lax.optimization_barrier((*keeps, block))
        parts[chunk] = [[keep] for keep in keeps]
        blocks.append(block)
        go_on(chunk, 0)
    *sends[-1], fg_cov = lax.optimization_barrier((*sends[-1], fg_cov))
    high, low = split(fg_cov)
    for place in range(1, n_steps):
        for chunk in range(n_chunks):
            go_on(chunk, place)

    coeffs = []
    for chunk, (first, units) in enumerate(chunks):
        for unit in reversed(range(units)):
            coeffs = project(
                parts[chunk], blocks[chunk], unit, units, first + unit, n_chan, n_units, coeffs
            )
    pieces = exchange_chan(*coeffs, n_chan)
    whole = fill(pieces, high, low, flags[None, :], f_dev)
    back = exchange_chan(*whole, n_chan)
    return gather(back, (n_slots, 2, degrees, f_dev))


def solution(mesh):
    placed = (P("tm", "chan", None), P("tm", "chan", None, None, None), P(), P(), P())
    return jax.shard_map(
        per_device,
        mesh=mesh,
        in_specs=placed,
        out_specs=P("tm", None, None, "chan"),
        check_vma=False,
    )
```

```python
import math

import jax
import jax.numpy as jnp
from jax import lax
from jax.experimental import pallas as pl
from jax.experimental.pallas import tpu as pltpu
from jax.sharding import PartitionSpec as P

ITERS = 10
EPS = 1e-06
FB = 16
PIECES = 8


def params(mebibytes):
    return pltpu.CompilerParams(vmem_limit_bytes=mebibytes * 1024 * 1024)


def bit_orders(n_tm):
    bits = [1 << i for i in range(n_tm.bit_length() - 1)]
    return bits, bits[::-1]


def target_order(n_tm, bits):
    return sorted(range(n_tm), key=lambda r: [int(bool(r & b)) for b in bits])


def transform_kernel(orders, n_slots, start, units, tab_ref, vis_ref, *refs):
    outs, (held_ref, wide_ref, full_ref, sems) = refs[:-4], refs[-4:]
    _, n_dev_time, _, width = held_ref.shape
    n_tm = len(orders[0])
    n_time = n_dev_time * n_tm
    n_rows = n_tm * n_slots
    half = width // 2
    depth = n_dev_time * FB
    scale = 1.0 / math.sqrt(n_time)

    def copies(unit):
        size = n_dev_time // PIECES
        for piece in range(PIECES):
            times = pl.ds(piece * size, size)
            source = vis_ref.at[times, pl.ds(start + unit * 2 * FB, 2 * FB), :]
            target = held_ref.at[unit, times]
            yield pltpu.make_async_copy(source, target, sems.at[unit, piece])

    for unit in range(units):
        for copy in copies(unit):
            copy.start()

    times = lax.broadcasted_iota(jnp.int32, (n_dev_time, depth), 0)
    lanes = lax.broadcasted_iota(jnp.int32, (n_dev_time, depth), 1)
    spread = jnp.where(lax.div(lanes, FB) == times, 1.0, 0.0).astype(jnp.bfloat16)
    wide_ref[...] = jnp.dot(tab_ref[...], spread, preferred_element_type=jnp.float32)
    me = lax.axis_index("tm")
    sub = lax.broadcasted_iota(jnp.int32, (FB, depth), 0)
    same = lax.rem(lax.broadcasted_iota(jnp.int32, (FB, depth), 1), FB) == sub
    for r in range(n_tm):
        for j in range(n_slots):
            for which in range(2):
                mode = which * n_rows + (me ^ r) * n_slots + j
                wide = jnp.broadcast_to(wide_ref[pl.ds(mode, 1), :], (FB, depth))
                at = (which * n_rows + r * n_slots + j) * FB
                full_ref[at : at + FB, :] = jnp.where(same, wide, 0.0).astype(jnp.bfloat16)

    for group in range(2 * units):
        part, place_f = group // units, group % units * FB
        order, keep, send = orders[part], outs[2 * part], outs[2 * part + 1]
        n_keep = keep.shape[0]
        if group % 2 == 0:
            for copy in copies(group // 2):
                copy.wait()
        first = group % 2 * FB
        data = held_ref[group // 2, :, first : first + FB, :].reshape(depth, width)
        prod = jnp.dot(full_ref[...], data, preferred_element_type=jnp.float32)
        cos_part, sin_part = prod[: n_rows * FB], prod[n_rows * FB :]
        real = (cos_part[:, :half] + sin_part[:, half:]) * scale
        imag = (cos_part[:, half:] - sin_part[:, :half]) * scale
        for place, r in enumerate(order):
            out = keep if place < n_keep else send
            for j in range(n_slots):
                at = (r * n_slots + j) * FB
                out[place % n_keep, j, place_f : place_f + FB, :half] = real[at : at + FB]
                out[place % n_keep, j, place_f : place_f + FB, half:] = imag[at : at + FB]


def transform(tab, vis, start, units, orders, n_slots):
    n_time, _, width = vis.shape
    n_tm = len(orders[0])
    depth = n_time * FB
    n_rows = n_tm * n_slots
    piece = jax.ShapeDtypeStruct((n_tm // 2, n_slots, units * FB, width), jnp.float32)

    def body(*refs):
        transform_kernel(orders, n_slots, start, units, *refs)

    return pl.pallas_call(
        body,
        in_specs=[
            pl.BlockSpec(memory_space=pltpu.VMEM),
            pl.BlockSpec(memory_space=pltpu.HBM),
        ],
        out_specs=[pl.BlockSpec(memory_space=pltpu.VMEM)] * 4,
        out_shape=[piece] * 4,
        scratch_shapes=[
            pltpu.VMEM((units, n_time, 2 * FB, width), jnp.bfloat16),
            pltpu.VMEM((2 * n_rows, depth), jnp.float32),
            pltpu.VMEM((2 * n_rows * FB, depth), jnp.bfloat16),
            pltpu.SemaphoreType.DMA((units, PIECES)),
        ],
        compiler_params=params(50),
        cost_estimate=pl.CostEstimate(
            flops=2 * 2 * n_rows * FB * depth * width * 2 * units,
            bytes_accessed=n_time * 2 * FB * units * width * 2 + 4 * 4 * piece.size,
            transcendentals=0,
        ),
        name="transform",
    )(tab, vis)


def position():
    me = lax.axis_index("chan")
    return lax.div(me, 2), lax.rem(me, 2)


def put(dst, keep_ref, send_ref, at, value):
    z, core = position()

    @pl.when(core == dst % 2)
    def _():
        keep_ref[(dst // 2) ^ z, *at] = value

    @pl.when(core != dst % 2)
    def _():
        send_ref[(dst // 2) ^ z, *at] = value


def exchange_chan(keep, send, n_chan):
    def swap(value, bits):
        return lax.ppermute(value, "chan", [(i, i ^ bits) for i in range(n_chan)])

    got = swap(send, 1)
    pairs = [(k, jnp.stack([keep[k], got[k]])) for k in reversed(range(1, n_chan // 2))]
    far = {k: swap(pair, 2 * k) for k, pair in pairs}
    return [keep, got, *(far[k] for k in reversed(range(1, n_chan // 2)))]


def arrivals(refs):
    z, core = position()
    keep, got, far = refs[0], refs[1], refs[2:]
    yield 2 * z + core, lambda *at: keep[0, *at]
    yield 2 * z + 1 - core, lambda *at: got[0, *at]
    for k, ref in enumerate(reversed(far), 1):
        yield 2 * (z ^ k) + core, lambda *at, ref=ref: ref[0, *at]
        yield 2 * (z ^ k) + 1 - core, lambda *at, ref=ref: ref[1, *at]


def project_kernel(halves, unit, units, n_terms, *refs):
    beam_ref, keep_ref, send_ref, vis_ref, flat_ref = refs[n_terms], *refs[-4:]
    _, double, width = beam_ref.shape
    half, degrees = double // 2, width // FB
    n_slots = refs[0].shape[1]
    pairs = n_slots // 2
    pieces = [(i, s, h) for i in range(pairs) for s in range(2) for h in range(2)]

    for at, (i, s, h) in enumerate(pieces):
        terms, place = halves[h]
        total = None
        for term in terms:
            value = refs[term][0, 2 * i + s, place : place + FB, :]
            total = value if total is None else total + value
        real = total[:, :half].astype(jnp.bfloat16)
        imag = total[:, half:].astype(jnp.bfloat16)
        vis_ref[at, :FB, :half] = real
        vis_ref[at, FB:, :half] = imag
        vis_ref[at, :FB, half:] = -imag
        vis_ref[at, FB:, half:] = real

    per_pair = 2 * keep_ref.shape[0] // pairs
    rows = keep_ref.shape[1]
    per_tile = 128 // degrees
    sub = lax.broadcasted_iota(jnp.int32, (8, 128), 0)
    for at, (i, s, h) in enumerate(pieces):
        turned = beam_ref[((2 * i + s) * units + unit) * 2 + h]
        prod = jnp.dot(vis_ref[at], turned, preferred_element_type=jnp.float32)
        for p in range(2):
            for g in range(FB // 8):
                own = prod[p * FB + g * 8 : p * FB + g * 8 + 8, g * 8 * degrees : (g + 1) * 8 * degrees]
                pick = own[:, :128]
                for v in range(1, 8 // per_tile):
                    pick = jnp.where(sub // per_tile == v, own[:, v * 128 : (v + 1) * 128], pick)
                if per_tile == 2:
                    pick = jnp.where(sub % 2 == 0, pick, pltpu.roll(pick, degrees, 1))
                row = s * 4 * FB + p * 2 * FB + h * FB + g * 8
                flat_ref[row : row + 8, :] = pick
        if s == 1 and h == 1:
            coeffs = flat_ref[...].T[:degrees]
            for b in range(per_pair):
                put(i * per_pair + b, keep_ref, send_ref, (), coeffs[b * rows : (b + 1) * rows])


def load(beam, start, size, depth=6):
    n_slots, _, _, degrees, half = beam.shape
    per_slot = size // FB
    n_pieces = n_slots * per_slot
    depth = min(depth, n_pieces)

    def body(beam_ref, out_ref, held_ref, sems):
        def copy(at):
            f = pl.multiple_of(start + lax.rem(at, per_slot) * FB, FB)
            slot = lax.rem(at, depth)
            return pltpu.make_async_copy(
                beam_ref.at[lax.div(at, per_slot), pl.ds(f, FB)], held_ref.at[slot], sems.at[slot]
            )

        def step(at, carry):
            copy(at).wait()
            for p in range(2):
                block = held_ref[lax.rem(at, depth), :, p].reshape(FB * degrees, half)
                out_ref[at, p * half : (p + 1) * half, :] = block.T

            @pl.when(at + depth < n_pieces)
            def _():
                copy(at + depth).start()

            return carry

        for at in range(depth):
            copy(at).start()
        lax.fori_loop(0, n_pieces, step, 0)

    return pl.pallas_call(
        body,
        in_specs=[pl.BlockSpec(memory_space=pltpu.HBM)],
        out_specs=pl.BlockSpec(memory_space=pltpu.VMEM),
        out_shape=jax.ShapeDtypeStruct((n_pieces, 2 * half, FB * degrees), beam.dtype),
        scratch_shapes=[
            pltpu.VMEM((depth, FB, 2, degrees, half), beam.dtype),
            pltpu.SemaphoreType.DMA((depth,)),
        ],
        compiler_params=params(10),
        cost_estimate=pl.CostEstimate(
            flops=0, bytes_accessed=4 * n_pieces * FB * 2 * degrees * half, transcendentals=0
        ),
        name="load",
    )(beam)


def project(parts, beam, unit, units, place, n_chan, n_units, buffers):
    _, double, width = beam.shape
    half, degrees = double // 2, width // FB
    n_slots = parts[0][0].shape[1]
    pairs = n_slots // 2
    rows = pairs * degrees // n_chan
    terms, halves = [], []
    for h in range(2):
        part, at = (2 * unit + h) // units, (2 * unit + h) % units * FB
        if not halves or part != (2 * unit) // units:
            terms += parts[part]
        halves.append((range(len(terms) - len(parts[part]), len(terms)), at))
    n_terms = len(terms)
    n_pieces = n_slots * 2

    def body(*refs):
        project_kernel(halves, unit, units, n_terms, *refs)

    term_spec = pl.BlockSpec((1, n_slots, units * FB, 2 * half), lambda i: (0, 0, 0, 0))
    return pl.pallas_call(
        body,
        grid=(1,),
        in_specs=[term_spec] * n_terms
        + [pl.BlockSpec(memory_space=pltpu.VMEM)]
        + [pl.BlockSpec(memory_space=pl.ANY)] * len(buffers),
        out_specs=[pl.BlockSpec((n_chan // 2, None, rows, 8 * FB), lambda i: (0, place, 0, 0))] * 2,
        out_shape=[jax.ShapeDtypeStruct((n_chan // 2, n_units, rows, 8 * FB), jnp.float32)] * 2,
        scratch_shapes=[
            pltpu.VMEM((n_pieces, 2 * FB, 2 * half), jnp.bfloat16),
            pltpu.VMEM((8 * FB, 128), jnp.float32),
        ],
        input_output_aliases={n_terms + 1 + i: i for i in range(len(buffers))},
        compiler_params=params(6),
        cost_estimate=pl.CostEstimate(
            flops=2 * n_slots * 2 * FB * 2 * degrees * half * 256,
            bytes_accessed=n_slots * 2 * FB * 2 * degrees * half * 2,
            transcendentals=0,
        ),
        name="project",
    )(*terms, beam, *buffers)


def split_kernel(cov_ref, high_ref, low_ref):
    cov = cov_ref[...]
    high = cov.astype(jnp.bfloat16)
    high_ref[...] = high
    low_ref[...] = (cov - high.astype(jnp.float32)).astype(jnp.bfloat16)


def split(cov, n_blocks=4):
    rows, cols = cov.shape
    spec = pl.BlockSpec((rows // n_blocks, cols), lambda i: (i, 0))
    half = jax.ShapeDtypeStruct(cov.shape, jnp.bfloat16)
    return pl.pallas_call(
        split_kernel,
        grid=(n_blocks,),
        in_specs=[spec],
        out_specs=[spec, spec],
        out_shape=[half, half],
        compiler_params=params(10),
        cost_estimate=pl.CostEstimate(
            flops=4 * cov.size, bytes_accessed=8 * cov.size, transcendentals=0
        ),
        name="split",
    )(cov)


def fill_kernel(n_in, *refs):
    high_ref, low_ref, flags_ref, keep_ref, send_ref, data_ref = refs[n_in:]
    n_src, n_rows, f_dev = data_ref.shape
    _, n_units, rows, lanes = refs[0].shape
    groups = lanes // (2 * FB)
    for src, take in arrivals(refs[:n_in]):
        for u in range(n_units):
            piece = take(u)
            for g in range(groups):
                data_ref[src, g * rows : (g + 1) * rows, u * 2 * FB : (u + 1) * 2 * FB] = piece[
                    :, g * 2 * FB : (g + 1) * 2 * FB
                ]
    data = jnp.concatenate([data_ref[src] for src in range(n_src)], axis=1)
    good = 1.0 - flags_ref[...].astype(jnp.float32)

    def total(values):
        return jnp.sum(values, axis=1, keepdims=True)

    def covered(vec):
        top = vec.astype(jnp.bfloat16)
        rest = (vec - top.astype(jnp.float32)).astype(jnp.bfloat16)
        both = jnp.concatenate([top, rest], axis=0)
        wide = jnp.dot(both, high_ref[...], preferred_element_type=jnp.float32)
        thin = jnp.dot(top, low_ref[...], preferred_element_type=jnp.float32)
        return wide[:n_rows] + (wide[n_rows:] + thin)

    resid = good * data
    direc = resid
    norm_now = total(resid * resid)
    signal = jnp.zeros_like(resid)

    def advance(step, carry):
        signal, resid, direc, norm_now = carry
        image = covered(direc)
        shifted = direc + good * image
        alpha = norm_now / (total(direc * shifted) + EPS)
        signal = signal + alpha * image
        resid = resid - alpha * shifted
        norm_next = total(resid * resid)
        direc = resid + norm_next / (norm_now + EPS) * direc
        return signal, resid, direc, norm_next

    signal, resid, direc, norm_now = lax.fori_loop(
        0, ITERS, advance, (signal, resid, direc, norm_now), unroll=True
    )
    data = jnp.concatenate([data_ref[src] for src in range(n_src)], axis=1)
    filled = good * data + (1.0 - good) * signal
    for dst in range(n_src):
        put(dst, keep_ref, send_ref, (), filled[:, dst * f_dev : (dst + 1) * f_dev])


def fill(pieces, high, low, flags, f_dev):
    n_hi, _, rows, lanes = pieces[0].shape
    n_rows = lanes // (2 * FB) * rows
    n_freq = high.shape[0]

    def body(*refs):
        fill_kernel(len(pieces), *refs)

    return pl.pallas_call(
        body,
        in_specs=[pl.BlockSpec(memory_space=pltpu.VMEM)] * (len(pieces) + 3),
        out_specs=[pl.BlockSpec(memory_space=pltpu.VMEM)] * 2,
        out_shape=[jax.ShapeDtypeStruct((n_hi, n_rows, f_dev), jnp.float32)] * 2,
        scratch_shapes=[pltpu.VMEM((2 * n_hi, n_rows, f_dev), jnp.float32)],
        compiler_params=params(8),
        cost_estimate=pl.CostEstimate(
            flops=2 * ITERS * 3 * n_rows * n_freq * n_freq,
            bytes_accessed=4 * n_freq * n_freq,
            transcendentals=0,
        ),
        name="fill",
    )(*pieces, high, low, flags)


def gather_kernel(n_in, *refs):
    out_ref, stage_ref = refs[n_in:]
    n_src, n_rows, _ = stage_ref.shape
    for src, take in arrivals(refs[:n_in]):
        stage_ref[src] = take()
    pairs = out_ref.shape[0] // 2
    per_pair = n_src // pairs
    rows = n_rows // 4
    for src in range(n_src):
        i, block = src // per_pair, src % per_pair
        for g in range(4):
            out_ref[2 * i + g // 2, g % 2, block * rows : (block + 1) * rows, :] = stage_ref[
                src, g * rows : (g + 1) * rows, :
            ]


def gather(pieces, shape):
    def body(*refs):
        gather_kernel(len(pieces), *refs)

    n_hi, n_rows, f_dev = pieces[0].shape
    return pl.pallas_call(
        body,
        in_specs=[pl.BlockSpec(memory_space=pltpu.VMEM)] * len(pieces),
        out_specs=pl.BlockSpec(memory_space=pltpu.VMEM),
        out_shape=jax.ShapeDtypeStruct(shape, jnp.float32),
        scratch_shapes=[pltpu.VMEM((2 * n_hi, n_rows, f_dev), jnp.float32)],
        compiler_params=params(4),
        name="gather",
    )(*pieces)


def make_tables(m_modes, n_tm, t_dev):
    n_time = t_dev * n_tm
    times = lax.axis_index("tm") * t_dev + jnp.arange(t_dev, dtype=jnp.int32)
    index = m_modes[:, None] * times[None, :] % n_time
    angle = 2.0 * math.pi / n_time * index.astype(jnp.float32)
    return jnp.concatenate([jnp.cos(angle), jnp.sin(angle)], axis=0).astype(jnp.bfloat16)


def exchange(send, bit, n_tm):
    return lax.ppermute(send, "tm", [(i, i ^ bit) for i in range(n_tm)])


def make_chunks(n_units):
    sizes = [2, 2] if n_units == 4 else [1] * n_units
    return [(sum(sizes[:i]), size) for i, size in enumerate(sizes)]


def per_device(vis, beam, fg_cov, flags, m_modes):
    t_dev, f_dev, _ = vis.shape
    n_tm = lax.axis_size("tm")
    n_chan = lax.axis_size("chan")
    n_slots = m_modes.shape[0] // n_tm
    degrees = beam.shape[3]
    orders = bit_orders(n_tm)
    targets = [target_order(n_tm, bits) for bits in orders]
    n_units = f_dev // (2 * FB)
    chunks = make_chunks(n_units)
    n_chunks = len(chunks)
    n_steps = len(orders[0])

    parts = [None] * n_chunks
    sends = [None] * n_chunks

    def begin(chunk, tab):
        first, units = chunks[chunk]
        outs = transform(tab, vis, first * 2 * FB, units, targets, n_slots)
        parts[chunk] = [[outs[0]], [outs[2]]]
        sends[chunk] = [outs[1], outs[3]]

    def go_on(chunk, place):
        for h, bits in enumerate(orders):
            if h and not place:
                sends[chunk][0], parts[chunk][h][0] = lax.optimization_barrier(
                    (sends[chunk][0], parts[chunk][h][0])
                )
            got = exchange(sends[chunk][h], bits[place], n_tm)
            parts[chunk][h].append(got)
            size = got.shape[0] // 2
            sends[chunk][h] = sum(term[size : 2 * size] for term in parts[chunk][h])

    tab = make_tables(m_modes, n_tm, t_dev)
    for chunk in range(n_chunks):
        begin(chunk, tab)
    blocks = []
    for chunk, (first, units) in enumerate(chunks):
        before = max(chunk - 1, 0)
        source = sends[-1][0] if chunk == 0 else sends[before][0]
        source, beam = lax.optimization_barrier((source, beam))
        if chunk == 0:
            sends[-1][0] = source
        else:
            sends[before][0] = source
        block = load(beam, first * 2 * FB, units * 2 * FB)
        keeps = [group[0] for group in parts[chunk]]
        *keeps, block = lax.optimization_barrier((*keeps, block))
        parts[chunk] = [[keep] for keep in keeps]
        blocks.append(block)
        go_on(chunk, 0)
    *sends[-1], fg_cov = lax.optimization_barrier((*sends[-1], fg_cov))
    high, low = split(fg_cov)
    for place in range(1, n_steps):
        for chunk in range(n_chunks):
            go_on(chunk, place)

    coeffs = []
    for chunk, (first, units) in enumerate(chunks):
        for unit in reversed(range(units)):
            coeffs = project(
                parts[chunk], blocks[chunk], unit, units, first + unit, n_chan, n_units, coeffs
            )
    pieces = exchange_chan(*coeffs, n_chan)
    whole = fill(pieces, high, low, flags[None, :], f_dev)
    back = exchange_chan(*whole, n_chan)
    return gather(back, (n_slots, 2, degrees, f_dev))


def solution(mesh):
    placed = (P("tm", "chan", None), P("tm", "chan", None, None, None), P(), P(), P())
    return jax.shard_map(
        per_device,
        mesh=mesh,
        in_specs=placed,
        out_specs=P("tm", None, None, "chan"),
        check_vma=False,
    )
```

```python
import math

import jax
import jax.numpy as jnp
from jax import lax
from jax.experimental import pallas as pl
from jax.experimental.pallas import tpu as pltpu
from jax.sharding import PartitionSpec as P

ITERS = 10
EPS = 1e-06
FB = 16
PIECES = 8


def params(mebibytes):
    return pltpu.CompilerParams(vmem_limit_bytes=mebibytes * 1024 * 1024)


def bit_orders(n_tm):
    bits = [1 << i for i in range(n_tm.bit_length() - 1)]
    return bits, bits[::-1]


def target_order(n_tm, bits):
    return sorted(range(n_tm), key=lambda r: [int(bool(r & b)) for b in bits])


def transform_kernel(orders, n_slots, start, units, tab_ref, vis_ref, *refs):
    outs, (held_ref, wide_ref, full_ref, sems) = refs[:-4], refs[-4:]
    _, n_dev_time, _, width = held_ref.shape
    n_tm = len(orders[0])
    n_time = n_dev_time * n_tm
    n_rows = n_tm * n_slots
    half = width // 2
    depth = n_dev_time * FB
    scale = 1.0 / math.sqrt(n_time)

    def copies(unit):
        size = n_dev_time // PIECES
        for piece in range(PIECES):
            times = pl.ds(piece * size, size)
            source = vis_ref.at[times, pl.ds(start + unit * 2 * FB, 2 * FB), :]
            target = held_ref.at[unit, times]
            yield pltpu.make_async_copy(source, target, sems.at[unit, piece])

    for unit in range(units):
        for copy in copies(unit):
            copy.start()

    times = lax.broadcasted_iota(jnp.int32, (n_dev_time, depth), 0)
    lanes = lax.broadcasted_iota(jnp.int32, (n_dev_time, depth), 1)
    spread = jnp.where(lax.div(lanes, FB) == times, 1.0, 0.0).astype(jnp.bfloat16)
    wide_ref[...] = jnp.dot(tab_ref[...], spread, preferred_element_type=jnp.float32)
    me = lax.axis_index("tm")
    sub = lax.broadcasted_iota(jnp.int32, (FB, depth), 0)
    same = lax.rem(lax.broadcasted_iota(jnp.int32, (FB, depth), 1), FB) == sub
    for r in range(n_tm):
        for j in range(n_slots):
            for which in range(2):
                mode = which * n_rows + (me ^ r) * n_slots + j
                wide = jnp.broadcast_to(wide_ref[pl.ds(mode, 1), :], (FB, depth))
                at = (which * n_rows + r * n_slots + j) * FB
                full_ref[at : at + FB, :] = jnp.where(same, wide, 0.0).astype(jnp.bfloat16)

    for group in range(2 * units):
        part, place_f = group // units, group % units * FB
        order, keep, send = orders[part], outs[2 * part], outs[2 * part + 1]
        n_keep = keep.shape[0]
        if group % 2 == 0:
            for copy in copies(group // 2):
                copy.wait()
        first = group % 2 * FB
        data = held_ref[group // 2, :, first : first + FB, :].reshape(depth, width)
        prod = jnp.dot(full_ref[...], data, preferred_element_type=jnp.float32)
        cos_part, sin_part = prod[: n_rows * FB], prod[n_rows * FB :]
        real = (cos_part[:, :half] + sin_part[:, half:]) * scale
        imag = (cos_part[:, half:] - sin_part[:, :half]) * scale
        for place, r in enumerate(order):
            out = keep if place < n_keep else send
            for j in range(n_slots):
                at = (r * n_slots + j) * FB
                out[place % n_keep, j, place_f : place_f + FB, :half] = real[at : at + FB]
                out[place % n_keep, j, place_f : place_f + FB, half:] = imag[at : at + FB]


def transform(tab, vis, start, units, orders, n_slots):
    n_time, _, width = vis.shape
    n_tm = len(orders[0])
    depth = n_time * FB
    n_rows = n_tm * n_slots
    piece = jax.ShapeDtypeStruct((n_tm // 2, n_slots, units * FB, width), jnp.float32)

    def body(*refs):
        transform_kernel(orders, n_slots, start, units, *refs)

    return pl.pallas_call(
        body,
        in_specs=[
            pl.BlockSpec(memory_space=pltpu.VMEM),
            pl.BlockSpec(memory_space=pltpu.HBM),
        ],
        out_specs=[pl.BlockSpec(memory_space=pltpu.VMEM)] * 4,
        out_shape=[piece] * 4,
        scratch_shapes=[
            pltpu.VMEM((units, n_time, 2 * FB, width), jnp.bfloat16),
            pltpu.VMEM((2 * n_rows, depth), jnp.float32),
            pltpu.VMEM((2 * n_rows * FB, depth), jnp.bfloat16),
            pltpu.SemaphoreType.DMA((units, PIECES)),
        ],
        compiler_params=params(50),
        cost_estimate=pl.CostEstimate(
            flops=2 * 2 * n_rows * FB * depth * width * 2 * units,
            bytes_accessed=n_time * 2 * FB * units * width * 2 + 4 * 4 * piece.size,
            transcendentals=0,
        ),
        name="transform",
    )(tab, vis)


def position():
    me = lax.axis_index("chan")
    return lax.div(me, 2), lax.rem(me, 2)


def put(dst, keep_ref, send_ref, at, value):
    z, core = position()

    @pl.when(core == dst % 2)
    def _():
        keep_ref[(dst // 2) ^ z, *at] = value

    @pl.when(core != dst % 2)
    def _():
        send_ref[(dst // 2) ^ z, *at] = value


def far_order(n_hi):
    return [*range(max(n_hi // 2, 1), n_hi), *reversed(range(1, n_hi // 2))]


def exchange_chan(keep, send, n_chan):
    def swap(value, bits):
        return lax.ppermute(value, "chan", [(i, i ^ bits) for i in range(n_chan)])

    got = swap(send, 1)
    far = [swap(jnp.stack([keep[k], got[k]]), 2 * k) for k in far_order(n_chan // 2)]
    return [keep, got, *far]


def arrivals(refs):
    z, core = position()
    keep, got, far = refs[0], refs[1], refs[2:]
    yield 2 * z + core, lambda *at: keep[0, *at]
    yield 2 * z + 1 - core, lambda *at: got[0, *at]
    for k, ref in zip(far_order(len(far) + 1), far):
        yield 2 * (z ^ k) + core, lambda *at, ref=ref: ref[0, *at]
        yield 2 * (z ^ k) + 1 - core, lambda *at, ref=ref: ref[1, *at]


def project_kernel(halves, unit, units, n_terms, *refs):
    beam_ref, keep_ref, send_ref, vis_ref, flat_ref = refs[n_terms], *refs[-4:]
    _, double, width = beam_ref.shape
    half, degrees = double // 2, width // FB
    n_slots = refs[0].shape[1]
    pairs = n_slots // 2
    pieces = [(i, s, h) for i in range(pairs) for s in range(2) for h in range(2)]

    for at, (i, s, h) in enumerate(pieces):
        terms, place = halves[h]
        total = None
        for term in terms:
            value = refs[term][0, 2 * i + s, place : place + FB, :]
            total = value if total is None else total + value
        real = total[:, :half].astype(jnp.bfloat16)
        imag = total[:, half:].astype(jnp.bfloat16)
        vis_ref[at, :FB, :half] = real
        vis_ref[at, FB:, :half] = imag
        vis_ref[at, :FB, half:] = -imag
        vis_ref[at, FB:, half:] = real

    per_pair = 2 * keep_ref.shape[0] // pairs
    rows = keep_ref.shape[1]
    per_tile = 128 // degrees
    sub = lax.broadcasted_iota(jnp.int32, (8, 128), 0)
    for at, (i, s, h) in enumerate(pieces):
        turned = beam_ref[((2 * i + s) * units + unit) * 2 + h]
        prod = jnp.dot(vis_ref[at], turned, preferred_element_type=jnp.float32)
        for p in range(2):
            for g in range(FB // 8):
                own = prod[p * FB + g * 8 : p * FB + g * 8 + 8, g * 8 * degrees : (g + 1) * 8 * degrees]
                pick = own[:, :128]
                for v in range(1, 8 // per_tile):
                    pick = jnp.where(sub // per_tile == v, own[:, v * 128 : (v + 1) * 128], pick)
                if per_tile == 2:
                    pick = jnp.where(sub % 2 == 0, pick, pltpu.roll(pick, degrees, 1))
                row = s * 4 * FB + p * 2 * FB + h * FB + g * 8
                flat_ref[row : row + 8, :] = pick
        if s == 1 and h == 1:
            coeffs = flat_ref[...].T[:degrees]
            for b in range(per_pair):
                put(i * per_pair + b, keep_ref, send_ref, (), coeffs[b * rows : (b + 1) * rows])


def load(beam, start, size, depth=6):
    n_slots, _, _, degrees, half = beam.shape
    per_slot = size // FB
    n_pieces = n_slots * per_slot
    depth = min(depth, n_pieces)

    def body(beam_ref, out_ref, held_ref, sems):
        def copy(at):
            f = pl.multiple_of(start + lax.rem(at, per_slot) * FB, FB)
            slot = lax.rem(at, depth)
            return pltpu.make_async_copy(
                beam_ref.at[lax.div(at, per_slot), pl.ds(f, FB)], held_ref.at[slot], sems.at[slot]
            )

        def step(at, carry):
            copy(at).wait()
            for p in range(2):
                block = held_ref[lax.rem(at, depth), :, p].reshape(FB * degrees, half)
                out_ref[at, p * half : (p + 1) * half, :] = block.T

            @pl.when(at + depth < n_pieces)
            def _():
                copy(at + depth).start()

            return carry

        for at in range(depth):
            copy(at).start()
        lax.fori_loop(0, n_pieces, step, 0)

    return pl.pallas_call(
        body,
        in_specs=[pl.BlockSpec(memory_space=pltpu.HBM)],
        out_specs=pl.BlockSpec(memory_space=pltpu.VMEM),
        out_shape=jax.ShapeDtypeStruct((n_pieces, 2 * half, FB * degrees), beam.dtype),
        scratch_shapes=[
            pltpu.VMEM((depth, FB, 2, degrees, half), beam.dtype),
            pltpu.SemaphoreType.DMA((depth,)),
        ],
        compiler_params=params(10),
        cost_estimate=pl.CostEstimate(
            flops=0, bytes_accessed=4 * n_pieces * FB * 2 * degrees * half, transcendentals=0
        ),
        name="load",
    )(beam)


def project(parts, beam, unit, units, place, n_chan, n_units, buffers):
    _, double, width = beam.shape
    half, degrees = double // 2, width // FB
    n_slots = parts[0][0].shape[1]
    pairs = n_slots // 2
    rows = pairs * degrees // n_chan
    terms, halves = [], []
    for h in range(2):
        part, at = (2 * unit + h) // units, (2 * unit + h) % units * FB
        if not halves or part != (2 * unit) // units:
            terms += parts[part]
        halves.append((range(len(terms) - len(parts[part]), len(terms)), at))
    n_terms = len(terms)
    n_pieces = n_slots * 2

    def body(*refs):
        project_kernel(halves, unit, units, n_terms, *refs)

    term_spec = pl.BlockSpec((1, n_slots, units * FB, 2 * half), lambda i: (0, 0, 0, 0))
    return pl.pallas_call(
        body,
        grid=(1,),
        in_specs=[term_spec] * n_terms
        + [pl.BlockSpec(memory_space=pltpu.VMEM)]
        + [pl.BlockSpec(memory_space=pl.ANY)] * len(buffers),
        out_specs=[pl.BlockSpec((n_chan // 2, None, rows, 8 * FB), lambda i: (0, place, 0, 0))] * 2,
        out_shape=[jax.ShapeDtypeStruct((n_chan // 2, n_units, rows, 8 * FB), jnp.float32)] * 2,
        scratch_shapes=[
            pltpu.VMEM((n_pieces, 2 * FB, 2 * half), jnp.bfloat16),
            pltpu.VMEM((8 * FB, 128), jnp.float32),
        ],
        input_output_aliases={n_terms + 1 + i: i for i in range(len(buffers))},
        compiler_params=params(6),
        cost_estimate=pl.CostEstimate(
            flops=2 * n_slots * 2 * FB * 2 * degrees * half * 256,
            bytes_accessed=n_slots * 2 * FB * 2 * degrees * half * 2,
            transcendentals=0,
        ),
        name="project",
    )(*terms, beam, *buffers)


def split_kernel(cov_ref, high_ref, low_ref):
    cov = cov_ref[...]
    high = cov.astype(jnp.bfloat16)
    high_ref[...] = high
    low_ref[...] = (cov - high.astype(jnp.float32)).astype(jnp.bfloat16)


def split(cov, n_blocks=4):
    rows, cols = cov.shape
    spec = pl.BlockSpec((rows // n_blocks, cols), lambda i: (i, 0))
    half = jax.ShapeDtypeStruct(cov.shape, jnp.bfloat16)
    return pl.pallas_call(
        split_kernel,
        grid=(n_blocks,),
        in_specs=[spec],
        out_specs=[spec, spec],
        out_shape=[half, half],
        compiler_params=params(10),
        cost_estimate=pl.CostEstimate(
            flops=4 * cov.size, bytes_accessed=8 * cov.size, transcendentals=0
        ),
        name="split",
    )(cov)


def fill_kernel(n_in, *refs):
    high_ref, low_ref, flags_ref, keep_ref, send_ref, data_ref = refs[n_in:]
    n_src, n_rows, f_dev = data_ref.shape
    _, n_units, rows, lanes = refs[0].shape
    groups = lanes // (2 * FB)
    for src, take in arrivals(refs[:n_in]):
        for u in range(n_units):
            piece = take(u)
            for g in range(groups):
                data_ref[src, g * rows : (g + 1) * rows, u * 2 * FB : (u + 1) * 2 * FB] = piece[
                    :, g * 2 * FB : (g + 1) * 2 * FB
                ]
    data = jnp.concatenate([data_ref[src] for src in range(n_src)], axis=1)
    good = 1.0 - flags_ref[...].astype(jnp.float32)

    def total(values):
        return jnp.sum(values, axis=1, keepdims=True)

    def covered(vec):
        top = vec.astype(jnp.bfloat16)
        rest = (vec - top.astype(jnp.float32)).astype(jnp.bfloat16)
        both = jnp.concatenate([top, rest], axis=0)
        wide = jnp.dot(both, high_ref[...], preferred_element_type=jnp.float32)
        thin = jnp.dot(top, low_ref[...], preferred_element_type=jnp.float32)
        return wide[:n_rows] + (wide[n_rows:] + thin)

    resid = good * data
    direc = resid
    norm_now = total(resid * resid)
    signal = jnp.zeros_like(resid)

    def advance(step, carry):
        signal, resid, direc, norm_now = carry
        image = covered(direc)
        shifted = direc + good * image
        alpha = norm_now / (total(direc * shifted) + EPS)
        signal = signal + alpha * image
        resid = resid - alpha * shifted
        norm_next = total(resid * resid)
        direc = resid + norm_next / (norm_now + EPS) * direc
        return signal, resid, direc, norm_next

    signal, resid, direc, norm_now = lax.fori_loop(
        0, ITERS, advance, (signal, resid, direc, norm_now), unroll=True
    )
    data = jnp.concatenate([data_ref[src] for src in range(n_src)], axis=1)
    filled = good * data + (1.0 - good) * signal
    for dst in range(n_src):
        put(dst, keep_ref, send_ref, (), filled[:, dst * f_dev : (dst + 1) * f_dev])


def fill(pieces, high, low, flags, f_dev):
    n_hi, _, rows, lanes = pieces[0].shape
    n_rows = lanes // (2 * FB) * rows
    n_freq = high.shape[0]

    def body(*refs):
        fill_kernel(len(pieces), *refs)

    return pl.pallas_call(
        body,
        in_specs=[pl.BlockSpec(memory_space=pltpu.VMEM)] * (len(pieces) + 3),
        out_specs=[pl.BlockSpec(memory_space=pltpu.VMEM)] * 2,
        out_shape=[jax.ShapeDtypeStruct((n_hi, n_rows, f_dev), jnp.float32)] * 2,
        scratch_shapes=[pltpu.VMEM((2 * n_hi, n_rows, f_dev), jnp.float32)],
        compiler_params=params(8),
        cost_estimate=pl.CostEstimate(
            flops=2 * ITERS * 3 * n_rows * n_freq * n_freq,
            bytes_accessed=4 * n_freq * n_freq,
            transcendentals=0,
        ),
        name="fill",
    )(*pieces, high, low, flags)


def gather_kernel(n_in, *refs):
    out_ref, stage_ref = refs[n_in:]
    n_src, n_rows, _ = stage_ref.shape
    for src, take in arrivals(refs[:n_in]):
        stage_ref[src] = take()
    pairs = out_ref.shape[0] // 2
    per_pair = n_src // pairs
    rows = n_rows // 4
    for src in range(n_src):
        i, block = src // per_pair, src % per_pair
        for g in range(4):
            out_ref[2 * i + g // 2, g % 2, block * rows : (block + 1) * rows, :] = stage_ref[
                src, g * rows : (g + 1) * rows, :
            ]


def gather(pieces, shape):
    def body(*refs):
        gather_kernel(len(pieces), *refs)

    n_hi, n_rows, f_dev = pieces[0].shape
    return pl.pallas_call(
        body,
        in_specs=[pl.BlockSpec(memory_space=pltpu.VMEM)] * len(pieces),
        out_specs=pl.BlockSpec(memory_space=pltpu.VMEM),
        out_shape=jax.ShapeDtypeStruct(shape, jnp.float32),
        scratch_shapes=[pltpu.VMEM((2 * n_hi, n_rows, f_dev), jnp.float32)],
        compiler_params=params(4),
        name="gather",
    )(*pieces)


def make_tables(m_modes, n_tm, t_dev):
    n_time = t_dev * n_tm
    times = lax.axis_index("tm") * t_dev + jnp.arange(t_dev, dtype=jnp.int32)
    index = m_modes[:, None] * times[None, :] % n_time
    angle = 2.0 * math.pi / n_time * index.astype(jnp.float32)
    return jnp.concatenate([jnp.cos(angle), jnp.sin(angle)], axis=0).astype(jnp.bfloat16)


def exchange(send, bit, n_tm):
    return lax.ppermute(send, "tm", [(i, i ^ bit) for i in range(n_tm)])


def make_chunks(n_units):
    sizes = [2, 2] if n_units == 4 else [1] * n_units
    return [(sum(sizes[:i]), size) for i, size in enumerate(sizes)]


def per_device(vis, beam, fg_cov, flags, m_modes):
    t_dev, f_dev, _ = vis.shape
    n_tm = lax.axis_size("tm")
    n_chan = lax.axis_size("chan")
    n_slots = m_modes.shape[0] // n_tm
    degrees = beam.shape[3]
    orders = bit_orders(n_tm)
    targets = [target_order(n_tm, bits) for bits in orders]
    n_units = f_dev // (2 * FB)
    chunks = make_chunks(n_units)
    n_chunks = len(chunks)
    n_steps = len(orders[0])

    parts = [None] * n_chunks
    sends = [None] * n_chunks

    def begin(chunk, tab):
        first, units = chunks[chunk]
        outs = transform(tab, vis, first * 2 * FB, units, targets, n_slots)
        parts[chunk] = [[outs[0]], [outs[2]]]
        sends[chunk] = [outs[1], outs[3]]

    def go_on(chunk, place):
        for h, bits in enumerate(orders):
            if h and not place:
                sends[chunk][0], parts[chunk][h][0] = lax.optimization_barrier(
                    (sends[chunk][0], parts[chunk][h][0])
                )
            got = exchange(sends[chunk][h], bits[place], n_tm)
            parts[chunk][h].append(got)
            size = got.shape[0] // 2
            sends[chunk][h] = sum(term[size : 2 * size] for term in parts[chunk][h])

    tab = make_tables(m_modes, n_tm, t_dev)
    for chunk in range(n_chunks):
        begin(chunk, tab)
    blocks = []
    for chunk, (first, units) in enumerate(chunks):
        before = max(chunk - 1, 0)
        source = sends[-1][0] if chunk == 0 else sends[before][0]
        source, beam = lax.optimization_barrier((source, beam))
        if chunk == 0:
            sends[-1][0] = source
        else:
            sends[before][0] = source
        block = load(beam, first * 2 * FB, units * 2 * FB)
        keeps = [group[0] for group in parts[chunk]]
        *keeps, block = lax.optimization_barrier((*keeps, block))
        parts[chunk] = [[keep] for keep in keeps]
        blocks.append(block)
        go_on(chunk, 0)
    *sends[-1], fg_cov = lax.optimization_barrier((*sends[-1], fg_cov))
    high, low = split(fg_cov)
    for place in range(1, n_steps):
        for chunk in range(n_chunks):
            go_on(chunk, place)

    coeffs = []
    for chunk, (first, units) in enumerate(chunks):
        for unit in reversed(range(units)):
            coeffs = project(
                parts[chunk], blocks[chunk], unit, units, first + unit, n_chan, n_units, coeffs
            )
    pieces = exchange_chan(*coeffs, n_chan)
    whole = fill(pieces, high, low, flags[None, :], f_dev)
    back = exchange_chan(*whole, n_chan)
    return gather(back, (n_slots, 2, degrees, f_dev))


def solution(mesh):
    placed = (P("tm", "chan", None), P("tm", "chan", None, None, None), P(), P(), P())
    return jax.shard_map(
        per_device,
        mesh=mesh,
        in_specs=placed,
        out_specs=P("tm", None, None, "chan"),
        check_vma=False,
    )
```
